128 devices in a mesh: kv: 16 (over x, z), head: 8 (over y, core).
Axes of the slice: x: 4, y: 4, z: 4, core: 2. Of those that a mesh axis runs over, the one named last changes fastest.
Arguments:
- queries: bfloat16 [32, 16384], P(None, 'head'), may hold values from -100 to 100
- key_cache: bfloat16 [384, 8, 128, 128], P('kv', 'head'), may hold values from -6 to 6
- value_cache: bfloat16 [384, 8, 128, 128], P('kv', 'head'), may hold values from -6 to 6
- block_table: int32 [2, 384], P(None, 'kv'), may hold values from 0 to 128, as said below
- lengths: int32 [16], replicated, may hold values from 2 to 16384, as said below
- new_keys: bfloat16 [32, 1024], P(None, 'head'), may hold values from -4 to 4
- new_values: bfloat16 [32, 1024], P(None, 'head'), may hold values from -6 to 6
- residual: bfloat16 [32, 16384], P(None, ('kv', 'head')), may hold values from -2 to 2
- out_weight: bfloat16 [8, 16, 128, 16384], P('head', 'kv'), may hold values from -0.0625 to 0.0625
- norm_gain: bfloat16 [16384], P(('kv', 'head')), may hold values from 0.5 to 1.5
- w_gate: bfloat16 [16384, 26624], P('kv', 'head'), may hold values from -0.046875 to 0.046875
- w_up: bfloat16 [16384, 26624], P('kv', 'head'), may hold values from -0.046875 to 0.046875
- w_down: bfloat16 [26624, 16384], P('head', 'kv'), may hold values from -0.0546875 to 0.0546875
Outputs:
- layer_out: bfloat16 [32, 16384], P(None, ('kv', 'head'))
The draws below stay inside these ranges and needn't reach their ends.
Inputs may be any that keep to these rules, and one draw needn't show every extreme that they name: `block_table`: each sequence's tokens fill blocks 0 to ceil(length / 128) - 1 of it; each such block is held by exactly one slot. Every other slot, and there is at least one, names sequence 0 and block position 128, so it holds no live token. Slots are spread over the devices in no particular order. `lengths`: the longest sequence has exactly 16384 tokens.
All inputs are finite; a program needn't handle non-finite values.
Results may differ from the reference program's by a relative error of at most 0.03.
Values may be sent and summed in bfloat16 or wider, within the bound.
No kernel may reach another device: no remote copies, remote signals or barrier semaphores. Data moves between devices by JAX's collectives and lax.ppermute only.
A program may use at most 128 MiB of HBM per device.

```python
import math
import jax
import jax.numpy as jnp
from jax import lax

D = 16384
FFW = 26624
HQ = 128
KVH = 8
HD = 128
BS = 128
SEQS = 16
BLOCKS = 384
SEQ_MAX_BLK = 128
ROWS = 32
N_HEAD = 8


def shared_keys(key):
    base_keys = jax.random.normal(key, (SEQS, KVH * HD), jnp.float32)
    return jnp.clip(base_keys, -4.0, 4.0)


def block_plan(key):
    key = jax.random.fold_in(key, 101)
    key_top, key_units, key_trim, key_perm = jax.random.split(key, 4)
    seq_index = jnp.arange(SEQS, dtype=jnp.int32)
    longest = jax.random.randint(key_top, (), 0, SEQS)
    extra_units = BLOCKS - SEQ_MAX_BLK - SEQS
    units = jax.random.randint(key_units, (extra_units,), 0, SEQS - 1)
    units = units + (units >= longest).astype(jnp.int32)
    counts = 1 + jnp.sum((units[:, None] == seq_index[None, :]).astype(jnp.int32), axis=0)
    counts = jnp.where(seq_index == longest, SEQ_MAX_BLK, jnp.minimum(counts, SEQ_MAX_BLK))
    trims = jax.random.randint(key_trim, (SEQS,), 0, BS - 1)
    lengths = counts * BS - jnp.where(seq_index == longest, 0, trims)
    ends = jnp.cumsum(counts)
    starts = ends - counts
    total_used = ends[SEQS - 1]
    slot_index = jnp.arange(BLOCKS, dtype=jnp.int32)
    seq_raw = jnp.sum((slot_index[:, None] >= ends[None, :]).astype(jnp.int32), axis=1)
    seq_safe = jnp.minimum(seq_raw, SEQS - 1)
    used = slot_index < total_used
    seq_of = jnp.where(used, seq_safe, 0)
    pos_of = jnp.where(used, slot_index - starts[seq_safe], SEQ_MAX_BLK)
    order = jax.random.permutation(key_perm, BLOCKS)
    table = jnp.stack([seq_of[order], pos_of[order]], axis=0)
    return (lengths.astype(jnp.int32), table.astype(jnp.int32))


def draw_lengths(key, part):
    lengths, table = block_plan(key)
    return lengths


def draw_block_table(key, part):
    lengths, table = block_plan(key)
    return table


def draw_key_cache(key, part):
    key = jax.random.fold_in(key, 7)
    drawn = jnp.clip(jax.random.normal(key, (BLOCKS, KVH, BS, HD), jnp.float32), -6.0, 6.0)
    return drawn.astype(jnp.bfloat16)


def draw_new_keys(key, part):
    first_keys = shared_keys(key)
    key = jax.random.fold_in(key, 3)
    noise = jax.random.normal(key, (SEQS, KVH * HD), jnp.float32)
    second_keys = jnp.clip(noise, -4.0, 4.0)
    stacked = jnp.stack([first_keys, second_keys], axis=1)
    return stacked.reshape(ROWS, KVH * HD).astype(jnp.bfloat16)


def draw_queries(key, part):
    key = jax.random.fold_in(key, 5)
    key_drawn = jax.random.fold_in(key, 0)
    drawn = jnp.clip(2.5 * jax.random.normal(key_drawn, (SEQS, 2, HQ, HD), jnp.float32), -10.0, 10.0)
    return drawn.reshape(ROWS, HQ * HD).astype(jnp.bfloat16)


def with_spikes(array, own_key, source, target, blocks, factor):
    owner, partner = [(jnp.arange(array.shape[axis_at]) // (array.shape[axis_at] // blocks)).reshape([-1 if axis == axis_at else 1 for axis in range(array.ndim)]) for axis_at in (source, target)]
    chosen = jax.random.permutation(own_key, blocks)[partner]
    strong = (owner == chosen) | (owner == (partner + blocks // 2) % blocks)
    return jnp.where(strong, factor * array, array)


def shard_levels(stream_key, dims, shards, smallest, high):
    loudness = 1.0
    for dim, shards_of in shards:
        steps = jax.random.uniform(jax.random.fold_in(jax.random.fold_in(stream_key, 6), dim), (shards_of,), jnp.float32, smallest / len(shards), high / len(shards))
        loudness = loudness * jnp.repeat(jnp.exp(steps), dims[dim] // shards_of).reshape((-1,) + (1,) * (len(dims) - 1 - dim))
    return loudness


def centred(own_key, dims, spread, bound, pieces=(), held_as=jnp.bfloat16):
    gain = shard_levels(own_key, dims, pieces, -0.22, 0.18) if pieces else 1.0
    values = jax.random.normal(own_key, dims, jnp.float32) * spread * gain
    return jnp.minimum(jnp.maximum(values, -bound), bound).astype(held_as)


def bell_draw_with(rng, extent, width, bound, cuts, heavy, kind=jnp.bfloat16):
    result = width * jax.random.normal(rng, extent, jnp.float32)
    if cuts:
        result = result * shard_levels(rng, extent, cuts, -0.22, 0.18)
    return jnp.clip(with_spikes(result, jax.random.fold_in(rng, 3), *heavy), -bound, bound).astype(kind)


def setup_inputs(seed: int = 0) -> dict:
    arg_keys = jax.random.split(jax.random.key(seed), 14)
    queries = draw_queries(jax.random.fold_in(arg_keys[13], 71), 0)
    key_cache = draw_key_cache(jax.random.fold_in(arg_keys[13], 71), 0)
    value_cache = centred(arg_keys[2], (BLOCKS, KVH, BS, HD), 1.0, 6.0, ((0, 16), (1, 8)))
    block_table = draw_block_table(jax.random.fold_in(arg_keys[13], 71), 0)
    lengths = draw_lengths(jax.random.fold_in(arg_keys[13], 71), 0)
    new_keys = draw_new_keys(jax.random.fold_in(arg_keys[13], 71), 0)
    new_values = centred(arg_keys[6], (ROWS, KVH * HD), 1.0, 6.0, ((1, 8),))
    residual = centred(arg_keys[7], (ROWS, D), 0.3, 2.0, ((1, 128),))
    out_weight = bell_draw_with(arg_keys[8], (N_HEAD, HQ // N_HEAD, HD, D), (HQ * HD) ** -0.5, 0.0625, ((0, 8), (1, 16)), (1, 3, 16, 2.0))
    norm_gain = jnp.clip(0.5 + 1.0 * jax.random.uniform(arg_keys[9], (D,), jnp.float32) ** shard_levels(arg_keys[9], (D,), ((0, 128),), -0.2, 0.2), 0.5, 1.5).astype(jnp.bfloat16)
    w_gate = centred(arg_keys[10], (D, FFW), D ** -0.5, 0.046875, ((0, 16), (1, 8)))
    w_up = centred(arg_keys[11], (D, FFW), D ** -0.5, 0.046875, ((0, 16), (1, 8)))
    w_down = bell_draw_with(arg_keys[12], (FFW, D), FFW ** -0.5, 0.0546875, ((0, 8), (1, 16)), (0, 1, 16, 2.0))
    return {"queries": queries, "key_cache": key_cache, "value_cache": value_cache, "block_table": block_table, "lengths": lengths, "new_keys": new_keys, "new_values": new_values, "residual": residual, "out_weight": out_weight, "norm_gain": norm_gain, "w_gate": w_gate, "w_up": w_up, "w_down": w_down}


def reference(queries, key_cache, value_cache, block_table, lengths, new_keys, new_values, residual, out_weight, norm_gain, w_gate, w_up, w_down):
    highest = lax.Precision.HIGHEST
    group = HQ // KVH
    query_all = queries.astype(jnp.float32).reshape(SEQS, 2, KVH, group, HD)
    seq_ids = block_table[0]
    pos_ids = block_table[1]
    picked = query_all[seq_ids]
    scores = jnp.einsum('btkgd,bkud->btkgu', picked, key_cache.astype(jnp.float32), precision=highest) / math.sqrt(HD)
    token_pos = pos_ids[:, None] * BS + jnp.arange(BS, dtype=jnp.int32)[None, :]
    live_mask = (token_pos < lengths[seq_ids][:, None])[:, None, None, None, :]
    block_max = lax.optimization_barrier(jnp.max(jnp.where(live_mask, scores, -1e+30), axis=-1))
    expo_vals = jnp.where(live_mask, jnp.exp(scores - block_max[..., None]), 0.0)
    block_sum = lax.optimization_barrier(jnp.sum(expo_vals, axis=-1))
    probs_low = expo_vals.astype(jnp.bfloat16)
    block_out = jnp.einsum('btkgu,bkud->btkgd', probs_low.astype(jnp.float32), value_cache.astype(jnp.float32), precision=highest)
    fresh_keys = new_keys.astype(jnp.float32).reshape(SEQS, 2, KVH, HD)
    fresh_vals = new_values.astype(jnp.float32).reshape(SEQS, 2, KVH, HD)
    fresh_scores = jnp.einsum('stkgd,sukd->stkgu', query_all, fresh_keys, precision=highest) / math.sqrt(HD)
    causal = (jnp.arange(2)[:, None] >= jnp.arange(2)[None, :])[None, :, None, None, :]
    fresh_max = lax.optimization_barrier(jnp.max(jnp.where(causal, fresh_scores, -1e+30), axis=-1))
    fresh_expo = jnp.where(causal, jnp.exp(fresh_scores - fresh_max[..., None]), 0.0)
    fresh_sum = lax.optimization_barrier(jnp.sum(fresh_expo, axis=-1))
    fresh_probs = fresh_expo.astype(jnp.bfloat16)
    fresh_out = jnp.einsum('stkgu,sukd->stkgd', fresh_probs.astype(jnp.float32), fresh_vals, precision=highest)
    member = (seq_ids[:, None] == jnp.arange(SEQS, dtype=jnp.int32)[None, :])[:, :, None, None, None]
    seq_max = jnp.maximum(lax.optimization_barrier(jnp.max(jnp.where(member, block_max[:, None], -1e+30), axis=0)), fresh_max)
    weights = jnp.where(member, jnp.exp(block_max[:, None] - seq_max[None]), 0.0)
    fresh_weight = jnp.exp(fresh_max - seq_max)
    numer = jnp.einsum('bstkg,btkgd->stkgd', weights, block_out, precision=highest) + fresh_weight[..., None] * fresh_out
    denom = jnp.einsum('bstkg,btkg->stkg', weights, block_sum, precision=highest) + fresh_weight * fresh_sum
    attn = (numer / denom[..., None]).astype(jnp.bfloat16).reshape(ROWS, HQ * HD)
    proj = jnp.dot(attn, out_weight.reshape(HQ * HD, D), preferred_element_type=jnp.float32)
    hidden_one = residual.astype(jnp.float32) + proj
    mean_sq = lax.optimization_barrier(jnp.mean(hidden_one * hidden_one, axis=1, keepdims=True))
    normed = (hidden_one * lax.rsqrt(mean_sq + 1e-05) * norm_gain.astype(jnp.float32)).astype(jnp.bfloat16)
    gate = jnp.dot(normed, w_gate, preferred_element_type=jnp.float32)
    upper = jnp.dot(normed, w_up, preferred_element_type=jnp.float32)
    hidden = (jax.nn.silu(gate) * upper).astype(jnp.bfloat16)
    down = jnp.dot(hidden, w_down, preferred_element_type=jnp.float32)
    return (hidden_one + down).astype(jnp.bfloat16)
```

```python
import math

import jax
import jax.numpy as jnp
from jax import lax
from jax.experimental import pallas as pl
from jax.experimental.pallas import tpu as pltpu
from jax.sharding import PartitionSpec as P

HQ = 128
KVH = 8
SEQS = 16
ROWS = 2 * SEQS
GROUP = HQ // KVH
HD = 128
SLOTS = 24
OWN = 128
HALF = 4 * OWN
N_KV = 16
UNITS = 3328
PART = UNITS // 2
EXTRA = 128
TILE = 256

F32 = jnp.float32
BF16 = jnp.bfloat16
MIB = 1 << 20


def whole(shape, space=pltpu.VMEM):
    zeros = (0,) * len(shape)
    return pl.BlockSpec(shape, lambda *_: zeros, memory_space=space)


def scalars():
    return pl.BlockSpec(memory_space=pltpu.SMEM)


def params(mib, steps=0):
    kinds = ("arbitrary",) * steps if steps else None
    return pltpu.CompilerParams(vmem_limit_bytes=mib * MIB, dimension_semantics=kinds)


def shape(dims, kind):
    return jax.ShapeDtypeStruct(dims, kind)


def attention_kernel(table, lengths, q_ref, k_ref, v_ref, out_ref, q_rows, scores, tops, sums, numer):
    for g in range(GROUP):
        q_rows[pl.ds(g, ROWS, stride=GROUP), :] = q_ref[:, g * HD : (g + 1) * HD].astype(F32)
    tops[...] = jnp.full(tops.shape, -1e30, F32)
    sums[...] = jnp.zeros(sums.shape, F32)
    numer[...] = jnp.zeros(numer.shape, F32)
    lane = lax.broadcasted_iota(jnp.int32, (ROWS, HD), 1)
    rows_of = []
    for b in range(SLOTS):
        seq = table[0, b]
        limit = lengths[seq] - table[1, b] * HD
        here = pl.ds(pl.multiple_of(seq * ROWS, ROWS), ROWS)
        rows_of.append(here)
        raw = lax.dot_general(
            q_rows[here, :].astype(BF16), k_ref[b, 0], (((1,), (1,)), ((), ())),
            preferred_element_type=F32,
        )
        masked = jnp.where(lane < limit, raw * (1.0 / math.sqrt(HD)), -1e30)
        scores[b] = masked
        tops[here, :] = jnp.maximum(tops[here, :], jnp.max(masked, axis=1, keepdims=True))
    tops[...] = tops[...].astype(BF16).astype(F32)
    for b in range(SLOTS):
        here = rows_of[b]
        masked = scores[b]
        expo = jnp.where(masked > -1e29, jnp.exp(masked - tops[here, :]), 0.0)
        sums[here, :] += jnp.sum(expo, axis=1, keepdims=True)
        numer[here, :] += jnp.dot(expo.astype(BF16), v_ref[b, 0], preferred_element_type=F32)
    for g in range(GROUP):
        pick = pl.ds(g, ROWS, stride=GROUP)
        out_ref[g, :, :HD] = numer[pick, :].astype(BF16)
        high = sums[pick, :].astype(BF16).astype(F32)
        stats = jnp.where(lane < 32, tops[pick, :], jnp.where(lane < 64, high, sums[pick, :] - high))
        out_ref[g, :, HD:] = stats.astype(BF16)


def attention_partials(table, lengths, queries, key_cache, value_cache):
    tall = pltpu.VMEM((ROWS * GROUP, HD), F32)
    return pl.pallas_call(
        attention_kernel,
        out_shape=shape((GROUP, ROWS, 2 * HD), BF16),
        in_specs=[scalars(), scalars()] + [whole(a.shape) for a in (queries, key_cache, value_cache)],
        out_specs=whole((GROUP, ROWS, 2 * HD)),
        scratch_shapes=[tall, pltpu.VMEM((SLOTS, ROWS, HD), F32), tall, tall, tall],
        compiler_params=params(16),
        name="attention",
    )(table, lengths, queries, key_cache, value_cache)


def project_kernel(place, got_ref, q_ref, k_ref, v_ref, w_ref, keep_ref, give_ref, attn):
    @pl.when(pl.program_id(0) == 0)
    def _():
        start = pl.multiple_of(place[0] * HD, HD)
        query = q_ref[:, pl.ds(start, HD)].astype(F32)
        keys, values = k_ref[...].astype(F32), v_ref[...].astype(F32)
        odd = lax.broadcasted_iota(jnp.int32, (ROWS, 1), 0) % 2 == 1
        unit = 1.0 / math.sqrt(HD)
        at_own = jnp.sum(query * keys, axis=1, keepdims=True) * unit
        at_prev = jnp.sum(query * pltpu.roll(keys, 1, 0), axis=1, keepdims=True) * unit
        new_max = jnp.where(odd, jnp.maximum(at_own, at_prev), at_own)
        expo_own = jnp.exp(at_own - new_max)
        expo_prev = jnp.where(odd, jnp.exp(at_prev - new_max), 0.0)
        new_out = expo_own.astype(BF16).astype(F32) * values
        new_out += expo_prev.astype(BF16).astype(F32) * pltpu.roll(values, 1, 0)
        maxes = [got_ref[i, :, HD : HD + 1].astype(F32) for i in range(N_KV)]
        peak = new_max
        for top in maxes:
            peak = jnp.maximum(peak, top)
        scale = jnp.exp(new_max - peak)
        total = scale * new_out
        denom = scale * (expo_own + expo_prev)
        for i in range(N_KV):
            scale = jnp.exp(maxes[i] - peak)
            high = got_ref[i, :, HD + 32 : HD + 33].astype(F32)
            low = got_ref[i, :, HD + 64 : HD + 65].astype(F32)
            total += scale * got_ref[i, :, :HD].astype(F32)
            denom += scale * (high + low)
        attn[...] = (total / denom).astype(BF16)

    even = place[2] == 0
    for d in range(w_ref.shape[1] // (2 * HALF)):
        for y in range(4):
            at = d * 2 * HALF + y * TILE
            both = jnp.dot(attn[...], w_ref[:, at : at + TILE], preferred_element_type=F32)
            here = slice(y * OWN, (y + 1) * OWN)
            keep_ref[d, :, here] = jnp.where(even, both[:, :OWN], both[:, OWN:])
            give_ref[d, :, here] = jnp.where(even, both[:, OWN:], both[:, :OWN]).astype(BF16)


def project(place, got, queries, new_keys, new_values, weight):
    steps, each = 8, N_KV // 8
    block = pl.BlockSpec((each, ROWS, HALF), lambda i: (i, 0, 0))
    return pl.pallas_call(
        project_kernel,
        grid=(steps,),
        out_shape=[shape((N_KV, ROWS, HALF), F32), shape((N_KV, ROWS, HALF), BF16)],
        in_specs=[scalars()]
        + [whole(a.shape) for a in (got, queries, new_keys, new_values)]
        + [pl.BlockSpec((HD, each * 2 * HALF), lambda i: (0, i))],
        out_specs=[block, block],
        scratch_shapes=[pltpu.VMEM((ROWS, HD), BF16)],
        compiler_params=params(16, 1),
        name="project",
    )(place, got, queries, new_keys, new_values, weight)


def pair_kernel(keep_ref, got_ref, out_ref):
    out_ref[...] = (keep_ref[...] + got_ref[...].astype(F32)).astype(BF16)


def add_pair(keep, got):
    return pl.pallas_call(
        pair_kernel,
        out_shape=shape(keep.shape, BF16),
        in_specs=[whole(keep.shape), whole(got.shape)],
        out_specs=whole(keep.shape),
        compiler_params=params(16),
        name="add_pair",
    )(keep, got)


def stream_kernel(place, parts_ref, res_ref, gain_ref, out_ref):
    total = parts_ref[0].astype(F32)
    for i in range(1, N_KV):
        total += parts_ref[i].astype(F32)
    for y in range(4):
        here = slice(y * OWN, (y + 1) * OWN)
        mine = place[3] == y
        rest = jnp.where(mine, res_ref[...].astype(F32), 0.0)
        out_ref[:ROWS, here] = (total[:, here] + rest).astype(BF16)
        gain = jnp.where(mine, gain_ref[...].astype(F32), 0.0)
        out_ref[ROWS:, here] = jnp.broadcast_to(gain, (16, OWN)).astype(BF16)


def stream(place, parts, residual, gain):
    return pl.pallas_call(
        stream_kernel,
        out_shape=shape((ROWS + 16, HALF), BF16),
        in_specs=[scalars()] + [whole(a.shape) for a in (parts, residual, gain)],
        out_specs=whole((ROWS + 16, HALF)),
        compiler_params=params(16),
        name="stream",
    )(place, parts, residual, gain)


def gate_kernel(place, mine_ref, other_ref, gate_ref, up_ref, out_ref, own_ref, x, gate, up, squares):
    step = pl.program_id(0)

    @pl.when(step == 0)
    def _():
        even = place[2] == 0
        mine, other = mine_ref[...].astype(F32), other_ref[...].astype(F32)
        halves = (jnp.where(even, mine, other), jnp.where(even, other, mine))
        square = jnp.zeros((ROWS, OWN), F32)
        own = jnp.zeros((ROWS, OWN), F32)
        for y in range(4):
            for c in range(2):
                block = halves[c][:ROWS, y * OWN : (y + 1) * OWN]
                gain = halves[c][ROWS : ROWS + 1, y * OWN : (y + 1) * OWN]
                at = (2 * y + c) * OWN
                x[:, at : at + OWN] = (block * gain).astype(BF16)
                square += block * block
            own += jnp.where(place[3] == y, mine[:ROWS, y * OWN : (y + 1) * OWN], 0.0)
        own_ref[...] = own
        total = jnp.sum(square, axis=1, keepdims=True)
        high = total.astype(BF16).astype(F32)
        lane = lax.broadcasted_iota(jnp.int32, (ROWS, EXTRA), 1)
        squares[...] = jnp.where(lane < 64, high, total - high)

    gate[step] = jnp.dot(x[...], gate_ref[...], preferred_element_type=F32)
    up[step] = jnp.dot(x[...], up_ref[...], preferred_element_type=F32)

    @pl.when(step == pl.num_programs(0) - 1)
    def _():
        for d in range(N_KV):
            rows = slice(4 * (d // 2), 4 * (d // 2) + 4)
            for t in range(13):
                tile = 13 * (d % 2) + t
                lanes = slice((tile % 2) * 128, (tile % 2) * 128 + 128)
                out_ref[d, :, t * 128 : (t + 1) * 128] = gate[tile // 2, rows, lanes].astype(BF16)
                at = PART + t * 128
                out_ref[d, :, at : at + 128] = up[tile // 2, rows, lanes].astype(BF16)
            out_ref[d, :, 2 * PART :] = squares[rows, :].astype(BF16)


def gate_up(place, mine, other, w_gate, w_up):
    steps = UNITS // TILE
    block = pl.BlockSpec((w_gate.shape[0], TILE), lambda i: (0, i))
    held = pltpu.VMEM((steps, ROWS, TILE), F32)
    wide = (N_KV, 4, 2 * PART + EXTRA)
    return pl.pallas_call(
        gate_kernel,
        grid=(steps,),
        out_shape=[shape(wide, BF16), shape((ROWS, OWN), F32)],
        in_specs=[scalars(), whole(mine.shape), whole(other.shape), block, block],
        out_specs=[whole(wide), whole((ROWS, OWN))],
        scratch_shapes=[
            pltpu.VMEM((ROWS, w_gate.shape[0]), BF16), held, held, pltpu.VMEM((ROWS, EXTRA), F32),
        ],
        compiler_params=params(16, 1),
        name="gate_up",
    )(place, mine, other, w_gate, w_up)


def hidden_kernel(parts_ref, out_ref):
    total = parts_ref[0].astype(F32)
    for i in range(1, N_KV):
        total += parts_ref[i].astype(F32)
    squares = total[:, 2 * PART : 2 * PART + 1] + total[:, 2 * PART + 64 : 2 * PART + 65]
    scale = lax.rsqrt(squares / (HQ * HD) + 1e-05)
    gate, up = total[:, :PART] * scale, total[:, PART : 2 * PART] * scale
    hidden = (gate / (1.0 + jnp.exp(-gate)) * up).astype(BF16)
    for i in range(N_KV):
        out_ref[i] = hidden


def hidden_units(parts):
    return pl.pallas_call(
        hidden_kernel,
        out_shape=shape((N_KV, 4, PART), BF16),
        in_specs=[whole(parts.shape)],
        out_specs=whole((N_KV, 4, PART)),
        compiler_params=params(16),
        name="hidden_units",
    )(parts)


def down_kernel(place, parts_ref, w_ref, keep_ref, give_ref, x, total):
    step = pl.program_id(0)

    @pl.when(step == 0)
    def _():
        for d in range(N_KV):
            piece = parts_ref[d].astype(F32)
            rows = slice(4 * (d // 2), 4 * (d // 2) + 4)
            for t in range(13):
                tile = 13 * (d % 2) + t
                lanes = slice((tile % 2) * 128, (tile % 2) * 128 + 128)
                x[tile // 2, rows, lanes] = piece[:, t * 128 : (t + 1) * 128]
        total[...] = jnp.zeros(total.shape, F32)

    total[...] += jnp.dot(x[step].astype(BF16), w_ref[...], preferred_element_type=F32)

    @pl.when(step == pl.num_programs(0) - 1)
    def _():
        even = place[2] == 0
        for y in range(4):
            zero = total[:, (2 * y) * OWN : (2 * y + 1) * OWN]
            one = total[:, (2 * y + 1) * OWN : (2 * y + 2) * OWN]
            keep_ref[y] = jnp.where(even, zero, one)
            give_ref[y] = jnp.where(even, one, zero).astype(BF16)


def down(place, parts, w_down):
    steps = UNITS // TILE
    out = (4, ROWS, OWN)
    return pl.pallas_call(
        down_kernel,
        grid=(steps,),
        out_shape=[shape(out, F32), shape(out, BF16)],
        in_specs=[
            scalars(), whole(parts.shape),
            pl.BlockSpec((TILE, w_down.shape[1]), lambda i: (i, 0)),
        ],
        out_specs=[whole(out), whole(out)],
        scratch_shapes=[
            pltpu.VMEM((steps, ROWS, TILE), F32), pltpu.VMEM((ROWS, w_down.shape[1]), F32),
        ],
        compiler_params=params(16, 1),
        name="down",
    )(place, parts, w_down)


def split_kernel(place, keep_ref, got_ref, *outs):
    for i, out_ref in enumerate(outs):
        at = place[3] ^ i
        out_ref[...] = (keep_ref[at] + got_ref[at].astype(F32)).astype(out_ref.dtype)


def split(place, keep, got):
    each = (ROWS, OWN)
    return pl.pallas_call(
        split_kernel,
        out_shape=[shape(each, F32)] + [shape(each, BF16)] * 3,
        in_specs=[scalars(), whole(keep.shape), whole(got.shape)],
        out_specs=[whole(each)] * 4,
        compiler_params=params(16),
        name="split",
    )(place, keep, got)


def exchange(value, axis):
    return lax.all_to_all(value, axis, 0, 0, tiled=True)


def swap(value, step):
    return lax.ppermute(value, "head", [(j, j ^ step) for j in range(KVH)])


def on_device(
    queries,
    key_cache,
    value_cache,
    block_table,
    lengths,
    new_keys,
    new_values,
    residual,
    out_weight,
    norm_gain,
    w_gate,
    w_up,
    w_down,
):
    me_kv, me_head = lax.axis_index("kv"), lax.axis_index("head")
    place = jnp.stack([me_kv, me_head, me_head % 2, me_head // 2]).astype(jnp.int32)
    partials = attention_partials(block_table, lengths, queries, key_cache, value_cache)
    keep, give = project(place, exchange(partials, "kv"), queries, new_keys, new_values, out_weight[0, 0])
    parts = exchange(add_pair(keep, swap(give, 1)), "kv")
    here = stream(place, parts, residual, norm_gain[None])
    here = (here.astype(F32) + swap(here, 2).astype(F32)).astype(BF16)
    here = (here.astype(F32) + swap(here, 4).astype(F32)).astype(BF16)
    gates, own = gate_up(place, here, swap(here, 1), w_gate, w_up)
    hidden = exchange(hidden_units(exchange(gates, "kv")), "kv")
    keep, give = down(place, hidden, w_down)
    mine, one, two, three = split(place, keep, swap(give, 1))
    total = own + mine
    for piece, step in ((one, 2), (two, 4), (three, 6)):
        total = total + swap(piece, step).astype(F32)
    return total.astype(BF16)


def solution(mesh):
    in_specs = (
        P(None, "head"),
        P("kv", "head", None, None),
        P("kv", "head", None, None),
        P(None, "kv"),
        P(),
        P(None, "head"),
        P(None, "head"),
        P(None, ("kv", "head")),
        P("head", "kv", None, None),
        P(("kv", "head")),
        P("kv", "head"),
        P("kv", "head"),
        P("head", "kv"),
    )
    out_specs = P(None, ("kv", "head"))
    return jax.shard_map(
        on_device, mesh=mesh, in_specs=in_specs, out_specs=out_specs, check_vma=False
    )
```

```python
import functools
import math

import jax
import jax.numpy as jnp
from jax import lax
from jax.experimental import pallas as pl
from jax.experimental.pallas import tpu as pltpu
from jax.sharding import PartitionSpec as P

HQ = 128
KVH = 8
SEQS = 16
ROWS = 2 * SEQS
GROUP = HQ // KVH
HD = 128
SLOTS = 24
OWN = 128
HALF = 4 * OWN
N_KV = 16
UNITS = 3328
PART = UNITS // 2
EXTRA = 128
TILE = 256

F32 = jnp.float32
BF16 = jnp.bfloat16
MIB = 1 << 20
W_SPACE = pltpu.HBM


def whole(shape, space=pltpu.VMEM):
    zeros = (0,) * len(shape)
    return pl.BlockSpec(shape, lambda *_: zeros, memory_space=space)


def is_even():
    return lax.axis_index("head") % 2 == 0


def own_y():
    return lax.axis_index("head") // 2


def params(mib, steps=0):
    kinds = ("arbitrary",) * steps if steps else None
    return pltpu.CompilerParams(vmem_limit_bytes=mib * MIB, dimension_semantics=kinds)


def in_hbm(array):
    return pltpu.with_memory_space_constraint(array, pltpu.HBM)


def cost(flops, moved):
    return pl.CostEstimate(flops=flops, bytes_accessed=moved, transcendentals=0)


def shape(dims, kind):
    return jax.ShapeDtypeStruct(dims, kind)


def parts_of_copy(src, dst, sems):
    count = sems.shape[0]
    deep = dst.shape[0] // count
    return [
        pltpu.make_async_copy(
            src.at[i * deep : (i + 1) * deep, :], dst.at[i * deep : (i + 1) * deep, :], sems.at[i]
        )
        for i in range(count)
    ]


def attention_kernel(
    table_hbm, lengths_hbm, q_hbm, k_hbm, v_hbm, new_k_hbm, new_v_hbm, w_hbm,
    out_ref, w_ref, table, lengths, q_ref, k_ref, v_ref, new_k, new_v, sems, w_sems,
    q_rows, scores, tops, sums, numer,
):
    pairs = (
        (table_hbm, table), (lengths_hbm, lengths), (q_hbm, q_ref), (k_hbm, k_ref), (v_hbm, v_ref),
        (new_k_hbm, new_k), (new_v_hbm, new_v),
    )
    copies = [pltpu.make_async_copy(src, dst, sems.at[i]) for i, (src, dst) in enumerate(pairs)]
    for i in (2, 0, 1, 5, 6, 3, 4):
        copies[i].start()
    w_copies = parts_of_copy(w_hbm, w_ref, w_sems)
    for copy in w_copies:
        copy.start()
    tops[...] = jnp.full(tops.shape, -1e30, F32)
    sums[...] = jnp.zeros(sums.shape, F32)
    numer[...] = jnp.zeros(numer.shape, F32)
    lane = lax.broadcasted_iota(jnp.int32, (ROWS, HD), 1)
    unit = 1.0 / math.sqrt(HD)
    copies[2].wait()
    for g in range(GROUP):
        q_rows[pl.ds(g, ROWS, stride=GROUP), :] = q_ref[:, g * HD : (g + 1) * HD].astype(F32)
    copies[5].wait()
    copies[6].wait()
    mine = pl.ds(lax.axis_index("kv"), ROWS, stride=GROUP)
    query = q_rows[mine, :]
    keys, values = new_k[...].astype(F32), new_v[...].astype(F32)
    odd = lax.broadcasted_iota(jnp.int32, (ROWS, 1), 0) % 2 == 1
    at_own = jnp.sum(query * keys, axis=1, keepdims=True) * unit
    at_prev = jnp.sum(query * pltpu.roll(keys, 1, 0), axis=1, keepdims=True) * unit
    new_max = jnp.where(odd, jnp.maximum(at_own, at_prev), at_own)
    expo_own = jnp.exp(at_own - new_max)
    expo_prev = jnp.where(odd, jnp.exp(at_prev - new_max), 0.0)
    new_out = expo_own.astype(BF16).astype(F32) * values
    new_out += expo_prev.astype(BF16).astype(F32) * pltpu.roll(values, 1, 0)
    tops[mine, :] = jnp.broadcast_to(new_max, (ROWS, HD))
    copies[0].wait()
    copies[1].wait()
    copies[3].wait()
    rows_of = []
    for b in range(SLOTS):
        seq = table[0, b]
        limit = lengths[seq] - table[1, b] * HD
        here = pl.ds(pl.multiple_of(seq * ROWS, ROWS), ROWS)
        rows_of.append(here)
        raw = lax.dot_general(
            q_rows[here, :].astype(BF16), k_ref[b, 0], (((1,), (1,)), ((), ())),
            preferred_element_type=F32,
        )
        masked = jnp.where(lane < limit, raw * unit, -1e30)
        scores[b] = masked
        tops[here, :] = jnp.maximum(tops[here, :], jnp.max(masked, axis=1, keepdims=True))
    tops[...] = tops[...].astype(BF16).astype(F32)
    new_scale = jnp.exp(new_max - tops[mine, :])
    sums[mine, :] = new_scale * (expo_own + expo_prev)
    numer[mine, :] = new_scale * new_out
    copies[4].wait()
    for b in range(SLOTS):
        here = rows_of[b]
        masked = scores[b]
        expo = jnp.where(masked > -1e29, jnp.exp(masked - tops[here, :]), 0.0)
        sums[here, :] += jnp.sum(expo, axis=1, keepdims=True)
        numer[here, :] += jnp.dot(expo.astype(BF16), v_ref[b, 0], preferred_element_type=F32)
    by_head = lax.broadcasted_iota(jnp.int32, (GROUP, HD), 1)
    stats = jnp.zeros((GROUP, HD), F32)
    for row in range(ROWS):
        heads = slice(row * GROUP, (row + 1) * GROUP)
        high = sums[heads, :].astype(BF16).astype(F32)
        stats = jnp.where(by_head == row, tops[heads, :], stats)
        stats = jnp.where(by_head == row + ROWS, high, stats)
        stats = jnp.where(by_head == row + 2 * ROWS, sums[heads, :] - high, stats)
    for g in range(GROUP):
        out_ref[g, :ROWS, :] = numer[pl.ds(g, ROWS, stride=GROUP), :].astype(BF16)
        out_ref[g, ROWS:, :] = jnp.broadcast_to(stats[g : g + 1, :], (16, HD)).astype(BF16)
    for copy in w_copies:
        copy.wait()


def attention_partials(
    table, lengths, queries, key_cache, value_cache, new_keys, new_values, weight
):
    tall = pltpu.VMEM((ROWS * GROUP, HD), F32)
    arrays = (queries, key_cache, value_cache, new_keys, new_values)
    return pl.pallas_call(
        attention_kernel,
        out_shape=[shape((GROUP, ROWS + 16, HD), BF16), shape(weight.shape, BF16)],
        in_specs=[pl.BlockSpec(memory_space=W_SPACE)] * 8,
        out_specs=[whole((GROUP, ROWS + 16, HD)), whole(weight.shape)],
        scratch_shapes=[pltpu.SMEM(table.shape, jnp.int32), pltpu.SMEM(lengths.shape, jnp.int32)]
        + [pltpu.VMEM(a.shape, BF16) for a in arrays]
        + [pltpu.SemaphoreType.DMA((7,)), pltpu.SemaphoreType.DMA((8,))]
        + [tall, pltpu.VMEM((SLOTS, ROWS, HD), F32), tall, tall, tall],
        compiler_params=params(16),
        cost_estimate=cost(SLOTS * ROWS * HD * HD * 4, 4 * SLOTS * HD * HD),
        name="attention",
    )(*[in_hbm(a) for a in (table, lengths, *arrays, weight)])


def project_kernel(got_ref, w_ref, keep_ref, give_ref):
    row = lax.broadcasted_iota(jnp.int32, (N_KV, HD), 0)
    stats = jnp.zeros((N_KV, HD), F32)
    for i in range(N_KV):
        stats = jnp.where(row == i, got_ref[i, ROWS:, :].astype(F32), stats)
    stats = jnp.concatenate([stats, jnp.zeros((HD - N_KV, HD), F32)], axis=0).T
    maxes = stats[:ROWS]
    lane = lax.broadcasted_iota(jnp.int32, (ROWS, HD), 1)
    real = lane < N_KV
    peak = jnp.max(jnp.where(real, maxes, -1e30), axis=1, keepdims=True)
    scales = jnp.where(real, jnp.exp(maxes - peak), 0.0)
    denom = jnp.sum(scales * (stats[ROWS : 2 * ROWS] + stats[2 * ROWS : 3 * ROWS]), axis=1, keepdims=True)
    total = jnp.zeros((ROWS, HD), F32)
    for i in range(N_KV):
        total += scales[:, i : i + 1] * got_ref[i, :ROWS, :].astype(F32)
    attn = (total / denom).astype(BF16)
    even = is_even()
    for d in range(N_KV):
        for y in range(4):
            at = d * 2 * HALF + y * TILE
            both = jnp.dot(attn, w_ref[:, at : at + TILE], preferred_element_type=F32)
            here = slice(y * OWN, (y + 1) * OWN)
            keep_ref[d, :, here] = jnp.where(even, both[:, :OWN], both[:, OWN:])
            give_ref[d, :, here] = jnp.where(even, both[:, OWN:], both[:, :OWN]).astype(BF16)


def project(got, weight):
    out = (N_KV, ROWS, HALF)
    return pl.pallas_call(
        project_kernel,
        out_shape=[shape(out, F32), shape(out, BF16)],
        in_specs=[whole(got.shape), whole(weight.shape)],
        out_specs=[whole(out), whole(out)],
        compiler_params=params(8),
        cost_estimate=cost(2 * ROWS * weight.size, 2 * weight.size),
        name="project",
    )(got, weight)


def pair_kernel(keep_ref, got_ref, out_ref):
    out_ref[...] = (keep_ref[...] + got_ref[...].astype(F32)).astype(BF16)


def add_pair(keep, got):
    return pl.pallas_call(
        pair_kernel,
        out_shape=shape(keep.shape, BF16),
        in_specs=[whole(keep.shape), whole(got.shape)],
        out_specs=whole(keep.shape),
        compiler_params=params(8),
        name="add_pair",
    )(keep, got)


def stream_kernel(parts_ref, res_ref, gain_ref, out_ref):
    total = parts_ref[0].astype(F32)
    for i in range(1, N_KV):
        total += parts_ref[i].astype(F32)
    me = own_y()
    blocks = []
    for y in range(4):
        rest = jnp.where(me == y, res_ref[...].astype(F32), 0.0)
        blocks.append(total[:, y * OWN : (y + 1) * OWN] + rest)
    row = lax.broadcasted_iota(jnp.int32, (ROWS, OWN), 0)
    blocks.append(jnp.where(row == me, gain_ref[...].astype(F32), 0.0))
    out_ref[...] = jnp.concatenate(blocks, axis=1).astype(BF16)


def stream(parts, residual, gain):
    out = (ROWS, HALF + OWN)
    return pl.pallas_call(
        stream_kernel,
        out_shape=shape(out, BF16),
        in_specs=[whole(a.shape) for a in (parts, residual, gain)],
        out_specs=whole(out),
        compiler_params=params(8),
        name="stream",
    )(parts, residual, gain)


def gate_kernel(mine_ref, other_ref, gate_a, gate_b, up_a, up_b, out_ref, own_ref):
    tiles = UNITS // TILE
    deep = gate_a.shape[0]
    even = is_even()
    mine, other = mine_ref[...].astype(F32), other_ref[...].astype(F32)
    halves = (jnp.where(even, mine, other), jnp.where(even, other, mine))
    square = jnp.zeros((ROWS, OWN), F32)
    own = jnp.zeros((ROWS, OWN), F32)
    blocks = []
    for y in range(4):
        for c in range(2):
            block = halves[c][:, y * OWN : (y + 1) * OWN]
            gain = halves[c][y : y + 1, HALF:]
            blocks.append((block * gain).astype(BF16))
            square += block * block
        own += jnp.where(own_y() == y, mine[:, y * OWN : (y + 1) * OWN], 0.0)
    own_ref[...] = own
    x = jnp.concatenate(blocks, axis=1)
    total = jnp.sum(square, axis=1, keepdims=True)
    high = total.astype(BF16).astype(F32)
    lane = lax.broadcasted_iota(jnp.int32, (ROWS, EXTRA), 1)
    squares = jnp.where(lane < 64, high, total - high).astype(BF16).astype(F32)
    for d in range(N_KV):
        out_ref[d, :, 2 * PART :] = squares[4 * (d // 2) : 4 * (d // 2) + 4, :].astype(BF16)
    for tile in range(tiles):
        for which in range(2):
            upper, lower = ((gate_a, gate_b), (up_a, up_b))[which]
            lanes = slice(tile * TILE, (tile + 1) * TILE)
            result = jnp.dot(x[:, :deep], upper[:, lanes], preferred_element_type=F32)
            result += jnp.dot(x[:, deep:], lower[:, lanes], preferred_element_type=F32)
            for part in range(2):
                column = 2 * tile + part
                at = which * PART + column % 13 * 128
                for r in range(8):
                    piece = result[4 * r : 4 * r + 4, part * 128 : (part + 1) * 128]
                    out_ref[2 * r + column // 13, :, at : at + 128] = piece.astype(BF16)


def gate_up(mine, other, gates, ups):
    wide = (N_KV, 4, 2 * PART + EXTRA)
    return pl.pallas_call(
        gate_kernel,
        out_shape=[shape(wide, BF16), shape((ROWS, OWN), F32)],
        in_specs=[whole(a.shape) for a in (mine, other, *gates, *ups)],
        out_specs=[whole(wide), whole((ROWS, OWN))],
        compiler_params=params(8),
        cost_estimate=cost(8 * ROWS * gates[0].size, 8 * gates[0].size),
        name="gate_up",
    )(mine, other, *gates, *ups)


def load_kernel(start, after_ref, w_hbm, out_ref, sems):
    copies = parts_of_copy(w_hbm.at[start : start + out_ref.shape[0], :], out_ref, sems)
    for copy in copies:
        copy.start()
    for copy in copies:
        copy.wait()


def load(weight, half, after):
    rows = weight.shape[0] // 2
    return pl.pallas_call(
        functools.partial(load_kernel, half * rows),
        out_shape=shape((rows, weight.shape[1]), BF16),
        in_specs=[pl.BlockSpec(memory_space=pl.ANY), pl.BlockSpec(memory_space=W_SPACE)],
        out_specs=whole((rows, weight.shape[1])),
        scratch_shapes=[pltpu.SemaphoreType.DMA((8,))],
        compiler_params=params(8),
        cost_estimate=cost(0, 2 * weight.size),
        name="load",
    )(after, in_hbm(weight))


def hidden_kernel(parts_ref, out_ref):
    total = parts_ref[0].astype(F32)
    for i in range(1, N_KV):
        total += parts_ref[i].astype(F32)
    squares = total[:, 2 * PART : 2 * PART + 1] + total[:, 2 * PART + 64 : 2 * PART + 65]
    scale = lax.rsqrt(squares / (HQ * HD) + 1e-05)
    gate, up = total[:, :PART] * scale, total[:, PART : 2 * PART] * scale
    hidden = (gate / (1.0 + jnp.exp(-gate)) * up).astype(BF16)
    for i in range(N_KV):
        out_ref[i] = hidden


def hidden_units(parts):
    return pl.pallas_call(
        hidden_kernel,
        out_shape=shape((N_KV, 4, PART), BF16),
        in_specs=[whole(parts.shape)],
        out_specs=whole((N_KV, 4, PART)),
        compiler_params=params(8),
        name="hidden_units",
    )(parts)


def down_kernel(parts_ref, w_ref, out_ref, x):
    for d in range(N_KV):
        x[4 * (d // 2) : 4 * (d // 2) + 4, d % 2 * PART : d % 2 * PART + PART] = parts_ref[d].astype(F32)
    total = jnp.dot(x[...].astype(BF16), w_ref[...], preferred_element_type=F32)
    for i in range(KVH):
        out_ref[i] = total[:, i * OWN : (i + 1) * OWN].astype(BF16)


def down(parts, w_down):
    out = (KVH, ROWS, OWN)
    return pl.pallas_call(
        down_kernel,
        out_shape=shape(out, BF16),
        in_specs=[whole(parts.shape), whole(w_down.shape)],
        out_specs=whole(out),
        scratch_shapes=[pltpu.VMEM((ROWS, UNITS), F32)],
        compiler_params=params(8),
        cost_estimate=cost(2 * ROWS * w_down.size, 2 * w_down.size),
        name="down",
    )(parts, w_down)


def finish_kernel(own_ref, parts_ref, out_ref):
    total = own_ref[...]
    for i in range(KVH):
        total += parts_ref[i].astype(F32)
    out_ref[...] = total.astype(BF16)


def finish(own, parts):
    return pl.pallas_call(
        finish_kernel,
        out_shape=shape(own.shape, BF16),
        in_specs=[whole(own.shape), whole(parts.shape)],
        out_specs=whole(own.shape),
        compiler_params=params(8),
        name="finish",
    )(own, parts)


def exchange(value, axis):
    return lax.all_to_all(value, axis, 0, 0, tiled=True)


def swap(value, step):
    return lax.ppermute(value, "head", [(j, j ^ step) for j in range(KVH)])


def swap_beside(value, step, weight, half):
    return lax.optimization_barrier((swap(value, step), load(weight, half, value)))


def on_device(
    queries,
    key_cache,
    value_cache,
    block_table,
    lengths,
    new_keys,
    new_values,
    residual,
    out_weight,
    norm_gain,
    w_gate,
    w_up,
    w_down,
):
    partials, weight = attention_partials(
        block_table, lengths, queries, key_cache, value_cache, new_keys, new_values, out_weight[0, 0]
    )
    keep, give = project(exchange(partials, "kv"), weight)
    swapped, up_a = swap_beside(give, 1, w_up, 0)
    parts = exchange(add_pair(keep, swapped), "kv")
    here = stream(parts, residual, norm_gain[None])
    swapped, up_b = swap_beside(here, 2, w_up, 1)
    here = (here.astype(F32) + swapped.astype(F32)).astype(BF16)
    swapped, gate_a = swap_beside(here, 6, w_gate, 0)
    here = (here.astype(F32) + swapped.astype(F32)).astype(BF16)
    other, gate_b = swap_beside(here, 1, w_gate, 1)
    gates, own = gate_up(here, other, (gate_a, gate_b), (up_a, up_b))
    hidden = exchange(hidden_units(exchange(gates, "kv")), "kv")
    parts = exchange(down(hidden, w_down), "head")
    return finish(own, parts)


def solution(mesh):
    in_specs = (
        P(None, "head"),
        P("kv", "head", None, None),
        P("kv", "head", None, None),
        P(None, "kv"),
        P(),
        P(None, "head"),
        P(None, "head"),
        P(None, ("kv", "head")),
        P("head", "kv", None, None),
        P(("kv", "head")),
        P("kv", "head"),
        P("kv", "head"),
        P("head", "kv"),
    )
    out_specs = P(None, ("kv", "head"))
    return jax.shard_map(
        on_device, mesh=mesh, in_specs=in_specs, out_specs=out_specs, check_vma=False
    )
```

```python
import math

import jax
import jax.numpy as jnp
from jax import lax
from jax.experimental import pallas as pl
from jax.experimental.pallas import tpu as pltpu
from jax.sharding import PartitionSpec as P

HQ = 128
KVH = 8
SEQS = 16
ROWS = 2 * SEQS
GROUP = HQ // KVH
HD = 128
SLOTS = 24
OWN = 128
HALF = 4 * OWN
N_KV = 16
UNITS = 3328
PART = UNITS // 2
EXTRA = 128
TILE = 256

F32 = jnp.float32
BF16 = jnp.bfloat16
MIB = 1 << 20
W_SPACE = pltpu.HBM
ATTENTION_ROOM = 58


def whole(shape, space=pltpu.VMEM):
    zeros = (0,) * len(shape)
    return pl.BlockSpec(shape, lambda *_: zeros, memory_space=space)


def is_even():
    return lax.axis_index("head") % 2 == 0


def own_y():
    return lax.axis_index("head") // 2


def params(mib, steps=0):
    kinds = ("arbitrary",) * steps if steps else None
    return pltpu.CompilerParams(vmem_limit_bytes=mib * MIB, dimension_semantics=kinds)


def in_hbm(array):
    return pltpu.with_memory_space_constraint(array, pltpu.HBM)


def in_vmem(array):
    return pltpu.with_memory_space_constraint(array, pltpu.VMEM)


def cost(flops, moved):
    return pl.CostEstimate(flops=flops, bytes_accessed=moved, transcendentals=0)


def shape(dims, kind):
    return jax.ShapeDtypeStruct(dims, kind)


def parts_of_copy(src, dst, sems):
    count = sems.shape[0]
    deep = dst.shape[0] // count
    return [
        pltpu.make_async_copy(
            src.at[i * deep : (i + 1) * deep, :], dst.at[i * deep : (i + 1) * deep, :], sems.at[i]
        )
        for i in range(count)
    ]


def attention_kernel(
    table_hbm, lengths_hbm, q_hbm, k_hbm, v_hbm, new_k_hbm, new_v_hbm, w_hbm,
    out_ref, w_ref, table, lengths, q_ref, k_ref, v_ref, new_k, new_v, sems, w_sems,
    q_rows, scores, tops, sums, numer,
):
    pairs = (
        (table_hbm, table), (lengths_hbm, lengths), (q_hbm, q_ref), (k_hbm, k_ref), (v_hbm, v_ref),
        (new_k_hbm, new_k), (new_v_hbm, new_v),
    )
    copies = [pltpu.make_async_copy(src, dst, sems.at[i]) for i, (src, dst) in enumerate(pairs)]
    for i in (2, 0, 1, 5, 6, 3, 4):
        copies[i].start()
    w_copies = parts_of_copy(w_hbm, w_ref, w_sems)
    for copy in w_copies:
        copy.start()
    tops[...] = jnp.full(tops.shape, -1e30, F32)
    sums[...] = jnp.zeros(sums.shape, F32)
    numer[...] = jnp.zeros(numer.shape, F32)
    lane = lax.broadcasted_iota(jnp.int32, (ROWS, HD), 1)
    unit = 1.0 / math.sqrt(HD)
    copies[2].wait()
    for g in range(GROUP):
        q_rows[pl.ds(g, ROWS, stride=GROUP), :] = q_ref[:, g * HD : (g + 1) * HD].astype(F32)
    copies[5].wait()
    copies[6].wait()
    mine = pl.ds(lax.axis_index("kv"), ROWS, stride=GROUP)
    query = q_rows[mine, :]
    keys, values = new_k[...].astype(F32), new_v[...].astype(F32)
    odd = lax.broadcasted_iota(jnp.int32, (ROWS, 1), 0) % 2 == 1
    at_own = jnp.sum(query * keys, axis=1, keepdims=True) * unit
    at_prev = jnp.sum(query * pltpu.roll(keys, 1, 0), axis=1, keepdims=True) * unit
    new_max = jnp.where(odd, jnp.maximum(at_own, at_prev), at_own)
    expo_own = jnp.exp(at_own - new_max)
    expo_prev = jnp.where(odd, jnp.exp(at_prev - new_max), 0.0)
    new_out = expo_own.astype(BF16).astype(F32) * values
    new_out += expo_prev.astype(BF16).astype(F32) * pltpu.roll(values, 1, 0)
    tops[mine, :] = jnp.broadcast_to(new_max, (ROWS, HD))
    copies[0].wait()
    copies[1].wait()
    copies[3].wait()
    rows_of = []
    for b in range(SLOTS):
        seq = table[0, b]
        limit = lengths[seq] - table[1, b] * HD
        here = pl.ds(pl.multiple_of(seq * ROWS, ROWS), ROWS)
        rows_of.append(here)
        raw = lax.dot_general(
            q_rows[here, :].astype(BF16), k_ref[b, 0], (((1,), (1,)), ((), ())),
            preferred_element_type=F32,
        )
        masked = jnp.where(lane < limit, raw * unit, -1e30)
        scores[b] = masked
        tops[here, :] = jnp.maximum(tops[here, :], jnp.max(masked, axis=1, keepdims=True))
    tops[...] = tops[...].astype(BF16).astype(F32)
    new_scale = jnp.exp(new_max - tops[mine, :])
    sums[mine, :] = new_scale * (expo_own + expo_prev)
    numer[mine, :] = new_scale * new_out
    copies[4].wait()
    for b in range(SLOTS):
        here = rows_of[b]
        masked = scores[b]
        expo = jnp.where(masked > -1e29, jnp.exp(masked - tops[here, :]), 0.0)
        sums[here, :] += jnp.sum(expo, axis=1, keepdims=True)
        numer[here, :] += jnp.dot(expo.astype(BF16), v_ref[b, 0], preferred_element_type=F32)
    by_head = lax.broadcasted_iota(jnp.int32, (GROUP, HD), 1)
    stats = jnp.zeros((GROUP, HD), F32)
    for row in range(ROWS):
        heads = slice(row * GROUP, (row + 1) * GROUP)
        high = sums[heads, :].astype(BF16).astype(F32)
        stats = jnp.where(by_head == row, tops[heads, :], stats)
        stats = jnp.where(by_head == row + ROWS, high, stats)
        stats = jnp.where(by_head == row + 2 * ROWS, sums[heads, :] - high, stats)
    for g in range(GROUP):
        out_ref[g, :ROWS, :] = numer[pl.ds(g, ROWS, stride=GROUP), :].astype(BF16)
        out_ref[g, ROWS:, :] = jnp.broadcast_to(stats[g : g + 1, :], (16, HD)).astype(BF16)
    for copy in w_copies:
        copy.wait()


def attention_partials(
    table, lengths, queries, key_cache, value_cache, new_keys, new_values, weight
):
    tall = pltpu.VMEM((ROWS * GROUP, HD), F32)
    arrays = (queries, key_cache, value_cache, new_keys, new_values)
    return pl.pallas_call(
        attention_kernel,
        out_shape=[shape((GROUP, ROWS + 16, HD), BF16), pltpu.VMEM(weight.shape, BF16)],
        in_specs=[pl.BlockSpec(memory_space=W_SPACE)] * 8,
        out_specs=[whole((GROUP, ROWS + 16, HD)), whole(weight.shape)],
        scratch_shapes=[pltpu.SMEM(table.shape, jnp.int32), pltpu.SMEM(lengths.shape, jnp.int32)]
        + [pltpu.VMEM(a.shape, BF16) for a in arrays]
        + [pltpu.SemaphoreType.DMA((7,)), pltpu.SemaphoreType.DMA((8,))]
        + [tall, pltpu.VMEM((SLOTS, ROWS, HD), F32), tall, tall, tall],
        compiler_params=params(ATTENTION_ROOM),
        cost_estimate=cost(SLOTS * ROWS * HD * HD * 4, 4 * SLOTS * HD * HD),
        name="attention",
    )(*[in_hbm(a) for a in (table, lengths, *arrays, weight)])


def project_kernel(got_ref, w_ref, keep_ref, give_ref):
    row = lax.broadcasted_iota(jnp.int32, (N_KV, HD), 0)
    stats = jnp.zeros((N_KV, HD), F32)
    for i in range(N_KV):
        stats = jnp.where(row == i, got_ref[i, ROWS:, :].astype(F32), stats)
    stats = jnp.concatenate([stats, jnp.zeros((HD - N_KV, HD), F32)], axis=0).T
    maxes = stats[:ROWS]
    lane = lax.broadcasted_iota(jnp.int32, (ROWS, HD), 1)
    real = lane < N_KV
    peak = jnp.max(jnp.where(real, maxes, -1e30), axis=1, keepdims=True)
    scales = jnp.where(real, jnp.exp(maxes - peak), 0.0)
    denom = jnp.sum(scales * (stats[ROWS : 2 * ROWS] + stats[2 * ROWS : 3 * ROWS]), axis=1, keepdims=True)
    total = jnp.zeros((ROWS, HD), F32)
    for i in range(N_KV):
        total += scales[:, i : i + 1] * got_ref[i, :ROWS, :].astype(F32)
    attn = (total / denom).astype(BF16)
    even = is_even()
    for d in range(N_KV):
        for y in range(4):
            at = d * 2 * HALF + y * TILE
            both = jnp.dot(attn, w_ref[:, at : at + TILE], preferred_element_type=F32)
            here = slice(y * OWN, (y + 1) * OWN)
            keep_ref[d, :, here] = jnp.where(even, both[:, :OWN], both[:, OWN:])
            give_ref[d, :, here] = jnp.where(even, both[:, OWN:], both[:, :OWN]).astype(BF16)


def project(got, weight):
    out = (N_KV, ROWS, HALF)
    return pl.pallas_call(
        project_kernel,
        out_shape=[shape(out, F32), shape(out, BF16)],
        in_specs=[whole(got.shape), whole(weight.shape)],
        out_specs=[whole(out), whole(out)],
        compiler_params=params(8),
        cost_estimate=cost(2 * ROWS * weight.size, 2 * weight.size),
        name="project",
    )(got, weight)


def pair_kernel(keep_ref, got_ref, out_ref):
    out_ref[...] = (keep_ref[...] + got_ref[...].astype(F32)).astype(BF16)


def add_pair(keep, got):
    return pl.pallas_call(
        pair_kernel,
        out_shape=shape(keep.shape, BF16),
        in_specs=[whole(keep.shape), whole(got.shape)],
        out_specs=whole(keep.shape),
        compiler_params=params(8),
        name="add_pair",
    )(keep, got)


def stream_kernel(_, parts_ref, res_ref, gain_ref, out_ref):
    total = parts_ref[0].astype(F32)
    for i in range(1, N_KV):
        total += parts_ref[i].astype(F32)
    me = own_y()
    blocks = []
    for y in range(4):
        rest = jnp.where(me == y, res_ref[...].astype(F32), 0.0)
        blocks.append(total[:, y * OWN : (y + 1) * OWN] + rest)
    blocks.append(jnp.broadcast_to(gain_ref[...].astype(F32), (ROWS, OWN)))
    message = jnp.concatenate(blocks, axis=1).astype(BF16)
    for y in range(4):
        out_ref[y] = message


def stream(parts, residual, gain, held):
    out = (4, ROWS, HALF + OWN)
    return pl.pallas_call(
        stream_kernel,
        out_shape=shape(out, BF16),
        in_specs=[whole(a.shape) for a in (held, parts, residual, gain)],
        out_specs=whole(out),
        compiler_params=params(8),
        name="stream",
    )(in_vmem(held), parts, residual, gain)


def column_kernel(parts_ref, out_ref):
    total = parts_ref[0, :, :HALF].astype(F32)
    for y in range(1, 4):
        total += parts_ref[y, :, :HALF].astype(F32)
    out_ref[:, :HALF] = total.astype(BF16)
    row = lax.broadcasted_iota(jnp.int32, (ROWS, OWN), 0)
    gains = jnp.zeros((ROWS, OWN), F32)
    for y in range(4):
        gains = jnp.where(row == y, parts_ref[y, :, HALF:].astype(F32), gains)
    out_ref[:, HALF:] = gains.astype(BF16)


def add_columns(parts):
    out = parts.shape[1:]
    return pl.pallas_call(
        column_kernel,
        out_shape=shape(out, BF16),
        in_specs=[whole(parts.shape)],
        out_specs=whole(out),
        compiler_params=params(8),
        name="add_columns",
    )(parts)


def gate_kernel(mine_ref, other_ref, gate_w, up_w, out_ref, own_ref):
    tiles = UNITS // TILE
    even = is_even()
    mine, other = mine_ref[...].astype(F32), other_ref[...].astype(F32)
    halves = (jnp.where(even, mine, other), jnp.where(even, other, mine))
    square = jnp.zeros((ROWS, OWN), F32)
    own = jnp.zeros((ROWS, OWN), F32)
    blocks = []
    for y in range(4):
        for c in range(2):
            block = halves[c][:, y * OWN : (y + 1) * OWN]
            gain = halves[c][y : y + 1, HALF:]
            blocks.append((block * gain).astype(BF16))
            square += block * block
        own += jnp.where(own_y() == y, mine[:, y * OWN : (y + 1) * OWN], 0.0)
    own_ref[...] = own
    x = jnp.concatenate(blocks, axis=1)
    total = jnp.sum(square, axis=1, keepdims=True)
    high = total.astype(BF16).astype(F32)
    lane = lax.broadcasted_iota(jnp.int32, (ROWS, EXTRA), 1)
    squares = jnp.where(lane < 64, high, total - high).astype(BF16).astype(F32)
    for d in range(N_KV):
        out_ref[d, :, 2 * PART :] = squares[4 * (d // 2) : 4 * (d // 2) + 4, :].astype(BF16)
    for tile in range(tiles):
        for which in range(2):
            weight = (gate_w, up_w)[which]
            lanes = slice(tile * TILE, (tile + 1) * TILE)
            result = jnp.dot(x, weight[:, lanes], preferred_element_type=F32)
            for part in range(2):
                column = 2 * tile + part
                at = which * PART + column % 13 * 128
                for r in range(8):
                    piece = result[4 * r : 4 * r + 4, part * 128 : (part + 1) * 128]
                    out_ref[2 * r + column // 13, :, at : at + 128] = piece.astype(BF16)


def gate_up(mine, other, w_gate, w_up):
    wide = (N_KV, 4, 2 * PART + EXTRA)
    return pl.pallas_call(
        gate_kernel,
        out_shape=[shape(wide, BF16), shape((ROWS, OWN), F32)],
        in_specs=[whole(a.shape) for a in (mine, other, w_gate, w_up)],
        out_specs=[whole(wide), whole((ROWS, OWN))],
        compiler_params=params(8),
        cost_estimate=cost(4 * ROWS * w_gate.size, 4 * w_gate.size),
        name="gate_up",
    )(mine, other, in_vmem(w_gate), in_vmem(w_up))


def hidden_kernel(parts_ref, out_ref):
    total = parts_ref[0].astype(F32)
    for i in range(1, N_KV):
        total += parts_ref[i].astype(F32)
    squares = total[:, 2 * PART : 2 * PART + 1] + total[:, 2 * PART + 64 : 2 * PART + 65]
    scale = lax.rsqrt(squares / (HQ * HD) + 1e-05)
    gate, up = total[:, :PART] * scale, total[:, PART : 2 * PART] * scale
    hidden = (gate / (1.0 + jnp.exp(-gate)) * up).astype(BF16)
    for i in range(N_KV):
        out_ref[i] = hidden


def hidden_units(parts):
    return pl.pallas_call(
        hidden_kernel,
        out_shape=shape((N_KV, 4, PART), BF16),
        in_specs=[whole(parts.shape)],
        out_specs=whole((N_KV, 4, PART)),
        compiler_params=params(8),
        name="hidden_units",
    )(parts)


def down_kernel(parts_ref, w_ref, out_ref, x):
    for d in range(N_KV):
        x[4 * (d // 2) : 4 * (d // 2) + 4, d % 2 * PART : d % 2 * PART + PART] = parts_ref[d].astype(F32)
    total = jnp.dot(x[...].astype(BF16), w_ref[...], preferred_element_type=F32)
    for i in range(KVH):
        out_ref[i] = total[:, i * OWN : (i + 1) * OWN].astype(BF16)


def down(parts, w_down):
    out = (KVH, ROWS, OWN)
    return pl.pallas_call(
        down_kernel,
        out_shape=shape(out, BF16),
        in_specs=[whole(parts.shape), whole(w_down.shape)],
        out_specs=whole(out),
        scratch_shapes=[pltpu.VMEM((ROWS, UNITS), F32)],
        compiler_params=params(8),
        cost_estimate=cost(2 * ROWS * w_down.size, 2 * w_down.size),
        name="down",
    )(parts, in_vmem(w_down))


def finish_kernel(own_ref, parts_ref, out_ref):
    total = own_ref[...]
    for i in range(KVH):
        total += parts_ref[i].astype(F32)
    out_ref[...] = total.astype(BF16)


def finish(own, parts):
    return pl.pallas_call(
        finish_kernel,
        out_shape=shape(own.shape, BF16),
        in_specs=[whole(own.shape), whole(parts.shape)],
        out_specs=whole(own.shape),
        compiler_params=params(8),
        name="finish",
    )(own, parts)


def exchange(value, axis, groups=None):
    return lax.all_to_all(value, axis, 0, 0, axis_index_groups=groups, tiled=True)


def swap(value, step):
    return lax.ppermute(value, "head", [(j, j ^ step) for j in range(KVH)])


def on_device(
    queries,
    key_cache,
    value_cache,
    block_table,
    lengths,
    new_keys,
    new_values,
    residual,
    out_weight,
    norm_gain,
    w_gate,
    w_up,
    w_down,
):
    partials, weight = attention_partials(
        block_table, lengths, queries, key_cache, value_cache, new_keys, new_values, out_weight[0, 0]
    )
    keep, give = project(exchange(partials, "kv"), weight)
    parts = exchange(add_pair(keep, swap(give, 1)), "kv")
    same_core = [[2 * y + c for y in range(4)] for c in range(2)]
    parts = exchange(stream(parts, residual, norm_gain[None], w_up), "head", same_core)
    here = add_columns(parts)
    gates, own = gate_up(here, swap(here, 1), w_gate, w_up)
    hidden = exchange(hidden_units(exchange(gates, "kv")), "kv")
    parts = exchange(down(hidden, w_down), "head")
    return finish(own, parts)


def solution(mesh):
    in_specs = (
        P(None, "head"),
        P("kv", "head", None, None),
        P("kv", "head", None, None),
        P(None, "kv"),
        P(),
        P(None, "head"),
        P(None, "head"),
        P(None, ("kv", "head")),
        P("head", "kv", None, None),
        P(("kv", "head")),
        P("kv", "head"),
        P("kv", "head"),
        P("head", "kv"),
    )
    out_specs = P(None, ("kv", "head"))
    return jax.shard_map(
        on_device, mesh=mesh, in_specs=in_specs, out_specs=out_specs, check_vma=False
    )
```

```python
import math

import jax
import jax.numpy as jnp
from jax import lax
from jax.experimental import pallas as pl
from jax.experimental.pallas import tpu as pltpu
from jax.sharding import PartitionSpec as P

HQ = 128
KVH = 8
SEQS = 16
ROWS = 2 * SEQS
GROUP = HQ // KVH
HD = 128
SLOTS = 24
OWN = 128
HALF = 4 * OWN
N_KV = 16
UNITS = 3328
PART = UNITS // 2
EXTRA = 128
TILE = 256

F32 = jnp.float32
BF16 = jnp.bfloat16
MIB = 1 << 20
W_SPACE = pltpu.HBM
ATTENTION_ROOM = 57


def whole(shape, space=pltpu.VMEM):
    zeros = (0,) * len(shape)
    return pl.BlockSpec(shape, lambda *_: zeros, memory_space=space)


def is_even():
    return lax.axis_index("head") % 2 == 0


def own_y():
    return lax.axis_index("head") // 2


def params(mib, steps=0):
    kinds = ("arbitrary",) * steps if steps else None
    return pltpu.CompilerParams(vmem_limit_bytes=mib * MIB, dimension_semantics=kinds)


def in_hbm(array):
    return pltpu.with_memory_space_constraint(array, pltpu.HBM)


def in_vmem(array):
    return pltpu.with_memory_space_constraint(array, pltpu.VMEM)


def cost(flops, moved):
    return pl.CostEstimate(flops=flops, bytes_accessed=moved, transcendentals=0)


def shape(dims, kind):
    return jax.ShapeDtypeStruct(dims, kind)


def parts_of_copy(src, dst, sems):
    count = sems.shape[0]
    deep = dst.shape[0] // count
    return [
        pltpu.make_async_copy(
            src.at[i * deep : (i + 1) * deep, :], dst.at[i * deep : (i + 1) * deep, :], sems.at[i]
        )
        for i in range(count)
    ]


def attention_kernel(
    table_hbm, lengths_hbm, q_hbm, k_hbm, v_hbm, new_k_hbm, new_v_hbm, w_hbm,
    out_ref, w_ref, table, lengths, q_ref, k_ref, v_ref, new_k, new_v, sems, w_sems,
    q_rows, scores, tops, sums, numer,
):
    pairs = (
        (table_hbm, table), (lengths_hbm, lengths), (q_hbm, q_ref), (k_hbm, k_ref), (v_hbm, v_ref),
        (new_k_hbm, new_k), (new_v_hbm, new_v),
    )
    copies = [pltpu.make_async_copy(src, dst, sems.at[i]) for i, (src, dst) in enumerate(pairs)]
    for i in (2, 0, 1, 5, 6, 3, 4):
        copies[i].start()
    w_copies = parts_of_copy(w_hbm, w_ref, w_sems)
    for copy in w_copies:
        copy.start()
    tops[...] = jnp.full(tops.shape, -1e30, F32)
    sums[...] = jnp.zeros(sums.shape, F32)
    numer[...] = jnp.zeros(numer.shape, F32)
    lane = lax.broadcasted_iota(jnp.int32, (ROWS, HD), 1)
    unit = 1.0 / math.sqrt(HD)
    copies[2].wait()
    for g in range(GROUP):
        q_rows[pl.ds(g, ROWS, stride=GROUP), :] = q_ref[:, g * HD : (g + 1) * HD].astype(F32)
    copies[5].wait()
    copies[6].wait()
    mine = pl.ds(lax.axis_index("kv"), ROWS, stride=GROUP)
    query = q_rows[mine, :]
    keys, values = new_k[...].astype(F32), new_v[...].astype(F32)
    odd = lax.broadcasted_iota(jnp.int32, (ROWS, 1), 0) % 2 == 1
    at_own = jnp.sum(query * keys, axis=1, keepdims=True) * unit
    at_prev = jnp.sum(query * pltpu.roll(keys, 1, 0), axis=1, keepdims=True) * unit
    new_max = jnp.where(odd, jnp.maximum(at_own, at_prev), at_own)
    expo_own = jnp.exp(at_own - new_max)
    expo_prev = jnp.where(odd, jnp.exp(at_prev - new_max), 0.0)
    new_out = expo_own.astype(BF16).astype(F32) * values
    new_out += expo_prev.astype(BF16).astype(F32) * pltpu.roll(values, 1, 0)
    tops[mine, :] = jnp.broadcast_to(new_max, (ROWS, HD))
    copies[0].wait()
    copies[1].wait()
    copies[3].wait()
    rows_of = []
    for b in range(SLOTS):
        seq = table[0, b]
        limit = lengths[seq] - table[1, b] * HD
        here = pl.ds(pl.multiple_of(seq * ROWS, ROWS), ROWS)
        rows_of.append(here)
        raw = lax.dot_general(
            q_rows[here, :].astype(BF16), k_ref[b, 0], (((1,), (1,)), ((), ())),
            preferred_element_type=F32,
        )
        masked = jnp.where(lane < limit, raw * unit, -1e30)
        scores[b] = masked
        tops[here, :] = jnp.maximum(tops[here, :], jnp.max(masked, axis=1, keepdims=True))
    tops[...] = tops[...].astype(BF16).astype(F32)
    new_scale = jnp.exp(new_max - tops[mine, :])
    sums[mine, :] = new_scale * (expo_own + expo_prev)
    numer[mine, :] = new_scale * new_out
    copies[4].wait()
    for b in range(SLOTS):
        here = rows_of[b]
        masked = scores[b]
        expo = jnp.where(masked > -1e29, jnp.exp(masked - tops[here, :]), 0.0)
        sums[here, :] += jnp.sum(expo, axis=1, keepdims=True)
        numer[here, :] += jnp.dot(expo.astype(BF16), v_ref[b, 0], preferred_element_type=F32)
    by_head = lax.broadcasted_iota(jnp.int32, (GROUP, HD), 1)
    stats = jnp.zeros((GROUP, HD), F32)
    for row in range(ROWS):
        heads = slice(row * GROUP, (row + 1) * GROUP)
        high = sums[heads, :].astype(BF16).astype(F32)
        stats = jnp.where(by_head == row, tops[heads, :], stats)
        stats = jnp.where(by_head == row + ROWS, high, stats)
        stats = jnp.where(by_head == row + 2 * ROWS, sums[heads, :] - high, stats)
    for g in range(GROUP):
        out_ref[g, :ROWS, :] = numer[pl.ds(g, ROWS, stride=GROUP), :].astype(BF16)
        out_ref[g, ROWS:, :] = jnp.broadcast_to(stats[g : g + 1, :], (16, HD)).astype(BF16)
    for copy in w_copies:
        copy.wait()


def attention_partials(
    table, lengths, queries, key_cache, value_cache, new_keys, new_values, weight
):
    tall = pltpu.VMEM((ROWS * GROUP, HD), F32)
    arrays = (queries, key_cache, value_cache, new_keys, new_values)
    return pl.pallas_call(
        attention_kernel,
        out_shape=[pltpu.VMEM((GROUP, ROWS + 16, HD), BF16), pltpu.VMEM(weight.shape, BF16)],
        in_specs=[pl.BlockSpec(memory_space=W_SPACE)] * 8,
        out_specs=[whole((GROUP, ROWS + 16, HD)), whole(weight.shape)],
        scratch_shapes=[pltpu.SMEM(table.shape, jnp.int32), pltpu.SMEM(lengths.shape, jnp.int32)]
        + [pltpu.VMEM(a.shape, BF16) for a in arrays]
        + [pltpu.SemaphoreType.DMA((7,)), pltpu.SemaphoreType.DMA((8,))]
        + [tall, pltpu.VMEM((SLOTS, ROWS, HD), F32), tall, tall, tall],
        compiler_params=params(ATTENTION_ROOM),
        cost_estimate=cost(SLOTS * ROWS * HD * HD * 4, 4 * SLOTS * HD * HD),
        name="attention",
    )(*[in_hbm(a) for a in (table, lengths, *arrays, weight)])


def project_kernel(got_ref, w_ref, keep_ref, give_ref):
    row = lax.broadcasted_iota(jnp.int32, (N_KV, HD), 0)
    stats = jnp.zeros((N_KV, HD), F32)
    for i in range(N_KV):
        stats = jnp.where(row == i, got_ref[i, ROWS:, :].astype(F32), stats)
    stats = jnp.concatenate([stats, jnp.zeros((HD - N_KV, HD), F32)], axis=0).T
    maxes = stats[:ROWS]
    lane = lax.broadcasted_iota(jnp.int32, (ROWS, HD), 1)
    real = lane < N_KV
    peak = jnp.max(jnp.where(real, maxes, -1e30), axis=1, keepdims=True)
    scales = jnp.where(real, jnp.exp(maxes - peak), 0.0)
    denom = jnp.sum(scales * (stats[ROWS : 2 * ROWS] + stats[2 * ROWS : 3 * ROWS]), axis=1, keepdims=True)
    total = jnp.zeros((ROWS, HD), F32)
    for i in range(N_KV):
        total += scales[:, i : i + 1] * got_ref[i, :ROWS, :].astype(F32)
    attn = (total / denom).astype(BF16)
    even = is_even()
    for d in range(N_KV):
        for y in range(4):
            at = d * 2 * HALF + y * TILE
            both = jnp.dot(attn, w_ref[:, at : at + TILE], preferred_element_type=F32)
            here = slice(y * OWN, (y + 1) * OWN)
            keep_ref[d, :, here] = jnp.where(even, both[:, :OWN], both[:, OWN:])
            give_ref[d, :, here] = jnp.where(even, both[:, OWN:], both[:, :OWN]).astype(BF16)


def project(got, weight):
    out = (N_KV, ROWS, HALF)
    return pl.pallas_call(
        project_kernel,
        out_shape=[shape(out, F32), shape(out, BF16)],
        in_specs=[whole(got.shape), whole(weight.shape)],
        out_specs=[whole(out), whole(out)],
        compiler_params=params(8),
        cost_estimate=cost(2 * ROWS * weight.size, 2 * weight.size),
        name="project",
    )(got, weight)


def pair_kernel(keep_ref, got_ref, out_ref):
    out_ref[...] = (keep_ref[...] + got_ref[...].astype(F32)).astype(BF16)


def add_pair(keep, got):
    return pl.pallas_call(
        pair_kernel,
        out_shape=shape(keep.shape, BF16),
        in_specs=[whole(keep.shape), whole(got.shape)],
        out_specs=whole(keep.shape),
        compiler_params=params(8),
        name="add_pair",
    )(keep, got)


def stream_kernel(_, parts_ref, res_ref, gain_ref, out_ref):
    total = parts_ref[0].astype(F32)
    for i in range(1, N_KV):
        total += parts_ref[i].astype(F32)
    me = own_y()
    blocks = []
    for y in range(4):
        rest = jnp.where(me == y, res_ref[...].astype(F32), 0.0)
        blocks.append(total[:, y * OWN : (y + 1) * OWN] + rest)
    blocks.append(jnp.broadcast_to(gain_ref[...].astype(F32), (ROWS, OWN)))
    message = jnp.concatenate(blocks, axis=1).astype(BF16)
    for y in range(4):
        out_ref[y] = message


def stream(parts, residual, gain, held):
    out = (4, ROWS, HALF + OWN)
    return pl.pallas_call(
        stream_kernel,
        out_shape=shape(out, BF16),
        in_specs=[whole(a.shape) for a in (held, parts, residual, gain)],
        out_specs=whole(out),
        compiler_params=params(8),
        name="stream",
    )(in_vmem(held), parts, residual, gain)


def column_kernel(_, parts_ref, out_ref):
    total = parts_ref[0, :, :HALF].astype(F32)
    for y in range(1, 4):
        total += parts_ref[y, :, :HALF].astype(F32)
    out_ref[:, :HALF] = total.astype(BF16)
    row = lax.broadcasted_iota(jnp.int32, (ROWS, OWN), 0)
    gains = jnp.zeros((ROWS, OWN), F32)
    for y in range(4):
        gains = jnp.where(row == y, parts_ref[y, :, HALF:].astype(F32), gains)
    out_ref[:, HALF:] = gains.astype(BF16)


def add_columns(parts, held):
    out = parts.shape[1:]
    return pl.pallas_call(
        column_kernel,
        out_shape=shape(out, BF16),
        in_specs=[whole(held.shape), whole(parts.shape)],
        out_specs=whole(out),
        compiler_params=params(8),
        name="add_columns",
    )(in_vmem(held), parts)


def gate_kernel(mine_ref, other_ref, gate_w, up_w, out_ref, own_ref):
    tiles = UNITS // TILE
    even = is_even()
    mine, other = mine_ref[...].astype(F32), other_ref[...].astype(F32)
    halves = (jnp.where(even, mine, other), jnp.where(even, other, mine))
    square = jnp.zeros((ROWS, OWN), F32)
    own = jnp.zeros((ROWS, OWN), F32)
    blocks = []
    for y in range(4):
        for c in range(2):
            block = halves[c][:, y * OWN : (y + 1) * OWN]
            gain = halves[c][y : y + 1, HALF:]
            blocks.append((block * gain).astype(BF16))
            square += block * block
        own += jnp.where(own_y() == y, mine[:, y * OWN : (y + 1) * OWN], 0.0)
    own_ref[...] = own
    x = jnp.concatenate(blocks, axis=1)
    total = jnp.sum(square, axis=1, keepdims=True)
    high = total.astype(BF16).astype(F32)
    lane = lax.broadcasted_iota(jnp.int32, (ROWS, EXTRA), 1)
    squares = jnp.where(lane < 64, high, total - high).astype(BF16).astype(F32)
    for d in range(N_KV):
        out_ref[d, :, 2 * PART :] = squares[4 * (d // 2) : 4 * (d // 2) + 4, :].astype(BF16)
    for tile in range(tiles):
        for which in range(2):
            weight = (gate_w, up_w)[which]
            lanes = slice(tile * TILE, (tile + 1) * TILE)
            result = jnp.dot(x, weight[:, lanes], preferred_element_type=F32)
            for part in range(2):
                column = 2 * tile + part
                at = which * PART + column % 13 * 128
                for r in range(8):
                    piece = result[4 * r : 4 * r + 4, part * 128 : (part + 1) * 128]
                    out_ref[2 * r + column // 13, :, at : at + 128] = piece.astype(BF16)


def gate_up(mine, other, w_gate, w_up):
    wide = (N_KV, 4, 2 * PART + EXTRA)
    return pl.pallas_call(
        gate_kernel,
        out_shape=[shape(wide, BF16), shape((ROWS, OWN), F32)],
        in_specs=[whole(a.shape) for a in (mine, other, w_gate, w_up)],
        out_specs=[whole(wide), whole((ROWS, OWN))],
        compiler_params=params(8),
        cost_estimate=cost(4 * ROWS * w_gate.size, 4 * w_gate.size),
        name="gate_up",
    )(mine, other, in_vmem(w_gate), in_vmem(w_up))


def hidden_kernel(parts_ref, out_ref):
    total = parts_ref[0].astype(F32)
    for i in range(1, N_KV):
        total += parts_ref[i].astype(F32)
    squares = total[:, 2 * PART : 2 * PART + 1] + total[:, 2 * PART + 64 : 2 * PART + 65]
    scale = lax.rsqrt(squares / (HQ * HD) + 1e-05)
    gate, up = total[:, :PART] * scale, total[:, PART : 2 * PART] * scale
    hidden = (gate / (1.0 + jnp.exp(-gate)) * up).astype(BF16)
    for i in range(N_KV):
        out_ref[i] = hidden


def hidden_units(parts):
    return pl.pallas_call(
        hidden_kernel,
        out_shape=shape((N_KV, 4, PART), BF16),
        in_specs=[whole(parts.shape)],
        out_specs=whole((N_KV, 4, PART)),
        compiler_params=params(8),
        name="hidden_units",
    )(parts)


def down_kernel(parts_ref, w_ref, out_ref, x):
    for d in range(N_KV):
        x[4 * (d // 2) : 4 * (d // 2) + 4, d % 2 * PART : d % 2 * PART + PART] = parts_ref[d].astype(F32)
    total = jnp.dot(x[...].astype(BF16), w_ref[...], preferred_element_type=F32)
    for i in range(KVH):
        out_ref[i] = total[:, i * OWN : (i + 1) * OWN].astype(BF16)


def down(parts, w_down):
    out = (KVH, ROWS, OWN)
    return pl.pallas_call(
        down_kernel,
        out_shape=shape(out, BF16),
        in_specs=[whole(parts.shape), whole(w_down.shape)],
        out_specs=whole(out),
        scratch_shapes=[pltpu.VMEM((ROWS, UNITS), F32)],
        compiler_params=params(8),
        cost_estimate=cost(2 * ROWS * w_down.size, 2 * w_down.size),
        name="down",
    )(parts, in_vmem(w_down))


def finish_kernel(own_ref, parts_ref, out_ref):
    total = own_ref[...]
    for i in range(KVH):
        total += parts_ref[i].astype(F32)
    out_ref[...] = total.astype(BF16)


def finish(own, parts):
    return pl.pallas_call(
        finish_kernel,
        out_shape=shape(own.shape, BF16),
        in_specs=[whole(own.shape), whole(parts.shape)],
        out_specs=whole(own.shape),
        compiler_params=params(8),
        name="finish",
    )(own, parts)


def exchange(value, axis, groups=None):
    return lax.all_to_all(value, axis, 0, 0, axis_index_groups=groups, tiled=True)


def swap(value, step):
    return lax.ppermute(value, "head", [(j, j ^ step) for j in range(KVH)])


def on_device(
    queries,
    key_cache,
    value_cache,
    block_table,
    lengths,
    new_keys,
    new_values,
    residual,
    out_weight,
    norm_gain,
    w_gate,
    w_up,
    w_down,
):
    partials, weight = attention_partials(
        block_table, lengths, queries, key_cache, value_cache, new_keys, new_values, out_weight[0, 0]
    )
    keep, give = project(exchange(partials, "kv"), weight)
    parts = exchange(add_pair(keep, swap(give, 1)), "kv")
    same_core = [[2 * y + c for y in range(4)] for c in range(2)]
    parts = exchange(stream(parts, residual, norm_gain[None], w_up), "head", same_core)
    here = add_columns(parts, w_gate)
    gates, own = gate_up(here, swap(here, 1), w_gate, w_up)
    hidden = exchange(hidden_units(exchange(gates, "kv")), "kv")
    parts = exchange(down(hidden, w_down), "head")
    return finish(own, parts)


def solution(mesh):
    in_specs = (
        P(None, "head"),
        P("kv", "head", None, None),
        P("kv", "head", None, None),
        P(None, "kv"),
        P(),
        P(None, "head"),
        P(None, "head"),
        P(None, ("kv", "head")),
        P("head", "kv", None, None),
        P(("kv", "head")),
        P("kv", "head"),
        P("kv", "head"),
        P("head", "kv"),
    )
    out_specs = P(None, ("kv", "head"))
    return jax.shard_map(
        on_device, mesh=mesh, in_specs=in_specs, out_specs=out_specs, check_vma=False
    )
```

```python
import math

import jax
import jax.numpy as jnp
from jax import lax
from jax.experimental import pallas as pl
from jax.experimental.pallas import tpu as pltpu
from jax.sharding import PartitionSpec as P

HQ = 128
KVH = 8
SEQS = 16
ROWS = 2 * SEQS
GROUP = HQ // KVH
HD = 128
SLOTS = 24
OWN = 128
HALF = 4 * OWN
N_KV = 16
UNITS = 3328
PART = UNITS // 2
EXTRA = 128
TILE = 256

F32 = jnp.float32
BF16 = jnp.bfloat16
MIB = 1 << 20
W_SPACE = pltpu.HBM
ATTENTION_ROOM = 57


def whole(shape, space=pltpu.VMEM):
    zeros = (0,) * len(shape)
    return pl.BlockSpec(shape, lambda *_: zeros, memory_space=space)


def is_even():
    return lax.axis_index("head") % 2 == 0


def own_y():
    return lax.axis_index("head") // 2


def params(mib, steps=0):
    kinds = ("arbitrary",) * steps if steps else None
    return pltpu.CompilerParams(vmem_limit_bytes=mib * MIB, dimension_semantics=kinds)


def in_hbm(array):
    return pltpu.with_memory_space_constraint(array, pltpu.HBM)


def in_vmem(array):
    return pltpu.with_memory_space_constraint(array, pltpu.VMEM)


def cost(flops, moved):
    return pl.CostEstimate(flops=flops, bytes_accessed=moved, transcendentals=0)


def shape(dims, kind):
    return jax.ShapeDtypeStruct(dims, kind)


def parts_of_copy(src, dst, sems):
    count = sems.shape[0]
    deep = dst.shape[0] // count
    return [
        pltpu.make_async_copy(
            src.at[i * deep : (i + 1) * deep, :], dst.at[i * deep : (i + 1) * deep, :], sems.at[i]
        )
        for i in range(count)
    ]


def attention_kernel(
    table_hbm, lengths_hbm, q_hbm, k_hbm, v_hbm, new_k_hbm, new_v_hbm, w_hbm,
    out_ref, w_ref, table, lengths, q_ref, k_ref, v_ref, new_k, new_v, sems, w_sems,
    q_rows, scores, tops, sums, numer,
):
    pairs = (
        (table_hbm, table), (lengths_hbm, lengths), (q_hbm, q_ref), (k_hbm, k_ref), (v_hbm, v_ref),
        (new_k_hbm, new_k), (new_v_hbm, new_v),
    )
    copies = [pltpu.make_async_copy(src, dst, sems.at[i]) for i, (src, dst) in enumerate(pairs)]
    for i in (2, 0, 1, 5, 6, 3, 4):
        copies[i].start()
    w_copies = parts_of_copy(w_hbm, w_ref, w_sems)
    for copy in w_copies:
        copy.start()
    tops[...] = jnp.full(tops.shape, -1e30, F32)
    sums[...] = jnp.zeros(sums.shape, F32)
    numer[...] = jnp.zeros(numer.shape, F32)
    lane = lax.broadcasted_iota(jnp.int32, (ROWS, HD), 1)
    unit = 1.0 / math.sqrt(HD)
    copies[2].wait()
    for g in range(GROUP):
        q_rows[pl.ds(g, ROWS, stride=GROUP), :] = q_ref[:, g * HD : (g + 1) * HD].astype(F32)
    copies[5].wait()
    copies[6].wait()
    mine = pl.ds(lax.axis_index("kv"), ROWS, stride=GROUP)
    query = q_rows[mine, :]
    keys, values = new_k[...].astype(F32), new_v[...].astype(F32)
    odd = lax.broadcasted_iota(jnp.int32, (ROWS, 1), 0) % 2 == 1
    at_own = jnp.sum(query * keys, axis=1, keepdims=True) * unit
    at_prev = jnp.sum(query * pltpu.roll(keys, 1, 0), axis=1, keepdims=True) * unit
    new_max = jnp.where(odd, jnp.maximum(at_own, at_prev), at_own)
    expo_own = jnp.exp(at_own - new_max)
    expo_prev = jnp.where(odd, jnp.exp(at_prev - new_max), 0.0)
    new_out = expo_own.astype(BF16).astype(F32) * values
    new_out += expo_prev.astype(BF16).astype(F32) * pltpu.roll(values, 1, 0)
    tops[mine, :] = jnp.broadcast_to(new_max, (ROWS, HD))
    copies[0].wait()
    copies[1].wait()
    copies[3].wait()
    rows_of = []
    for b in range(SLOTS):
        seq = table[0, b]
        limit = lengths[seq] - table[1, b] * HD
        here = pl.ds(pl.multiple_of(seq * ROWS, ROWS), ROWS)
        rows_of.append(here)
        raw = lax.dot_general(
            q_rows[here, :].astype(BF16), k_ref[b, 0], (((1,), (1,)), ((), ())),
            preferred_element_type=F32,
        )
        masked = jnp.where(lane < limit, raw * unit, -1e30)
        scores[b] = masked
        tops[here, :] = jnp.maximum(tops[here, :], jnp.max(masked, axis=1, keepdims=True))
    tops[...] = tops[...].astype(BF16).astype(F32)
    new_scale = jnp.exp(new_max - tops[mine, :])
    sums[mine, :] = new_scale * (expo_own + expo_prev)
    numer[mine, :] = new_scale * new_out
    copies[4].wait()
    for b in range(SLOTS):
        here = rows_of[b]
        masked = scores[b]
        expo = jnp.where(masked > -1e29, jnp.exp(masked - tops[here, :]), 0.0)
        sums[here, :] += jnp.sum(expo, axis=1, keepdims=True)
        numer[here, :] += jnp.dot(expo.astype(BF16), v_ref[b, 0], preferred_element_type=F32)
    by_head = lax.broadcasted_iota(jnp.int32, (GROUP, HD), 1)
    stats = jnp.zeros((GROUP, HD), F32)
    for row in range(ROWS):
        heads = slice(row * GROUP, (row + 1) * GROUP)
        high = sums[heads, :].astype(BF16).astype(F32)
        stats = jnp.where(by_head == row, tops[heads, :], stats)
        stats = jnp.where(by_head == row + ROWS, high, stats)
        stats = jnp.where(by_head == row + 2 * ROWS, sums[heads, :] - high, stats)
    for g in range(GROUP):
        out_ref[g, :ROWS, :] = numer[pl.ds(g, ROWS, stride=GROUP), :].astype(BF16)
        out_ref[g, ROWS:, :] = jnp.broadcast_to(stats[g : g + 1, :], (16, HD)).astype(BF16)
    for copy in w_copies:
        copy.wait()


def attention_partials(
    table, lengths, queries, key_cache, value_cache, new_keys, new_values, weight
):
    tall = pltpu.VMEM((ROWS * GROUP, HD), F32)
    arrays = (queries, key_cache, value_cache, new_keys, new_values)
    return pl.pallas_call(
        attention_kernel,
        out_shape=[pltpu.VMEM((GROUP, ROWS + 16, HD), BF16), pltpu.VMEM(weight.shape, BF16)],
        in_specs=[pl.BlockSpec(memory_space=W_SPACE)] * 8,
        out_specs=[whole((GROUP, ROWS + 16, HD)), whole(weight.shape)],
        scratch_shapes=[pltpu.SMEM(table.shape, jnp.int32), pltpu.SMEM(lengths.shape, jnp.int32)]
        + [pltpu.VMEM(a.shape, BF16) for a in arrays]
        + [pltpu.SemaphoreType.DMA((7,)), pltpu.SemaphoreType.DMA((8,))]
        + [tall, pltpu.VMEM((SLOTS, ROWS, HD), F32), tall, tall, tall],
        compiler_params=params(ATTENTION_ROOM),
        cost_estimate=cost(SLOTS * ROWS * HD * HD * 4, 4 * SLOTS * HD * HD),
        name="attention",
    )(*[in_hbm(a) for a in (table, lengths, *arrays, weight)])


def project_kernel(got_ref, w_ref, keep_ref, give_ref):
    row = lax.broadcasted_iota(jnp.int32, (N_KV, HD), 0)
    stats = jnp.zeros((N_KV, HD), F32)
    for i in range(N_KV):
        stats = jnp.where(row == i, got_ref[i, ROWS:, :].astype(F32), stats)
    stats = jnp.concatenate([stats, jnp.zeros((HD - N_KV, HD), F32)], axis=0).T
    maxes = stats[:ROWS]
    lane = lax.broadcasted_iota(jnp.int32, (ROWS, HD), 1)
    real = lane < N_KV
    peak = jnp.max(jnp.where(real, maxes, -1e30), axis=1, keepdims=True)
    scales = jnp.where(real, jnp.exp(maxes - peak), 0.0)
    denom = jnp.sum(scales * (stats[ROWS : 2 * ROWS] + stats[2 * ROWS : 3 * ROWS]), axis=1, keepdims=True)
    total = jnp.zeros((ROWS, HD), F32)
    for i in range(N_KV):
        total += scales[:, i : i + 1] * got_ref[i, :ROWS, :].astype(F32)
    attn = (total / denom).astype(BF16)
    even = is_even()
    for d in range(N_KV):
        for y in range(4):
            at = d * 2 * HALF + y * TILE
            both = jnp.dot(attn, w_ref[:, at : at + TILE], preferred_element_type=F32)
            here = slice(y * OWN, (y + 1) * OWN)
            keep_ref[d, :, here] = jnp.where(even, both[:, :OWN], both[:, OWN:])
            give_ref[d, :, here] = jnp.where(even, both[:, OWN:], both[:, :OWN]).astype(BF16)


def project(got, weight):
    out = (N_KV, ROWS, HALF)
    return pl.pallas_call(
        project_kernel,
        out_shape=[shape(out, F32), shape(out, BF16)],
        in_specs=[whole(got.shape), whole(weight.shape)],
        out_specs=[whole(out), whole(out)],
        compiler_params=params(8),
        cost_estimate=cost(2 * ROWS * weight.size, 2 * weight.size),
        name="project",
    )(got, weight)


def pair_kernel(keep_ref, got_ref, out_ref):
    out_ref[...] = (keep_ref[...] + got_ref[...].astype(F32)).astype(BF16)


def add_pair(keep, got):
    return pl.pallas_call(
        pair_kernel,
        out_shape=shape(keep.shape, BF16),
        in_specs=[whole(keep.shape), whole(got.shape)],
        out_specs=whole(keep.shape),
        compiler_params=params(8),
        name="add_pair",
    )(keep, got)


def stream_kernel(_, parts_ref, res_ref, gain_ref, out_ref):
    total = parts_ref[0].astype(F32)
    for i in range(1, N_KV):
        total += parts_ref[i].astype(F32)
    me = own_y()
    blocks = []
    for y in range(4):
        rest = jnp.where(me == y, res_ref[...].astype(F32), 0.0)
        blocks.append(total[:, y * OWN : (y + 1) * OWN] + rest)
    row = lax.broadcasted_iota(jnp.int32, (ROWS, OWN), 0)
    blocks.append(jnp.where(row == me, gain_ref[...].astype(F32), 0.0))
    out_ref[...] = jnp.concatenate(blocks, axis=1).astype(BF16)


def stream(parts, residual, gain, held):
    out = (ROWS, HALF + OWN)
    return pl.pallas_call(
        stream_kernel,
        out_shape=shape(out, BF16),
        in_specs=[whole(a.shape) for a in (held, parts, residual, gain)],
        out_specs=whole(out),
        compiler_params=params(8),
        name="stream",
    )(in_vmem(held), parts, residual, gain)


def sum_kernel(_, mine_ref, got_ref, out_ref):
    out_ref[...] = (mine_ref[...].astype(F32) + got_ref[...].astype(F32)).astype(BF16)


def add_swapped(mine, got, held):
    return pl.pallas_call(
        sum_kernel,
        out_shape=shape(mine.shape, BF16),
        in_specs=[whole(a.shape) for a in (held, mine, got)],
        out_specs=whole(mine.shape),
        compiler_params=params(8),
        name="add_swapped",
    )(in_vmem(held), mine, got)


def gate_kernel(mine_ref, other_ref, gate_w, up_w, out_ref, own_ref):
    tiles = UNITS // TILE
    even = is_even()
    mine, other = mine_ref[...].astype(F32), other_ref[...].astype(F32)
    halves = (jnp.where(even, mine, other), jnp.where(even, other, mine))
    square = jnp.zeros((ROWS, OWN), F32)
    own = jnp.zeros((ROWS, OWN), F32)
    blocks = []
    for y in range(4):
        for c in range(2):
            block = halves[c][:, y * OWN : (y + 1) * OWN]
            gain = halves[c][y : y + 1, HALF:]
            blocks.append((block * gain).astype(BF16))
            square += block * block
        own += jnp.where(own_y() == y, mine[:, y * OWN : (y + 1) * OWN], 0.0)
    own_ref[...] = own
    x = jnp.concatenate(blocks, axis=1)
    total = jnp.sum(square, axis=1, keepdims=True)
    high = total.astype(BF16).astype(F32)
    lane = lax.broadcasted_iota(jnp.int32, (ROWS, EXTRA), 1)
    squares = jnp.where(lane < 64, high, total - high).astype(BF16).astype(F32)
    for d in range(N_KV):
        out_ref[d, :, 2 * PART :] = squares[4 * (d // 2) : 4 * (d // 2) + 4, :].astype(BF16)
    for tile in range(tiles):
        for which in range(2):
            weight = (gate_w, up_w)[which]
            lanes = slice(tile * TILE, (tile + 1) * TILE)
            result = jnp.dot(x, weight[:, lanes], preferred_element_type=F32)
            for part in range(2):
                column = 2 * tile + part
                at = which * PART + column % 13 * 128
                for r in range(8):
                    piece = result[4 * r : 4 * r + 4, part * 128 : (part + 1) * 128]
                    out_ref[2 * r + column // 13, :, at : at + 128] = piece.astype(BF16)


def gate_up(mine, other, w_gate, w_up):
    wide = (N_KV, 4, 2 * PART + EXTRA)
    return pl.pallas_call(
        gate_kernel,
        out_shape=[shape(wide, BF16), shape((ROWS, OWN), F32)],
        in_specs=[whole(a.shape) for a in (mine, other, w_gate, w_up)],
        out_specs=[whole(wide), whole((ROWS, OWN))],
        compiler_params=params(8),
        cost_estimate=cost(4 * ROWS * w_gate.size, 4 * w_gate.size),
        name="gate_up",
    )(mine, other, in_vmem(w_gate), in_vmem(w_up))


def hidden_kernel(parts_ref, out_ref):
    total = parts_ref[0].astype(F32)
    for i in range(1, N_KV):
        total += parts_ref[i].astype(F32)
    squares = total[:, 2 * PART : 2 * PART + 1] + total[:, 2 * PART + 64 : 2 * PART + 65]
    scale = lax.rsqrt(squares / (HQ * HD) + 1e-05)
    gate, up = total[:, :PART] * scale, total[:, PART : 2 * PART] * scale
    hidden = (gate / (1.0 + jnp.exp(-gate)) * up).astype(BF16)
    for i in range(N_KV):
        out_ref[i] = hidden


def hidden_units(parts):
    return pl.pallas_call(
        hidden_kernel,
        out_shape=shape((N_KV, 4, PART), BF16),
        in_specs=[whole(parts.shape)],
        out_specs=whole((N_KV, 4, PART)),
        compiler_params=params(8),
        name="hidden_units",
    )(parts)


def down_kernel(parts_ref, w_ref, out_ref, x):
    for d in range(N_KV):
        x[4 * (d // 2) : 4 * (d // 2) + 4, d % 2 * PART : d % 2 * PART + PART] = parts_ref[d].astype(F32)
    total = jnp.dot(x[...].astype(BF16), w_ref[...], preferred_element_type=F32)
    for i in range(KVH):
        out_ref[i] = total[:, i * OWN : (i + 1) * OWN].astype(BF16)


def down(parts, w_down):
    out = (KVH, ROWS, OWN)
    return pl.pallas_call(
        down_kernel,
        out_shape=shape(out, BF16),
        in_specs=[whole(parts.shape), whole(w_down.shape)],
        out_specs=whole(out),
        scratch_shapes=[pltpu.VMEM((ROWS, UNITS), F32)],
        compiler_params=params(8),
        cost_estimate=cost(2 * ROWS * w_down.size, 2 * w_down.size),
        name="down",
    )(parts, in_vmem(w_down))


def finish_kernel(own_ref, parts_ref, out_ref):
    total = own_ref[...]
    for i in range(KVH):
        total += parts_ref[i].astype(F32)
    out_ref[...] = total.astype(BF16)


def finish(own, parts):
    return pl.pallas_call(
        finish_kernel,
        out_shape=shape(own.shape, BF16),
        in_specs=[whole(own.shape), whole(parts.shape)],
        out_specs=whole(own.shape),
        compiler_params=params(8),
        name="finish",
    )(own, parts)


def exchange(value, axis):
    return lax.all_to_all(value, axis, 0, 0, tiled=True)


def swap(value, step):
    return lax.ppermute(value, "head", [(j, j ^ step) for j in range(KVH)])


def on_device(
    queries,
    key_cache,
    value_cache,
    block_table,
    lengths,
    new_keys,
    new_values,
    residual,
    out_weight,
    norm_gain,
    w_gate,
    w_up,
    w_down,
):
    partials, weight = attention_partials(
        block_table, lengths, queries, key_cache, value_cache, new_keys, new_values, out_weight[0, 0]
    )
    keep, give = project(exchange(partials, "kv"), weight)
    parts = exchange(add_pair(keep, swap(give, 1)), "kv")
    here = stream(parts, residual, norm_gain[None], w_up)
    here = add_swapped(here, swap(here, 2), w_gate)
    here = add_swapped(here, swap(here, 6), w_gate)
    gates, own = gate_up(here, swap(here, 1), w_gate, w_up)
    hidden = exchange(hidden_units(exchange(gates, "kv")), "kv")
    parts = exchange(down(hidden, w_down), "head")
    return finish(own, parts)


def solution(mesh):
    in_specs = (
        P(None, "head"),
        P("kv", "head", None, None),
        P("kv", "head", None, None),
        P(None, "kv"),
        P(),
        P(None, "head"),
        P(None, "head"),
        P(None, ("kv", "head")),
        P("head", "kv", None, None),
        P(("kv", "head")),
        P("kv", "head"),
        P("kv", "head"),
        P("head", "kv"),
    )
    out_specs = P(None, ("kv", "head"))
    return jax.shard_map(
        on_device, mesh=mesh, in_specs=in_specs, out_specs=out_specs, check_vma=False
    )
```

```python
import math

import jax
import jax.numpy as jnp
from jax import lax
from jax.experimental import pallas as pl
from jax.experimental.pallas import tpu as pltpu
from jax.sharding import PartitionSpec as P

HQ = 128
KVH = 8
SEQS = 16
ROWS = 2 * SEQS
GROUP = HQ // KVH
HD = 128
SLOTS = 24
OWN = 128
HALF = 4 * OWN
N_KV = 16
UNITS = 3328
PART = UNITS // 2
EXTRA = 128
TILE = 256

F32 = jnp.float32
BF16 = jnp.bfloat16
MIB = 1 << 20
W_SPACE = pltpu.HBM
ATTENTION_ROOM = 58


def whole(shape, space=pltpu.VMEM):
    zeros = (0,) * len(shape)
    return pl.BlockSpec(shape, lambda *_: zeros, memory_space=space)


def is_even():
    return lax.axis_index("head") % 2 == 0


def own_y():
    return lax.axis_index("head") // 2


def params(mib, steps=0):
    kinds = ("arbitrary",) * steps if steps else None
    return pltpu.CompilerParams(vmem_limit_bytes=mib * MIB, dimension_semantics=kinds)


def in_hbm(array):
    return pltpu.with_memory_space_constraint(array, pltpu.HBM)


def in_vmem(array):
    return pltpu.with_memory_space_constraint(array, pltpu.VMEM)


def cost(flops, moved):
    return pl.CostEstimate(flops=flops, bytes_accessed=moved, transcendentals=0)


def shape(dims, kind):
    return jax.ShapeDtypeStruct(dims, kind)


def parts_of_copy(src, dst, sems):
    count = sems.shape[0]
    deep = dst.shape[0] // count
    return [
        pltpu.make_async_copy(
            src.at[i * deep : (i + 1) * deep, :], dst.at[i * deep : (i + 1) * deep, :], sems.at[i]
        )
        for i in range(count)
    ]


def attention_kernel(
    table_hbm, lengths_hbm, q_hbm, k_hbm, v_hbm, new_k_hbm, new_v_hbm, w_hbm,
    out_ref, w_ref, table, lengths, q_ref, k_ref, v_ref, new_k, new_v, sems, w_sems,
    q_rows, scores, outs, tops, sums, numer,
):
    pairs = (
        (table_hbm, table), (lengths_hbm, lengths), (q_hbm, q_ref), (k_hbm, k_ref), (v_hbm, v_ref),
        (new_k_hbm, new_k), (new_v_hbm, new_v),
    )
    copies = [pltpu.make_async_copy(src, dst, sems.at[i]) for i, (src, dst) in enumerate(pairs)]
    for i in (2, 0, 1, 5, 6, 3, 4):
        copies[i].start()
    tops[...] = jnp.full(tops.shape, -1e30, F32)
    sums[...] = jnp.zeros(sums.shape, F32)
    numer[...] = jnp.zeros(numer.shape, F32)
    lane = lax.broadcasted_iota(jnp.int32, (ROWS, HD), 1)
    unit = 1.0 / math.sqrt(HD)
    copies[2].wait()
    for g in range(GROUP):
        q_rows[pl.ds(g, ROWS, stride=GROUP), :] = q_ref[:, g * HD : (g + 1) * HD].astype(F32)
    copies[5].wait()
    copies[6].wait()
    mine = pl.ds(lax.axis_index("kv"), ROWS, stride=GROUP)
    query = q_rows[mine, :]
    keys, values = new_k[...].astype(F32), new_v[...].astype(F32)
    odd = lax.broadcasted_iota(jnp.int32, (ROWS, 1), 0) % 2 == 1
    at_own = jnp.sum(query * keys, axis=1, keepdims=True) * unit
    at_prev = jnp.sum(query * pltpu.roll(keys, 1, 0), axis=1, keepdims=True) * unit
    new_max = jnp.where(odd, jnp.maximum(at_own, at_prev), at_own)
    expo_own = jnp.exp(at_own - new_max)
    expo_prev = jnp.where(odd, jnp.exp(at_prev - new_max), 0.0)
    new_out = expo_own.astype(BF16).astype(F32) * values
    new_out += expo_prev.astype(BF16).astype(F32) * pltpu.roll(values, 1, 0)
    tops[mine, :] = jnp.broadcast_to(new_max, (ROWS, HD))
    copies[0].wait()
    copies[1].wait()
    copies[3].wait()
    w_copies = parts_of_copy(w_hbm, w_ref, w_sems)
    for copy in w_copies:
        copy.start()
    rows_of = []
    for b in range(SLOTS):
        seq = table[0, b]
        limit = lengths[seq] - table[1, b] * HD
        here = pl.ds(pl.multiple_of(seq * ROWS, ROWS), ROWS)
        rows_of.append(here)
        raw = lax.dot_general(
            q_rows[here, :].astype(BF16), k_ref[b, 0], (((1,), (1,)), ((), ())),
            preferred_element_type=F32,
        )
        masked = jnp.where(lane < limit, raw * unit, -1e30)
        scores[b] = masked
        outs[b] = jnp.broadcast_to(jnp.max(masked, axis=1, keepdims=True), (ROWS, HD))
    for b in range(SLOTS):
        tops[rows_of[b], :] = jnp.maximum(tops[rows_of[b], :], outs[b])
    tops[...] = tops[...].astype(BF16).astype(F32)
    new_scale = jnp.exp(new_max - tops[mine, :])
    sums[mine, :] = new_scale * (expo_own + expo_prev)
    numer[mine, :] = new_scale * new_out
    copies[4].wait()
    for b in range(SLOTS):
        masked = scores[b]
        expo = jnp.where(masked > -1e29, jnp.exp(masked - tops[rows_of[b], :]), 0.0)
        scores[b] = jnp.broadcast_to(jnp.sum(expo, axis=1, keepdims=True), (ROWS, HD))
        outs[b] = jnp.dot(expo.astype(BF16), v_ref[b, 0], preferred_element_type=F32)
    for b in range(SLOTS):
        sums[rows_of[b], :] += scores[b]
        numer[rows_of[b], :] += outs[b]
    by_head = lax.broadcasted_iota(jnp.int32, (GROUP, HD), 1)
    stats = jnp.zeros((GROUP, HD), F32)
    for row in range(ROWS):
        heads = slice(row * GROUP, (row + 1) * GROUP)
        high = sums[heads, :].astype(BF16).astype(F32)
        stats = jnp.where(by_head == row, tops[heads, :], stats)
        stats = jnp.where(by_head == row + ROWS, high, stats)
        stats = jnp.where(by_head == row + 2 * ROWS, sums[heads, :] - high, stats)
    for g in range(GROUP):
        out_ref[g, :ROWS, :] = numer[pl.ds(g, ROWS, stride=GROUP), :].astype(BF16)
        out_ref[g, ROWS:, :] = jnp.broadcast_to(stats[g : g + 1, :], (16, HD)).astype(BF16)
    for copy in w_copies:
        copy.wait()


def attention_partials(
    table, lengths, queries, key_cache, value_cache, new_keys, new_values, weight
):
    tall = pltpu.VMEM((ROWS * GROUP, HD), F32)
    by_slot = pltpu.VMEM((SLOTS, ROWS, HD), F32)
    arrays = (queries, key_cache, value_cache, new_keys, new_values)
    return pl.pallas_call(
        attention_kernel,
        out_shape=[pltpu.VMEM((GROUP, ROWS + 16, HD), BF16), pltpu.VMEM(weight.shape, BF16)],
        in_specs=[pl.BlockSpec(memory_space=W_SPACE)] * 8,
        out_specs=[whole((GROUP, ROWS + 16, HD)), whole(weight.shape)],
        scratch_shapes=[pltpu.SMEM(table.shape, jnp.int32), pltpu.SMEM(lengths.shape, jnp.int32)]
        + [pltpu.VMEM(a.shape, BF16) for a in arrays]
        + [pltpu.SemaphoreType.DMA((7,)), pltpu.SemaphoreType.DMA((8,))]
        + [tall, by_slot, by_slot, tall, tall, tall],
        compiler_params=params(ATTENTION_ROOM),
        cost_estimate=cost(SLOTS * ROWS * HD * HD * 4, 4 * SLOTS * HD * HD),
        name="attention",
    )(*[in_hbm(a) for a in (table, lengths, *arrays, weight)])


def project_part(first, attn, w_ref, keep_ref, give_ref):
    even = is_even()
    for d in range(N_KV // 2):
        for y in range(4):
            at = (first + d) * 2 * HALF + y * TILE
            both = jnp.dot(attn, w_ref[:, at : at + TILE], preferred_element_type=F32)
            here = slice(y * OWN, (y + 1) * OWN)
            keep_ref[d, :, here] = jnp.where(even, both[:, :OWN], both[:, OWN:])
            give_ref[d, :, here] = jnp.where(even, both[:, OWN:], both[:, :OWN]).astype(BF16)


def early_kernel(got_ref, w_ref, keep_ref, give_ref, attn_ref):
    row = lax.broadcasted_iota(jnp.int32, (N_KV, HD), 0)
    stats = jnp.zeros((N_KV, HD), F32)
    for i in range(N_KV):
        stats = jnp.where(row == i, got_ref[i, ROWS:, :].astype(F32), stats)
    stats = jnp.concatenate([stats, jnp.zeros((HD - N_KV, HD), F32)], axis=0).T
    maxes = stats[:ROWS]
    lane = lax.broadcasted_iota(jnp.int32, (ROWS, HD), 1)
    real = lane < N_KV
    peak = jnp.max(jnp.where(real, maxes, -1e30), axis=1, keepdims=True)
    scales = jnp.where(real, jnp.exp(maxes - peak), 0.0)
    denom = jnp.sum(scales * (stats[ROWS : 2 * ROWS] + stats[2 * ROWS : 3 * ROWS]), axis=1, keepdims=True)
    total = jnp.zeros((ROWS, HD), F32)
    for i in range(N_KV):
        total += scales[:, i : i + 1] * got_ref[i, :ROWS, :].astype(F32)
    attn = (total / denom).astype(BF16)
    attn_ref[...] = attn
    project_part(0, attn, w_ref, keep_ref, give_ref)


def late_kernel(attn_ref, w_ref, keep_ref, give_ref):
    project_part(N_KV // 2, attn_ref[...], w_ref, keep_ref, give_ref)


def project(kernel, given, weight, name):
    out = (N_KV // 2, ROWS, HALF)
    outs = [shape(out, F32), shape(out, BF16)]
    if kernel is early_kernel:
        outs.append(shape((ROWS, HD), BF16))
    return pl.pallas_call(
        kernel,
        out_shape=outs,
        in_specs=[whole(given.shape), whole(weight.shape)],
        out_specs=[whole(o.shape) for o in outs],
        compiler_params=params(8),
        cost_estimate=cost(ROWS * weight.size, weight.size),
        name=name,
    )(given, in_vmem(weight))


def pair_kernel(keep_a, got_a, keep_b, got_b, out_ref):
    half = N_KV // 2
    out_ref[:half] = (keep_a[...] + got_a[...].astype(F32)).astype(BF16)
    out_ref[half:] = (keep_b[...] + got_b[...].astype(F32)).astype(BF16)


def add_pair(*parts):
    out = (N_KV, ROWS, HALF)
    return pl.pallas_call(
        pair_kernel,
        out_shape=shape(out, BF16),
        in_specs=[whole(a.shape) for a in parts],
        out_specs=whole(out),
        compiler_params=params(8),
        name="add_pair",
    )(*parts)


def stream_kernel(parts_ref, res_ref, gain_ref, out_ref):
    total = parts_ref[0].astype(F32)
    for i in range(1, N_KV):
        total += parts_ref[i].astype(F32)
    me = own_y()
    blocks = []
    for y in range(4):
        rest = jnp.where(me == y, res_ref[...].astype(F32), 0.0)
        blocks.append(total[:, y * OWN : (y + 1) * OWN] + rest)
    blocks.append(jnp.broadcast_to(gain_ref[...].astype(F32), (ROWS, OWN)))
    message = jnp.concatenate(blocks, axis=1).astype(BF16)
    for y in range(4):
        out_ref[y] = message


def stream(parts, residual, gain):
    out = (4, ROWS, HALF + OWN)
    return pl.pallas_call(
        stream_kernel,
        out_shape=shape(out, BF16),
        in_specs=[whole(a.shape) for a in (parts, residual, gain)],
        out_specs=whole(out),
        compiler_params=params(8),
        name="stream",
    )(parts, residual, gain)


def column_kernel(_, parts_ref, out_ref):
    total = parts_ref[0, :, :HALF].astype(F32)
    for y in range(1, 4):
        total += parts_ref[y, :, :HALF].astype(F32)
    out_ref[:, :HALF] = total.astype(BF16)
    row = lax.broadcasted_iota(jnp.int32, (ROWS, OWN), 0)
    gains = jnp.zeros((ROWS, OWN), F32)
    for y in range(4):
        gains = jnp.where(row == y, parts_ref[y, :, HALF:].astype(F32), gains)
    out_ref[:, HALF:] = gains.astype(BF16)


def add_columns(parts, held):
    out = parts.shape[1:]
    return pl.pallas_call(
        column_kernel,
        out_shape=shape(out, BF16),
        in_specs=[whole(held.shape), whole(parts.shape)],
        out_specs=whole(out),
        compiler_params=params(8),
        name="add_columns",
    )(in_vmem(held), parts)


def gate_kernel(mine_ref, other_ref, gate_w, up_w, out_ref, own_ref):
    tiles = UNITS // TILE
    even = is_even()
    mine, other = mine_ref[...].astype(F32), other_ref[...].astype(F32)
    halves = (jnp.where(even, mine, other), jnp.where(even, other, mine))
    square = jnp.zeros((ROWS, OWN), F32)
    own = jnp.zeros((ROWS, OWN), F32)
    blocks = []
    for y in range(4):
        for c in range(2):
            block = halves[c][:, y * OWN : (y + 1) * OWN]
            gain = halves[c][y : y + 1, HALF:]
            blocks.append((block * gain).astype(BF16))
            square += block * block
        own += jnp.where(own_y() == y, mine[:, y * OWN : (y + 1) * OWN], 0.0)
    own_ref[...] = own
    x = jnp.concatenate(blocks, axis=1)
    total = jnp.sum(square, axis=1, keepdims=True)
    high = total.astype(BF16).astype(F32)
    lane = lax.broadcasted_iota(jnp.int32, (ROWS, EXTRA), 1)
    squares = jnp.where(lane < 64, high, total - high).astype(BF16).astype(F32)
    for d in range(N_KV):
        out_ref[d, :, 2 * PART :] = squares[4 * (d // 2) : 4 * (d // 2) + 4, :].astype(BF16)
    for tile in range(tiles):
        for which in range(2):
            weight = (gate_w, up_w)[which]
            lanes = slice(tile * TILE, (tile + 1) * TILE)
            result = jnp.dot(x, weight[:, lanes], preferred_element_type=F32)
            for part in range(2):
                column = 2 * tile + part
                at = which * PART + column % 13 * 128
                for r in range(8):
                    piece = result[4 * r : 4 * r + 4, part * 128 : (part + 1) * 128]
                    out_ref[2 * r + column // 13, :, at : at + 128] = piece.astype(BF16)


def gate_up(mine, other, w_gate, w_up):
    wide = (N_KV, 4, 2 * PART + EXTRA)
    return pl.pallas_call(
        gate_kernel,
        out_shape=[shape(wide, BF16), shape((ROWS, OWN), F32)],
        in_specs=[whole(a.shape) for a in (mine, other, w_gate, w_up)],
        out_specs=[whole(wide), whole((ROWS, OWN))],
        compiler_params=params(8),
        cost_estimate=cost(4 * ROWS * w_gate.size, 4 * w_gate.size),
        name="gate_up",
    )(mine, other, in_vmem(w_gate), in_vmem(w_up))


def hidden_kernel(parts_ref, out_ref):
    total = parts_ref[0].astype(F32)
    for i in range(1, N_KV):
        total += parts_ref[i].astype(F32)
    squares = total[:, 2 * PART : 2 * PART + 1] + total[:, 2 * PART + 64 : 2 * PART + 65]
    scale = lax.rsqrt(squares / (HQ * HD) + 1e-05)
    gate, up = total[:, :PART] * scale, total[:, PART : 2 * PART] * scale
    hidden = (gate / (1.0 + jnp.exp(-gate)) * up).astype(BF16)
    for i in range(N_KV):
        out_ref[i] = hidden


def hidden_units(parts):
    return pl.pallas_call(
        hidden_kernel,
        out_shape=shape((N_KV, 4, PART), BF16),
        in_specs=[whole(parts.shape)],
        out_specs=whole((N_KV, 4, PART)),
        compiler_params=params(8),
        name="hidden_units",
    )(parts)


def down_kernel(parts_ref, w_ref, out_ref, x):
    for d in range(N_KV):
        x[4 * (d // 2) : 4 * (d // 2) + 4, d % 2 * PART : d % 2 * PART + PART] = parts_ref[d].astype(F32)
    total = jnp.dot(x[...].astype(BF16), w_ref[...], preferred_element_type=F32)
    for i in range(KVH):
        out_ref[i] = total[:, i * OWN : (i + 1) * OWN].astype(BF16)


def down(parts, w_down):
    out = (KVH, ROWS, OWN)
    return pl.pallas_call(
        down_kernel,
        out_shape=shape(out, BF16),
        in_specs=[whole(parts.shape), whole(w_down.shape)],
        out_specs=whole(out),
        scratch_shapes=[pltpu.VMEM((ROWS, UNITS), F32)],
        compiler_params=params(8),
        cost_estimate=cost(2 * ROWS * w_down.size, 2 * w_down.size),
        name="down",
    )(parts, in_vmem(w_down))


def finish_kernel(own_ref, parts_ref, out_ref):
    total = own_ref[...]
    for i in range(KVH):
        total += parts_ref[i].astype(F32)
    out_ref[...] = total.astype(BF16)


def finish(own, parts):
    return pl.pallas_call(
        finish_kernel,
        out_shape=shape(own.shape, BF16),
        in_specs=[whole(own.shape), whole(parts.shape)],
        out_specs=whole(own.shape),
        compiler_params=params(8),
        name="finish",
    )(own, parts)


def exchange(value, axis, groups=None):
    return lax.all_to_all(value, axis, 0, 0, axis_index_groups=groups, tiled=True)


def swap(value, step):
    return lax.ppermute(value, "head", [(j, j ^ step) for j in range(KVH)])


def on_device(
    queries,
    key_cache,
    value_cache,
    block_table,
    lengths,
    new_keys,
    new_values,
    residual,
    out_weight,
    norm_gain,
    w_gate,
    w_up,
    w_down,
):
    partials, weight = attention_partials(
        block_table, lengths, queries, key_cache, value_cache, new_keys, new_values, out_weight[0, 0]
    )
    keep_a, give_a, attn = project(early_kernel, exchange(partials, "kv"), weight, "project_early")
    keep_b, give_b = project(late_kernel, attn, weight, "project_late")
    parts = exchange(add_pair(keep_a, swap(give_a, 1), keep_b, swap(give_b, 1)), "kv")
    same_core = [[2 * y + c for y in range(4)] for c in range(2)]
    parts = exchange(stream(parts, residual, norm_gain[None]), "head", same_core)
    here = add_columns(parts, w_up)
    gates, own = gate_up(here, swap(here, 1), w_gate, w_up)
    hidden = exchange(hidden_units(exchange(gates, "kv")), "kv")
    parts = exchange(down(hidden, w_down), "head")
    return finish(own, parts)


def solution(mesh):
    in_specs = (
        P(None, "head"),
        P("kv", "head", None, None),
        P("kv", "head", None, None),
        P(None, "kv"),
        P(),
        P(None, "head"),
        P(None, "head"),
        P(None, ("kv", "head")),
        P("head", "kv", None, None),
        P(("kv", "head")),
        P("kv", "head"),
        P("kv", "head"),
        P("head", "kv"),
    )
    out_specs = P(None, ("kv", "head"))
    return jax.shard_map(
        on_device, mesh=mesh, in_specs=in_specs, out_specs=out_specs, check_vma=False
    )
```

```python
import math

import jax
import jax.numpy as jnp
from jax import lax
from jax.experimental import pallas as pl
from jax.experimental.pallas import tpu as pltpu
from jax.sharding import PartitionSpec as P

HQ = 128
KVH = 8
SEQS = 16
ROWS = 2 * SEQS
GROUP = HQ // KVH
HD = 128
SLOTS = 24
OWN = 128
HALF = 4 * OWN
N_KV = 16
UNITS = 3328
PART = UNITS // 2
EXTRA = 128
TILE = 256

F32 = jnp.float32
BF16 = jnp.bfloat16
MIB = 1 << 20
W_SPACE = pltpu.HBM
ATTENTION_ROOM = 57


def whole(shape, space=pltpu.VMEM):
    zeros = (0,) * len(shape)
    return pl.BlockSpec(shape, lambda *_: zeros, memory_space=space)


def is_even():
    return lax.axis_index("head") % 2 == 0


def place_of(kv, even):
    return jnp.where(even, kv, N_KV - 1 - kv)


def own_y():
    return lax.axis_index("head") // 2


def params(mib, steps=0):
    kinds = ("arbitrary",) * steps if steps else None
    return pltpu.CompilerParams(vmem_limit_bytes=mib * MIB, dimension_semantics=kinds)


def in_hbm(array):
    return pltpu.with_memory_space_constraint(array, pltpu.HBM)


def in_vmem(array):
    return pltpu.with_memory_space_constraint(array, pltpu.VMEM)


def cost(flops, moved):
    return pl.CostEstimate(flops=flops, bytes_accessed=moved, transcendentals=0)


def shape(dims, kind):
    return jax.ShapeDtypeStruct(dims, kind)


def parts_of_copy(src, dst, sems):
    count = sems.shape[0]
    deep = dst.shape[0] // count
    return [
        pltpu.make_async_copy(
            src.at[i * deep : (i + 1) * deep, :], dst.at[i * deep : (i + 1) * deep, :], sems.at[i]
        )
        for i in range(count)
    ]


def attention_kernel(
    table_hbm, lengths_hbm, q_hbm, k_hbm, v_hbm, new_k_hbm, new_v_hbm, w_hbm,
    out_ref, w_ref, table, lengths, q_ref, k_ref, v_ref, new_k, new_v, sems, w_sems,
    q_rows, scores, tops, sums, numer,
):
    pairs = (
        (table_hbm, table), (lengths_hbm, lengths), (q_hbm, q_ref), (k_hbm, k_ref), (v_hbm, v_ref),
        (new_k_hbm, new_k), (new_v_hbm, new_v),
    )
    copies = [pltpu.make_async_copy(src, dst, sems.at[i]) for i, (src, dst) in enumerate(pairs)]
    for i in (2, 0, 1, 5, 6, 3, 4):
        copies[i].start()
    w_copies = parts_of_copy(w_hbm, w_ref, w_sems)
    for copy in w_copies:
        copy.start()
    tops[...] = jnp.full(tops.shape, -1e30, F32)
    sums[...] = jnp.zeros(sums.shape, F32)
    numer[...] = jnp.zeros(numer.shape, F32)
    lane = lax.broadcasted_iota(jnp.int32, (ROWS, HD), 1)
    unit = 1.0 / math.sqrt(HD)
    copies[2].wait()
    for g in range(GROUP):
        q_rows[pl.ds(g, ROWS, stride=GROUP), :] = q_ref[:, g * HD : (g + 1) * HD].astype(F32)
    copies[5].wait()
    copies[6].wait()
    mine = pl.ds(lax.axis_index("kv"), ROWS, stride=GROUP)
    query = q_rows[mine, :]
    keys, values = new_k[...].astype(F32), new_v[...].astype(F32)
    odd = lax.broadcasted_iota(jnp.int32, (ROWS, 1), 0) % 2 == 1
    at_own = jnp.sum(query * keys, axis=1, keepdims=True) * unit
    at_prev = jnp.sum(query * pltpu.roll(keys, 1, 0), axis=1, keepdims=True) * unit
    new_max = jnp.where(odd, jnp.maximum(at_own, at_prev), at_own)
    expo_own = jnp.exp(at_own - new_max)
    expo_prev = jnp.where(odd, jnp.exp(at_prev - new_max), 0.0)
    new_out = expo_own.astype(BF16).astype(F32) * values
    new_out += expo_prev.astype(BF16).astype(F32) * pltpu.roll(values, 1, 0)
    tops[mine, :] = jnp.broadcast_to(new_max, (ROWS, HD))
    copies[0].wait()
    copies[1].wait()
    copies[3].wait()
    rows_of = []
    for b in range(SLOTS):
        seq = table[0, b]
        limit = lengths[seq] - table[1, b] * HD
        here = pl.ds(pl.multiple_of(seq * ROWS, ROWS), ROWS)
        rows_of.append(here)
        raw = lax.dot_general(
            q_rows[here, :].astype(BF16), k_ref[b, 0], (((1,), (1,)), ((), ())),
            preferred_element_type=F32,
        )
        masked = jnp.where(lane < limit, raw * unit, -1e30)
        scores[b] = masked
        tops[here, :] = jnp.maximum(tops[here, :], jnp.max(masked, axis=1, keepdims=True))
    tops[...] = tops[...].astype(BF16).astype(F32)
    new_scale = jnp.exp(new_max - tops[mine, :])
    sums[mine, :] = new_scale * (expo_own + expo_prev)
    numer[mine, :] = new_scale * new_out
    copies[4].wait()
    for b in range(SLOTS):
        here = rows_of[b]
        masked = scores[b]
        expo = jnp.where(masked > -1e29, jnp.exp(masked - tops[here, :]), 0.0)
        sums[here, :] += jnp.sum(expo, axis=1, keepdims=True)
        numer[here, :] += jnp.dot(expo.astype(BF16), v_ref[b, 0], preferred_element_type=F32)
    by_head = lax.broadcasted_iota(jnp.int32, (GROUP, HD), 1)
    stats = jnp.zeros((GROUP, HD), F32)
    for row in range(ROWS):
        heads = slice(row * GROUP, (row + 1) * GROUP)
        high = sums[heads, :].astype(BF16).astype(F32)
        stats = jnp.where(by_head == row, tops[heads, :], stats)
        stats = jnp.where(by_head == row + ROWS, high, stats)
        stats = jnp.where(by_head == row + 2 * ROWS, sums[heads, :] - high, stats)
    for g in range(GROUP):
        at = place_of(g, is_even())
        out_ref[at, :ROWS, :] = numer[pl.ds(g, ROWS, stride=GROUP), :].astype(BF16)
        out_ref[at, ROWS:, :] = jnp.broadcast_to(stats[g : g + 1, :], (16, HD)).astype(BF16)
    for copy in w_copies:
        copy.wait()


def attention_partials(
    table, lengths, queries, key_cache, value_cache, new_keys, new_values, weight
):
    tall = pltpu.VMEM((ROWS * GROUP, HD), F32)
    arrays = (queries, key_cache, value_cache, new_keys, new_values)
    return pl.pallas_call(
        attention_kernel,
        out_shape=[pltpu.VMEM((GROUP, ROWS + 16, HD), BF16), pltpu.VMEM(weight.shape, BF16)],
        in_specs=[pl.BlockSpec(memory_space=W_SPACE)] * 8,
        out_specs=[whole((GROUP, ROWS + 16, HD)), whole(weight.shape)],
        scratch_shapes=[pltpu.SMEM(table.shape, jnp.int32), pltpu.SMEM(lengths.shape, jnp.int32)]
        + [pltpu.VMEM(a.shape, BF16) for a in arrays]
        + [pltpu.SemaphoreType.DMA((7,)), pltpu.SemaphoreType.DMA((8,))]
        + [tall, pltpu.VMEM((SLOTS, ROWS, HD), F32), tall, tall, tall],
        compiler_params=params(ATTENTION_ROOM),
        cost_estimate=cost(SLOTS * ROWS * HD * HD * 4, 4 * SLOTS * HD * HD),
        name="attention",
    )(*[in_hbm(a) for a in (table, lengths, *arrays, weight)])


def project_kernel(got_ref, w_ref, keep_ref, give_ref):
    row = lax.broadcasted_iota(jnp.int32, (N_KV, HD), 0)
    stats = jnp.zeros((N_KV, HD), F32)
    for i in range(N_KV):
        stats = jnp.where(row == i, got_ref[i, ROWS:, :].astype(F32), stats)
    stats = jnp.concatenate([stats, jnp.zeros((HD - N_KV, HD), F32)], axis=0).T
    maxes = stats[:ROWS]
    lane = lax.broadcasted_iota(jnp.int32, (ROWS, HD), 1)
    real = lane < N_KV
    peak = jnp.max(jnp.where(real, maxes, -1e30), axis=1, keepdims=True)
    scales = jnp.where(real, jnp.exp(maxes - peak), 0.0)
    denom = jnp.sum(scales * (stats[ROWS : 2 * ROWS] + stats[2 * ROWS : 3 * ROWS]), axis=1, keepdims=True)
    total = jnp.zeros((ROWS, HD), F32)
    for i in range(N_KV):
        total += scales[:, i : i + 1] * got_ref[i, :ROWS, :].astype(F32)
    attn = (total / denom).astype(BF16)
    even = is_even()
    for d in range(N_KV):
        for y in range(4):
            at = d * 2 * HALF + y * TILE
            both = jnp.dot(attn, w_ref[:, at : at + TILE], preferred_element_type=F32)
            here = slice(y * OWN, (y + 1) * OWN)
            keep_ref[place_of(d, even), :, here] = jnp.where(even, both[:, :OWN], both[:, OWN:])
            give_ref[place_of(d, ~even), :, here] = jnp.where(even, both[:, OWN:], both[:, :OWN]).astype(BF16)


def project(got, weight):
    out = (N_KV, ROWS, HALF)
    return pl.pallas_call(
        project_kernel,
        out_shape=[shape(out, F32), shape(out, BF16)],
        in_specs=[whole(got.shape), whole(weight.shape)],
        out_specs=[whole(out), whole(out)],
        compiler_params=params(8),
        cost_estimate=cost(2 * ROWS * weight.size, 2 * weight.size),
        name="project",
    )(got, weight)


def pair_kernel(keep_ref, got_ref, out_ref):
    out_ref[...] = (keep_ref[...] + got_ref[...].astype(F32)).astype(BF16)


def add_pair(keep, got):
    return pl.pallas_call(
        pair_kernel,
        out_shape=shape(keep.shape, BF16),
        in_specs=[whole(keep.shape), whole(got.shape)],
        out_specs=whole(keep.shape),
        compiler_params=params(8),
        name="add_pair",
    )(keep, got)


def stream_kernel(_, parts_ref, res_ref, gain_ref, out_ref):
    total = parts_ref[0].astype(F32)
    for i in range(1, N_KV):
        total += parts_ref[i].astype(F32)
    me = own_y()
    blocks = []
    for y in range(4):
        rest = jnp.where(me == y, res_ref[...].astype(F32), 0.0)
        blocks.append(total[:, y * OWN : (y + 1) * OWN] + rest)
    blocks.append(jnp.broadcast_to(gain_ref[...].astype(F32), (ROWS, OWN)))
    message = jnp.concatenate(blocks, axis=1).astype(BF16)
    for y in range(4):
        out_ref[y] = message


def stream(parts, residual, gain, held):
    out = (4, ROWS, HALF + OWN)
    return pl.pallas_call(
        stream_kernel,
        out_shape=shape(out, BF16),
        in_specs=[whole(a.shape) for a in (held, parts, residual, gain)],
        out_specs=whole(out),
        compiler_params=params(8),
        name="stream",
    )(in_vmem(held), parts, residual, gain)


def column_kernel(_, parts_ref, out_ref):
    total = parts_ref[0, :, :HALF].astype(F32)
    for y in range(1, 4):
        total += parts_ref[y, :, :HALF].astype(F32)
    out_ref[:, :HALF] = total.astype(BF16)
    row = lax.broadcasted_iota(jnp.int32, (ROWS, OWN), 0)
    gains = jnp.zeros((ROWS, OWN), F32)
    for y in range(4):
        gains = jnp.where(row == y, parts_ref[y, :, HALF:].astype(F32), gains)
    out_ref[:, HALF:] = gains.astype(BF16)


def add_columns(parts, held):
    out = parts.shape[1:]
    return pl.pallas_call(
        column_kernel,
        out_shape=shape(out, BF16),
        in_specs=[whole(held.shape), whole(parts.shape)],
        out_specs=whole(out),
        compiler_params=params(8),
        name="add_columns",
    )(in_vmem(held), parts)


def gate_kernel(mine_ref, other_ref, gate_w, up_w, out_ref, own_ref):
    tiles = UNITS // TILE
    even = is_even()
    mine, other = mine_ref[...].astype(F32), other_ref[...].astype(F32)
    halves = (jnp.where(even, mine, other), jnp.where(even, other, mine))
    square = jnp.zeros((ROWS, OWN), F32)
    own = jnp.zeros((ROWS, OWN), F32)
    blocks = []
    for y in range(4):
        for c in range(2):
            block = halves[c][:, y * OWN : (y + 1) * OWN]
            gain = halves[c][y : y + 1, HALF:]
            blocks.append((block * gain).astype(BF16))
            square += block * block
        own += jnp.where(own_y() == y, mine[:, y * OWN : (y + 1) * OWN], 0.0)
    own_ref[...] = own
    x = jnp.concatenate(blocks, axis=1)
    total = jnp.sum(square, axis=1, keepdims=True)
    high = total.astype(BF16).astype(F32)
    lane = lax.broadcasted_iota(jnp.int32, (ROWS, EXTRA), 1)
    squares = jnp.where(lane < 64, high, total - high).astype(BF16).astype(F32)
    for d in range(N_KV):
        out_ref[place_of(d, even), :, 2 * PART :] = squares[4 * (d // 2) : 4 * (d // 2) + 4, :].astype(BF16)
    for tile in range(tiles):
        for which in range(2):
            weight = (gate_w, up_w)[which]
            lanes = slice(tile * TILE, (tile + 1) * TILE)
            result = jnp.dot(x, weight[:, lanes], preferred_element_type=F32)
            for part in range(2):
                column = 2 * tile + part
                at = which * PART + column % 13 * 128
                for r in range(8):
                    piece = result[4 * r : 4 * r + 4, part * 128 : (part + 1) * 128]
                    out_ref[place_of(2 * r + column // 13, even), :, at : at + 128] = piece.astype(BF16)


def gate_up(mine, other, w_gate, w_up):
    wide = (N_KV, 4, 2 * PART + EXTRA)
    return pl.pallas_call(
        gate_kernel,
        out_shape=[shape(wide, BF16), shape((ROWS, OWN), F32)],
        in_specs=[whole(a.shape) for a in (mine, other, w_gate, w_up)],
        out_specs=[whole(wide), whole((ROWS, OWN))],
        compiler_params=params(8),
        cost_estimate=cost(4 * ROWS * w_gate.size, 4 * w_gate.size),
        name="gate_up",
    )(mine, other, in_vmem(w_gate), in_vmem(w_up))


def hidden_kernel(parts_ref, out_ref):
    total = parts_ref[0].astype(F32)
    for i in range(1, N_KV):
        total += parts_ref[i].astype(F32)
    squares = total[:, 2 * PART : 2 * PART + 1] + total[:, 2 * PART + 64 : 2 * PART + 65]
    scale = lax.rsqrt(squares / (HQ * HD) + 1e-05)
    gate, up = total[:, :PART] * scale, total[:, PART : 2 * PART] * scale
    hidden = (gate / (1.0 + jnp.exp(-gate)) * up).astype(BF16)
    for i in range(N_KV):
        out_ref[i] = hidden


def hidden_units(parts):
    return pl.pallas_call(
        hidden_kernel,
        out_shape=shape((N_KV, 4, PART), BF16),
        in_specs=[whole(parts.shape)],
        out_specs=whole((N_KV, 4, PART)),
        compiler_params=params(8),
        name="hidden_units",
    )(parts)


def down_kernel(parts_ref, w_ref, out_ref, x):
    for d in range(N_KV):
        piece = parts_ref[place_of(d, is_even())].astype(F32)
        x[4 * (d // 2) : 4 * (d // 2) + 4, d % 2 * PART : d % 2 * PART + PART] = piece
    total = jnp.dot(x[...].astype(BF16), w_ref[...], preferred_element_type=F32)
    for i in range(KVH):
        out_ref[i] = total[:, i * OWN : (i + 1) * OWN].astype(BF16)


def down(parts, w_down):
    out = (KVH, ROWS, OWN)
    return pl.pallas_call(
        down_kernel,
        out_shape=shape(out, BF16),
        in_specs=[whole(parts.shape), whole(w_down.shape)],
        out_specs=whole(out),
        scratch_shapes=[pltpu.VMEM((ROWS, UNITS), F32)],
        compiler_params=params(8),
        cost_estimate=cost(2 * ROWS * w_down.size, 2 * w_down.size),
        name="down",
    )(parts, in_vmem(w_down))


def finish_kernel(own_ref, parts_ref, out_ref):
    total = own_ref[...]
    for i in range(KVH):
        total += parts_ref[i].astype(F32)
    out_ref[...] = total.astype(BF16)


def finish(own, parts):
    return pl.pallas_call(
        finish_kernel,
        out_shape=shape(own.shape, BF16),
        in_specs=[whole(own.shape), whole(parts.shape)],
        out_specs=whole(own.shape),
        compiler_params=params(8),
        name="finish",
    )(own, parts)


def exchange(value, axis, groups=None):
    return lax.all_to_all(value, axis, 0, 0, axis_index_groups=groups, tiled=True)


def exchange_kv(value):
    groups = [
        [kv * KVH + head for kv in (range(N_KV) if head % 2 == 0 else reversed(range(N_KV)))]
        for head in range(KVH)
    ]
    return exchange(value, ("kv", "head"), groups)


def swap(value, step):
    return lax.ppermute(value, "head", [(j, j ^ step) for j in range(KVH)])


def on_device(
    queries,
    key_cache,
    value_cache,
    block_table,
    lengths,
    new_keys,
    new_values,
    residual,
    out_weight,
    norm_gain,
    w_gate,
    w_up,
    w_down,
):
    partials, weight = attention_partials(
        block_table, lengths, queries, key_cache, value_cache, new_keys, new_values, out_weight[0, 0]
    )
    keep, give = project(exchange_kv(partials), weight)
    parts = exchange_kv(add_pair(keep, swap(give, 1)))
    same_core = [[2 * y + c for y in range(4)] for c in range(2)]
    parts = exchange(stream(parts, residual, norm_gain[None], w_up), "head", same_core)
    here = add_columns(parts, w_gate)
    gates, own = gate_up(here, swap(here, 1), w_gate, w_up)
    hidden = exchange_kv(hidden_units(exchange_kv(gates)))
    parts = exchange(down(hidden, w_down), "head")
    return finish(own, parts)


def solution(mesh):
    in_specs = (
        P(None, "head"),
        P("kv", "head", None, None),
        P("kv", "head", None, None),
        P(None, "kv"),
        P(),
        P(None, "head"),
        P(None, "head"),
        P(None, ("kv", "head")),
        P("head", "kv", None, None),
        P(("kv", "head")),
        P("kv", "head"),
        P("kv", "head"),
        P("head", "kv"),
    )
    out_specs = P(None, ("kv", "head"))
    return jax.shard_map(
        on_device, mesh=mesh, in_specs=in_specs, out_specs=out_specs, check_vma=False
    )
```

```python
import math

import jax
import jax.numpy as jnp
from jax import lax
from jax.experimental import pallas as pl
from jax.experimental.pallas import tpu as pltpu
from jax.sharding import PartitionSpec as P

HQ = 128
KVH = 8
SEQS = 16
ROWS = 2 * SEQS
GROUP = HQ // KVH
HD = 128
SLOTS = 24
OWN = 128
HALF = 4 * OWN
N_KV = 16
UNITS = 3328
PART = UNITS // 2
EXTRA = 128
TILE = 256

F32 = jnp.float32
BF16 = jnp.bfloat16
MIB = 1 << 20
W_SPACE = pltpu.HBM
ATTENTION_ROOM = 57


def whole(shape, space=pltpu.VMEM):
    zeros = (0,) * len(shape)
    return pl.BlockSpec(shape, lambda *_: zeros, memory_space=space)


def is_even():
    return lax.axis_index("head") % 2 == 0


BACK = tuple(reversed(range(N_KV)))
Z_FIRST = tuple(4 * x + z for z in range(4) for x in range(4))
SNAKE = tuple(4 * x + (3 - z if x % 2 else z) for x in range(4) for z in range(4))
MERGE_ORDER, PROJ_ORDER, GATE_ORDER, HIDDEN_ORDER = BACK, Z_FIRST, SNAKE, Z_FIRST


def own_y():
    return lax.axis_index("head") // 2


def params(mib, steps=0):
    kinds = ("arbitrary",) * steps if steps else None
    return pltpu.CompilerParams(vmem_limit_bytes=mib * MIB, dimension_semantics=kinds)


def in_hbm(array):
    return pltpu.with_memory_space_constraint(array, pltpu.HBM)


def in_vmem(array):
    return pltpu.with_memory_space_constraint(array, pltpu.VMEM)


def cost(flops, moved):
    return pl.CostEstimate(flops=flops, bytes_accessed=moved, transcendentals=0)


def shape(dims, kind):
    return jax.ShapeDtypeStruct(dims, kind)


def parts_of_copy(src, dst, sems):
    count = sems.shape[0]
    deep = dst.shape[0] // count
    return [
        pltpu.make_async_copy(
            src.at[i * deep : (i + 1) * deep, :], dst.at[i * deep : (i + 1) * deep, :], sems.at[i]
        )
        for i in range(count)
    ]


def attention_kernel(
    table_hbm, lengths_hbm, q_hbm, k_hbm, v_hbm, new_k_hbm, new_v_hbm, w_hbm,
    out_ref, w_ref, table, lengths, q_ref, k_ref, v_ref, new_k, new_v, sems, w_sems,
    q_rows, scores, tops, sums, numer,
):
    pairs = (
        (table_hbm, table), (lengths_hbm, lengths), (q_hbm, q_ref), (k_hbm, k_ref), (v_hbm, v_ref),
        (new_k_hbm, new_k), (new_v_hbm, new_v),
    )
    copies = [pltpu.make_async_copy(src, dst, sems.at[i]) for i, (src, dst) in enumerate(pairs)]
    for i in (2, 0, 1, 5, 6, 3, 4):
        copies[i].start()
    w_copies = parts_of_copy(w_hbm, w_ref, w_sems)
    for copy in w_copies:
        copy.start()
    tops[...] = jnp.full(tops.shape, -1e30, F32)
    sums[...] = jnp.zeros(sums.shape, F32)
    numer[...] = jnp.zeros(numer.shape, F32)
    lane = lax.broadcasted_iota(jnp.int32, (ROWS, HD), 1)
    unit = 1.0 / math.sqrt(HD)
    copies[2].wait()
    for g in range(GROUP):
        q_rows[pl.ds(g, ROWS, stride=GROUP), :] = q_ref[:, g * HD : (g + 1) * HD].astype(F32)
    copies[5].wait()
    copies[6].wait()
    mine = pl.ds(lax.axis_index("kv"), ROWS, stride=GROUP)
    query = q_rows[mine, :]
    keys, values = new_k[...].astype(F32), new_v[...].astype(F32)
    odd = lax.broadcasted_iota(jnp.int32, (ROWS, 1), 0) % 2 == 1
    at_own = jnp.sum(query * keys, axis=1, keepdims=True) * unit
    at_prev = jnp.sum(query * pltpu.roll(keys, 1, 0), axis=1, keepdims=True) * unit
    new_max = jnp.where(odd, jnp.maximum(at_own, at_prev), at_own)
    expo_own = jnp.exp(at_own - new_max)
    expo_prev = jnp.where(odd, jnp.exp(at_prev - new_max), 0.0)
    new_out = expo_own.astype(BF16).astype(F32) * values
    new_out += expo_prev.astype(BF16).astype(F32) * pltpu.roll(values, 1, 0)
    tops[mine, :] = jnp.broadcast_to(new_max, (ROWS, HD))
    copies[0].wait()
    copies[1].wait()
    copies[3].wait()
    rows_of = []
    for b in range(SLOTS):
        seq = table[0, b]
        limit = lengths[seq] - table[1, b] * HD
        here = pl.ds(pl.multiple_of(seq * ROWS, ROWS), ROWS)
        rows_of.append(here)
        raw = lax.dot_general(
            q_rows[here, :].astype(BF16), k_ref[b, 0], (((1,), (1,)), ((), ())),
            preferred_element_type=F32,
        )
        masked = jnp.where(lane < limit, raw * unit, -1e30)
        scores[b] = masked
        tops[here, :] = jnp.maximum(tops[here, :], jnp.max(masked, axis=1, keepdims=True))
    tops[...] = tops[...].astype(BF16).astype(F32)
    new_scale = jnp.exp(new_max - tops[mine, :])
    sums[mine, :] = new_scale * (expo_own + expo_prev)
    numer[mine, :] = new_scale * new_out
    copies[4].wait()
    for b in range(SLOTS):
        here = rows_of[b]
        masked = scores[b]
        expo = jnp.where(masked > -1e29, jnp.exp(masked - tops[here, :]), 0.0)
        sums[here, :] += jnp.sum(expo, axis=1, keepdims=True)
        numer[here, :] += jnp.dot(expo.astype(BF16), v_ref[b, 0], preferred_element_type=F32)
    by_head = lax.broadcasted_iota(jnp.int32, (GROUP, HD), 1)
    stats = jnp.zeros((GROUP, HD), F32)
    for row in range(ROWS):
        heads = slice(row * GROUP, (row + 1) * GROUP)
        high = sums[heads, :].astype(BF16).astype(F32)
        stats = jnp.where(by_head == row, tops[heads, :], stats)
        stats = jnp.where(by_head == row + ROWS, high, stats)
        stats = jnp.where(by_head == row + 2 * ROWS, sums[heads, :] - high, stats)
    for g in range(GROUP):
        at = MERGE_ORDER.index(g)
        out_ref[at, :ROWS, :] = numer[pl.ds(g, ROWS, stride=GROUP), :].astype(BF16)
        out_ref[at, ROWS:, :] = jnp.broadcast_to(stats[g : g + 1, :], (16, HD)).astype(BF16)
    for copy in w_copies:
        copy.wait()


def attention_partials(
    table, lengths, queries, key_cache, value_cache, new_keys, new_values, weight
):
    tall = pltpu.VMEM((ROWS * GROUP, HD), F32)
    arrays = (queries, key_cache, value_cache, new_keys, new_values)
    return pl.pallas_call(
        attention_kernel,
        out_shape=[pltpu.VMEM((GROUP, ROWS + 16, HD), BF16), pltpu.VMEM(weight.shape, BF16)],
        in_specs=[pl.BlockSpec(memory_space=W_SPACE)] * 8,
        out_specs=[whole((GROUP, ROWS + 16, HD)), whole(weight.shape)],
        scratch_shapes=[pltpu.SMEM(table.shape, jnp.int32), pltpu.SMEM(lengths.shape, jnp.int32)]
        + [pltpu.VMEM(a.shape, BF16) for a in arrays]
        + [pltpu.SemaphoreType.DMA((7,)), pltpu.SemaphoreType.DMA((8,))]
        + [tall, pltpu.VMEM((SLOTS, ROWS, HD), F32), tall, tall, tall],
        compiler_params=params(ATTENTION_ROOM),
        cost_estimate=cost(SLOTS * ROWS * HD * HD * 4, 4 * SLOTS * HD * HD),
        name="attention",
    )(*[in_hbm(a) for a in (table, lengths, *arrays, weight)])


def project_kernel(got_ref, w_ref, keep_ref, give_ref):
    row = lax.broadcasted_iota(jnp.int32, (N_KV, HD), 0)
    stats = jnp.zeros((N_KV, HD), F32)
    for i in range(N_KV):
        stats = jnp.where(row == i, got_ref[i, ROWS:, :].astype(F32), stats)
    stats = jnp.concatenate([stats, jnp.zeros((HD - N_KV, HD), F32)], axis=0).T
    maxes = stats[:ROWS]
    lane = lax.broadcasted_iota(jnp.int32, (ROWS, HD), 1)
    real = lane < N_KV
    peak = jnp.max(jnp.where(real, maxes, -1e30), axis=1, keepdims=True)
    scales = jnp.where(real, jnp.exp(maxes - peak), 0.0)
    denom = jnp.sum(scales * (stats[ROWS : 2 * ROWS] + stats[2 * ROWS : 3 * ROWS]), axis=1, keepdims=True)
    total = jnp.zeros((ROWS, HD), F32)
    for i in range(N_KV):
        total += scales[:, i : i + 1] * got_ref[i, :ROWS, :].astype(F32)
    attn = (total / denom).astype(BF16)
    even = is_even()
    for d in range(N_KV):
        for y in range(4):
            at = d * 2 * HALF + y * TILE
            both = jnp.dot(attn, w_ref[:, at : at + TILE], preferred_element_type=F32)
            here = slice(y * OWN, (y + 1) * OWN)
            place = PROJ_ORDER.index(d)
            keep_ref[place, :, here] = jnp.where(even, both[:, :OWN], both[:, OWN:])
            give_ref[place, :, here] = jnp.where(even, both[:, OWN:], both[:, :OWN]).astype(BF16)


def project(got, weight):
    out = (N_KV, ROWS, HALF)
    return pl.pallas_call(
        project_kernel,
        out_shape=[shape(out, F32), shape(out, BF16)],
        in_specs=[whole(got.shape), whole(weight.shape)],
        out_specs=[whole(out), whole(out)],
        compiler_params=params(8),
        cost_estimate=cost(2 * ROWS * weight.size, 2 * weight.size),
        name="project",
    )(got, weight)


def pair_kernel(keep_ref, got_ref, out_ref):
    out_ref[...] = (keep_ref[...] + got_ref[...].astype(F32)).astype(BF16)


def add_pair(keep, got):
    return pl.pallas_call(
        pair_kernel,
        out_shape=shape(keep.shape, BF16),
        in_specs=[whole(keep.shape), whole(got.shape)],
        out_specs=whole(keep.shape),
        compiler_params=params(8),
        name="add_pair",
    )(keep, got)


def stream_kernel(_, parts_ref, res_ref, gain_ref, out_ref):
    total = parts_ref[0].astype(F32)
    for i in range(1, N_KV):
        total += parts_ref[i].astype(F32)
    me = own_y()
    blocks = []
    for y in range(4):
        rest = jnp.where(me == y, res_ref[...].astype(F32), 0.0)
        blocks.append(total[:, y * OWN : (y + 1) * OWN] + rest)
    blocks.append(jnp.broadcast_to(gain_ref[...].astype(F32), (ROWS, OWN)))
    message = jnp.concatenate(blocks, axis=1).astype(BF16)
    for y in range(4):
        out_ref[y] = message


def stream(parts, residual, gain, held):
    out = (4, ROWS, HALF + OWN)
    return pl.pallas_call(
        stream_kernel,
        out_shape=shape(out, BF16),
        in_specs=[whole(a.shape) for a in (held, parts, residual, gain)],
        out_specs=whole(out),
        compiler_params=params(8),
        name="stream",
    )(in_vmem(held), parts, residual, gain)


def column_kernel(_, parts_ref, out_ref):
    total = parts_ref[0, :, :HALF].astype(F32)
    for y in range(1, 4):
        total += parts_ref[y, :, :HALF].astype(F32)
    out_ref[:, :HALF] = total.astype(BF16)
    row = lax.broadcasted_iota(jnp.int32, (ROWS, OWN), 0)
    gains = jnp.zeros((ROWS, OWN), F32)
    for y in range(4):
        gains = jnp.where(row == y, parts_ref[y, :, HALF:].astype(F32), gains)
    out_ref[:, HALF:] = gains.astype(BF16)


def add_columns(parts, held):
    out = parts.shape[1:]
    return pl.pallas_call(
        column_kernel,
        out_shape=shape(out, BF16),
        in_specs=[whole(held.shape), whole(parts.shape)],
        out_specs=whole(out),
        compiler_params=params(8),
        name="add_columns",
    )(in_vmem(held), parts)


def gate_kernel(mine_ref, other_ref, gate_w, up_w, out_ref, own_ref):
    tiles = UNITS // TILE
    even = is_even()
    mine, other = mine_ref[...].astype(F32), other_ref[...].astype(F32)
    halves = (jnp.where(even, mine, other), jnp.where(even, other, mine))
    square = jnp.zeros((ROWS, OWN), F32)
    own = jnp.zeros((ROWS, OWN), F32)
    blocks = []
    for y in range(4):
        for c in range(2):
            block = halves[c][:, y * OWN : (y + 1) * OWN]
            gain = halves[c][y : y + 1, HALF:]
            blocks.append((block * gain).astype(BF16))
            square += block * block
        own += jnp.where(own_y() == y, mine[:, y * OWN : (y + 1) * OWN], 0.0)
    own_ref[...] = own
    x = jnp.concatenate(blocks, axis=1)
    total = jnp.sum(square, axis=1, keepdims=True)
    high = total.astype(BF16).astype(F32)
    lane = lax.broadcasted_iota(jnp.int32, (ROWS, EXTRA), 1)
    squares = jnp.where(lane < 64, high, total - high).astype(BF16).astype(F32)
    for d in range(N_KV):
        out_ref[GATE_ORDER.index(d), :, 2 * PART :] = squares[4 * (d // 2) : 4 * (d // 2) + 4, :].astype(BF16)
    for tile in range(tiles):
        for which in range(2):
            weight = (gate_w, up_w)[which]
            lanes = slice(tile * TILE, (tile + 1) * TILE)
            result = jnp.dot(x, weight[:, lanes], preferred_element_type=F32)
            for part in range(2):
                column = 2 * tile + part
                at = which * PART + column % 13 * 128
                for r in range(8):
                    piece = result[4 * r : 4 * r + 4, part * 128 : (part + 1) * 128]
                    out_ref[GATE_ORDER.index(2 * r + column // 13), :, at : at + 128] = piece.astype(BF16)


def gate_up(mine, other, w_gate, w_up):
    wide = (N_KV, 4, 2 * PART + EXTRA)
    return pl.pallas_call(
        gate_kernel,
        out_shape=[shape(wide, BF16), shape((ROWS, OWN), F32)],
        in_specs=[whole(a.shape) for a in (mine, other, w_gate, w_up)],
        out_specs=[whole(wide), whole((ROWS, OWN))],
        compiler_params=params(8),
        cost_estimate=cost(4 * ROWS * w_gate.size, 4 * w_gate.size),
        name="gate_up",
    )(mine, other, in_vmem(w_gate), in_vmem(w_up))


def hidden_kernel(parts_ref, out_ref):
    total = parts_ref[0].astype(F32)
    for i in range(1, N_KV):
        total += parts_ref[i].astype(F32)
    squares = total[:, 2 * PART : 2 * PART + 1] + total[:, 2 * PART + 64 : 2 * PART + 65]
    scale = lax.rsqrt(squares / (HQ * HD) + 1e-05)
    gate, up = total[:, :PART] * scale, total[:, PART : 2 * PART] * scale
    hidden = (gate / (1.0 + jnp.exp(-gate)) * up).astype(BF16)
    for i in range(N_KV):
        out_ref[i] = hidden


def hidden_units(parts):
    return pl.pallas_call(
        hidden_kernel,
        out_shape=shape((N_KV, 4, PART), BF16),
        in_specs=[whole(parts.shape)],
        out_specs=whole((N_KV, 4, PART)),
        compiler_params=params(8),
        name="hidden_units",
    )(parts)


def down_kernel(parts_ref, w_ref, out_ref, x):
    for d in range(N_KV):
        piece = parts_ref[HIDDEN_ORDER.index(d)].astype(F32)
        x[4 * (d // 2) : 4 * (d // 2) + 4, d % 2 * PART : d % 2 * PART + PART] = piece
    total = jnp.dot(x[...].astype(BF16), w_ref[...], preferred_element_type=F32)
    for i in range(KVH):
        out_ref[i] = total[:, i * OWN : (i + 1) * OWN].astype(BF16)


def down(parts, w_down):
    out = (KVH, ROWS, OWN)
    return pl.pallas_call(
        down_kernel,
        out_shape=shape(out, BF16),
        in_specs=[whole(parts.shape), whole(w_down.shape)],
        out_specs=whole(out),
        scratch_shapes=[pltpu.VMEM((ROWS, UNITS), F32)],
        compiler_params=params(8),
        cost_estimate=cost(2 * ROWS * w_down.size, 2 * w_down.size),
        name="down",
    )(parts, in_vmem(w_down))


def finish_kernel(own_ref, parts_ref, out_ref):
    total = own_ref[...]
    for i in range(KVH):
        total += parts_ref[i].astype(F32)
    out_ref[...] = total.astype(BF16)


def finish(own, parts):
    return pl.pallas_call(
        finish_kernel,
        out_shape=shape(own.shape, BF16),
        in_specs=[whole(own.shape), whole(parts.shape)],
        out_specs=whole(own.shape),
        compiler_params=params(8),
        name="finish",
    )(own, parts)


def exchange(value, axis, groups=None):
    return lax.all_to_all(value, axis, 0, 0, axis_index_groups=groups, tiled=True)


def exchange_kv(value, order):
    groups = [[kv * KVH + head for kv in order] for head in range(KVH)]
    return exchange(value, ("kv", "head"), groups)


def swap(value, step):
    return lax.ppermute(value, "head", [(j, j ^ step) for j in range(KVH)])


def on_device(
    queries,
    key_cache,
    value_cache,
    block_table,
    lengths,
    new_keys,
    new_values,
    residual,
    out_weight,
    norm_gain,
    w_gate,
    w_up,
    w_down,
):
    partials, weight = attention_partials(
        block_table, lengths, queries, key_cache, value_cache, new_keys, new_values, out_weight[0, 0]
    )
    keep, give = project(exchange_kv(partials, MERGE_ORDER), weight)
    parts = exchange_kv(add_pair(keep, swap(give, 1)), PROJ_ORDER)
    same_core = [[2 * y + c for y in range(4)] for c in range(2)]
    parts = exchange(stream(parts, residual, norm_gain[None], w_up), "head", same_core)
    here = add_columns(parts, w_gate)
    gates, own = gate_up(here, swap(here, 1), w_gate, w_up)
    hidden = exchange_kv(hidden_units(exchange_kv(gates, GATE_ORDER)), HIDDEN_ORDER)
    parts = exchange(down(hidden, w_down), "head")
    return finish(own, parts)


def solution(mesh):
    in_specs = (
        P(None, "head"),
        P("kv", "head", None, None),
        P("kv", "head", None, None),
        P(None, "kv"),
        P(),
        P(None, "head"),
        P(None, "head"),
        P(None, ("kv", "head")),
        P("head", "kv", None, None),
        P(("kv", "head")),
        P("kv", "head"),
        P("kv", "head"),
        P("head", "kv"),
    )
    out_specs = P(None, ("kv", "head"))
    return jax.shard_map(
        on_device, mesh=mesh, in_specs=in_specs, out_specs=out_specs, check_vma=False
    )
```

```python
import math

import jax
import jax.numpy as jnp
from jax import lax
from jax.experimental import pallas as pl
from jax.experimental.pallas import tpu as pltpu
from jax.sharding import PartitionSpec as P

HQ = 128
KVH = 8
SEQS = 16
ROWS = 2 * SEQS
GROUP = HQ // KVH
HD = 128
SLOTS = 24
OWN = 128
HALF = 4 * OWN
N_KV = 16
UNITS = 3328
PART = UNITS // 2
EXTRA = 128
TILE = 256

F32 = jnp.float32
BF16 = jnp.bfloat16
MIB = 1 << 20
W_SPACE = pltpu.HBM
ATTENTION_ROOM = 57


def whole(shape, space=pltpu.VMEM):
    zeros = (0,) * len(shape)
    return pl.BlockSpec(shape, lambda *_: zeros, memory_space=space)


def is_even():
    return lax.axis_index("head") % 2 == 0


BACK = tuple(reversed(range(N_KV)))
Z_FIRST = tuple(4 * x + z for z in range(4) for x in range(4))
SNAKE = tuple(4 * x + (3 - z if x % 2 else z) for x in range(4) for z in range(4))
SNAKE_BACK = tuple(reversed(SNAKE))
MERGE_ORDER, PROJ_ORDER, GATE_ORDER, HIDDEN_ORDER = BACK, SNAKE, SNAKE_BACK, SNAKE
Y_ORDER = (3, 2, 1, 0)
HEAD_ORDER = tuple(reversed(range(KVH)))


def own_y():
    return lax.axis_index("head") // 2


def params(mib, steps=0):
    kinds = ("arbitrary",) * steps if steps else None
    return pltpu.CompilerParams(vmem_limit_bytes=mib * MIB, dimension_semantics=kinds)


def in_hbm(array):
    return pltpu.with_memory_space_constraint(array, pltpu.HBM)


def in_vmem(array):
    return pltpu.with_memory_space_constraint(array, pltpu.VMEM)


def cost(flops, moved):
    return pl.CostEstimate(flops=flops, bytes_accessed=moved, transcendentals=0)


def shape(dims, kind):
    return jax.ShapeDtypeStruct(dims, kind)


def parts_of_copy(src, dst, sems):
    count = sems.shape[0]
    deep = dst.shape[0] // count
    return [
        pltpu.make_async_copy(
            src.at[i * deep : (i + 1) * deep, :], dst.at[i * deep : (i + 1) * deep, :], sems.at[i]
        )
        for i in range(count)
    ]


def attention_kernel(
    table_hbm, lengths_hbm, q_hbm, k_hbm, v_hbm, new_k_hbm, new_v_hbm, w_hbm,
    out_ref, w_ref, table, lengths, q_ref, k_ref, v_ref, new_k, new_v, sems, w_sems,
    q_rows, scores, tops, sums, numer,
):
    pairs = (
        (table_hbm, table), (lengths_hbm, lengths), (q_hbm, q_ref), (k_hbm, k_ref), (v_hbm, v_ref),
        (new_k_hbm, new_k), (new_v_hbm, new_v),
    )
    copies = [pltpu.make_async_copy(src, dst, sems.at[i]) for i, (src, dst) in enumerate(pairs)]
    for i in (2, 0, 1, 5, 6, 3, 4):
        copies[i].start()
    w_copies = parts_of_copy(w_hbm, w_ref, w_sems)
    for copy in w_copies:
        copy.start()
    tops[...] = jnp.full(tops.shape, -1e30, F32)
    sums[...] = jnp.zeros(sums.shape, F32)
    numer[...] = jnp.zeros(numer.shape, F32)
    lane = lax.broadcasted_iota(jnp.int32, (ROWS, HD), 1)
    unit = 1.0 / math.sqrt(HD)
    copies[2].wait()
    for g in range(GROUP):
        q_rows[pl.ds(g, ROWS, stride=GROUP), :] = q_ref[:, g * HD : (g + 1) * HD].astype(F32)
    copies[5].wait()
    copies[6].wait()
    mine = pl.ds(lax.axis_index("kv"), ROWS, stride=GROUP)
    query = q_rows[mine, :]
    keys, values = new_k[...].astype(F32), new_v[...].astype(F32)
    odd = lax.broadcasted_iota(jnp.int32, (ROWS, 1), 0) % 2 == 1
    at_own = jnp.sum(query * keys, axis=1, keepdims=True) * unit
    at_prev = jnp.sum(query * pltpu.roll(keys, 1, 0), axis=1, keepdims=True) * unit
    new_max = jnp.where(odd, jnp.maximum(at_own, at_prev), at_own)
    expo_own = jnp.exp(at_own - new_max)
    expo_prev = jnp.where(odd, jnp.exp(at_prev - new_max), 0.0)
    new_out = expo_own.astype(BF16).astype(F32) * values
    new_out += expo_prev.astype(BF16).astype(F32) * pltpu.roll(values, 1, 0)
    tops[mine, :] = jnp.broadcast_to(new_max, (ROWS, HD))
    copies[0].wait()
    copies[1].wait()
    copies[3].wait()
    rows_of = []
    for b in range(SLOTS):
        seq = table[0, b]
        limit = lengths[seq] - table[1, b] * HD
        here = pl.ds(pl.multiple_of(seq * ROWS, ROWS), ROWS)
        rows_of.append(here)
        raw = lax.dot_general(
            q_rows[here, :].astype(BF16), k_ref[b, 0], (((1,), (1,)), ((), ())),
            preferred_element_type=F32,
        )
        masked = jnp.where(lane < limit, raw * unit, -1e30)
        scores[b] = masked
        tops[here, :] = jnp.maximum(tops[here, :], jnp.max(masked, axis=1, keepdims=True))
    tops[...] = tops[...].astype(BF16).astype(F32)
    new_scale = jnp.exp(new_max - tops[mine, :])
    sums[mine, :] = new_scale * (expo_own + expo_prev)
    numer[mine, :] = new_scale * new_out
    copies[4].wait()
    for b in range(SLOTS):
        here = rows_of[b]
        masked = scores[b]
        expo = jnp.where(masked > -1e29, jnp.exp(masked - tops[here, :]), 0.0)
        sums[here, :] += jnp.sum(expo, axis=1, keepdims=True)
        numer[here, :] += jnp.dot(expo.astype(BF16), v_ref[b, 0], preferred_element_type=F32)
    by_head = lax.broadcasted_iota(jnp.int32, (GROUP, HD), 1)
    stats = jnp.zeros((GROUP, HD), F32)
    for row in range(ROWS):
        heads = slice(row * GROUP, (row + 1) * GROUP)
        high = sums[heads, :].astype(BF16).astype(F32)
        stats = jnp.where(by_head == row, tops[heads, :], stats)
        stats = jnp.where(by_head == row + ROWS, high, stats)
        stats = jnp.where(by_head == row + 2 * ROWS, sums[heads, :] - high, stats)
    for g in range(GROUP):
        at = MERGE_ORDER.index(g)
        out_ref[at, :ROWS, :] = numer[pl.ds(g, ROWS, stride=GROUP), :].astype(BF16)
        out_ref[at, ROWS:, :] = jnp.broadcast_to(stats[g : g + 1, :], (16, HD)).astype(BF16)
    for copy in w_copies:
        copy.wait()


def attention_partials(
    table, lengths, queries, key_cache, value_cache, new_keys, new_values, weight
):
    tall = pltpu.VMEM((ROWS * GROUP, HD), F32)
    arrays = (queries, key_cache, value_cache, new_keys, new_values)
    return pl.pallas_call(
        attention_kernel,
        out_shape=[pltpu.VMEM((GROUP, ROWS + 16, HD), BF16), pltpu.VMEM(weight.shape, BF16)],
        in_specs=[pl.BlockSpec(memory_space=W_SPACE)] * 8,
        out_specs=[whole((GROUP, ROWS + 16, HD)), whole(weight.shape)],
        scratch_shapes=[pltpu.SMEM(table.shape, jnp.int32), pltpu.SMEM(lengths.shape, jnp.int32)]
        + [pltpu.VMEM(a.shape, BF16) for a in arrays]
        + [pltpu.SemaphoreType.DMA((7,)), pltpu.SemaphoreType.DMA((8,))]
        + [tall, pltpu.VMEM((SLOTS, ROWS, HD), F32), tall, tall, tall],
        compiler_params=params(ATTENTION_ROOM),
        cost_estimate=cost(SLOTS * ROWS * HD * HD * 4, 4 * SLOTS * HD * HD),
        name="attention",
    )(*[in_hbm(a) for a in (table, lengths, *arrays, weight)])


def project_kernel(got_ref, w_ref, keep_ref, give_ref):
    row = lax.broadcasted_iota(jnp.int32, (N_KV, HD), 0)
    stats = jnp.zeros((N_KV, HD), F32)
    for i in range(N_KV):
        stats = jnp.where(row == i, got_ref[i, ROWS:, :].astype(F32), stats)
    stats = jnp.concatenate([stats, jnp.zeros((HD - N_KV, HD), F32)], axis=0).T
    maxes = stats[:ROWS]
    lane = lax.broadcasted_iota(jnp.int32, (ROWS, HD), 1)
    real = lane < N_KV
    peak = jnp.max(jnp.where(real, maxes, -1e30), axis=1, keepdims=True)
    scales = jnp.where(real, jnp.exp(maxes - peak), 0.0)
    denom = jnp.sum(scales * (stats[ROWS : 2 * ROWS] + stats[2 * ROWS : 3 * ROWS]), axis=1, keepdims=True)
    total = jnp.zeros((ROWS, HD), F32)
    for i in range(N_KV):
        total += scales[:, i : i + 1] * got_ref[i, :ROWS, :].astype(F32)
    attn = (total / denom).astype(BF16)
    even = is_even()
    for d in range(N_KV):
        for y in range(4):
            at = d * 2 * HALF + y * TILE
            both = jnp.dot(attn, w_ref[:, at : at + TILE], preferred_element_type=F32)
            here = slice(y * OWN, (y + 1) * OWN)
            place = PROJ_ORDER.index(d)
            keep_ref[place, :, here] = jnp.where(even, both[:, :OWN], both[:, OWN:])
            give_ref[place, :, here] = jnp.where(even, both[:, OWN:], both[:, :OWN]).astype(BF16)


def project(got, weight):
    out = (N_KV, ROWS, HALF)
    return pl.pallas_call(
        project_kernel,
        out_shape=[shape(out, F32), shape(out, BF16)],
        in_specs=[whole(got.shape), whole(weight.shape)],
        out_specs=[whole(out), whole(out)],
        compiler_params=params(8),
        cost_estimate=cost(2 * ROWS * weight.size, 2 * weight.size),
        name="project",
    )(got, weight)


def pair_kernel(keep_ref, got_ref, out_ref):
    out_ref[...] = (keep_ref[...] + got_ref[...].astype(F32)).astype(BF16)


def add_pair(keep, got):
    return pl.pallas_call(
        pair_kernel,
        out_shape=shape(keep.shape, BF16),
        in_specs=[whole(keep.shape), whole(got.shape)],
        out_specs=whole(keep.shape),
        compiler_params=params(8),
        name="add_pair",
    )(keep, got)


def stream_kernel(_, parts_ref, res_ref, gain_ref, out_ref):
    total = parts_ref[0].astype(F32)
    for i in range(1, N_KV):
        total += parts_ref[i].astype(F32)
    me = own_y()
    blocks = []
    for y in range(4):
        rest = jnp.where(me == y, res_ref[...].astype(F32), 0.0)
        blocks.append(total[:, y * OWN : (y + 1) * OWN] + rest)
    blocks.append(jnp.broadcast_to(gain_ref[...].astype(F32), (ROWS, OWN)))
    message = jnp.concatenate(blocks, axis=1).astype(BF16)
    for y in range(4):
        out_ref[y] = message


def stream(parts, residual, gain, held):
    out = (4, ROWS, HALF + OWN)
    return pl.pallas_call(
        stream_kernel,
        out_shape=shape(out, BF16),
        in_specs=[whole(a.shape) for a in (held, parts, residual, gain)],
        out_specs=whole(out),
        compiler_params=params(8),
        name="stream",
    )(in_vmem(held), parts, residual, gain)


def column_kernel(_, parts_ref, out_ref):
    total = parts_ref[0, :, :HALF].astype(F32)
    for y in range(1, 4):
        total += parts_ref[y, :, :HALF].astype(F32)
    out_ref[:, :HALF] = total.astype(BF16)
    row = lax.broadcasted_iota(jnp.int32, (ROWS, OWN), 0)
    gains = jnp.zeros((ROWS, OWN), F32)
    for y in range(4):
        gains = jnp.where(row == Y_ORDER[y], parts_ref[y, :, HALF:].astype(F32), gains)
    out_ref[:, HALF:] = gains.astype(BF16)


def add_columns(parts, held):
    out = parts.shape[1:]
    return pl.pallas_call(
        column_kernel,
        out_shape=shape(out, BF16),
        in_specs=[whole(held.shape), whole(parts.shape)],
        out_specs=whole(out),
        compiler_params=params(8),
        name="add_columns",
    )(in_vmem(held), parts)


def gate_kernel(mine_ref, other_ref, gate_w, up_w, out_ref, own_ref):
    tiles = UNITS // TILE
    even = is_even()
    mine, other = mine_ref[...].astype(F32), other_ref[...].astype(F32)
    halves = (jnp.where(even, mine, other), jnp.where(even, other, mine))
    square = jnp.zeros((ROWS, OWN), F32)
    own = jnp.zeros((ROWS, OWN), F32)
    blocks = []
    for y in range(4):
        for c in range(2):
            block = halves[c][:, y * OWN : (y + 1) * OWN]
            gain = halves[c][y : y + 1, HALF:]
            blocks.append((block * gain).astype(BF16))
            square += block * block
        own += jnp.where(own_y() == y, mine[:, y * OWN : (y + 1) * OWN], 0.0)
    own_ref[...] = own
    x = jnp.concatenate(blocks, axis=1)
    total = jnp.sum(square, axis=1, keepdims=True)
    high = total.astype(BF16).astype(F32)
    lane = lax.broadcasted_iota(jnp.int32, (ROWS, EXTRA), 1)
    squares = jnp.where(lane < 64, high, total - high).astype(BF16).astype(F32)
    for d in range(N_KV):
        out_ref[GATE_ORDER.index(d), :, 2 * PART :] = squares[4 * (d // 2) : 4 * (d // 2) + 4, :].astype(BF16)
    for tile in range(tiles):
        for which in range(2):
            weight = (gate_w, up_w)[which]
            lanes = slice(tile * TILE, (tile + 1) * TILE)
            result = jnp.dot(x, weight[:, lanes], preferred_element_type=F32)
            for part in range(2):
                column = 2 * tile + part
                at = which * PART + column % 13 * 128
                for r in range(8):
                    piece = result[4 * r : 4 * r + 4, part * 128 : (part + 1) * 128]
                    out_ref[GATE_ORDER.index(2 * r + column // 13), :, at : at + 128] = piece.astype(BF16)


def gate_up(mine, other, w_gate, w_up):
    wide = (N_KV, 4, 2 * PART + EXTRA)
    return pl.pallas_call(
        gate_kernel,
        out_shape=[shape(wide, BF16), shape((ROWS, OWN), F32)],
        in_specs=[whole(a.shape) for a in (mine, other, w_gate, w_up)],
        out_specs=[whole(wide), whole((ROWS, OWN))],
        compiler_params=params(8),
        cost_estimate=cost(4 * ROWS * w_gate.size, 4 * w_gate.size),
        name="gate_up",
    )(mine, other, in_vmem(w_gate), in_vmem(w_up))


def hidden_kernel(parts_ref, out_ref):
    total = parts_ref[0].astype(F32)
    for i in range(1, N_KV):
        total += parts_ref[i].astype(F32)
    squares = total[:, 2 * PART : 2 * PART + 1] + total[:, 2 * PART + 64 : 2 * PART + 65]
    scale = lax.rsqrt(squares / (HQ * HD) + 1e-05)
    gate, up = total[:, :PART] * scale, total[:, PART : 2 * PART] * scale
    hidden = (gate / (1.0 + jnp.exp(-gate)) * up).astype(BF16)
    for i in range(N_KV):
        out_ref[i] = hidden


def hidden_units(parts):
    return pl.pallas_call(
        hidden_kernel,
        out_shape=shape((N_KV, 4, PART), BF16),
        in_specs=[whole(parts.shape)],
        out_specs=whole((N_KV, 4, PART)),
        compiler_params=params(8),
        name="hidden_units",
    )(parts)


def down_kernel(parts_ref, w_ref, out_ref, x):
    for d in range(N_KV):
        piece = parts_ref[HIDDEN_ORDER.index(d)].astype(F32)
        x[4 * (d // 2) : 4 * (d // 2) + 4, d % 2 * PART : d % 2 * PART + PART] = piece
    total = jnp.dot(x[...].astype(BF16), w_ref[...], preferred_element_type=F32)
    for i in range(KVH):
        out_ref[HEAD_ORDER.index(i)] = total[:, i * OWN : (i + 1) * OWN].astype(BF16)


def down(parts, w_down):
    out = (KVH, ROWS, OWN)
    return pl.pallas_call(
        down_kernel,
        out_shape=shape(out, BF16),
        in_specs=[whole(parts.shape), whole(w_down.shape)],
        out_specs=whole(out),
        scratch_shapes=[pltpu.VMEM((ROWS, UNITS), F32)],
        compiler_params=params(8),
        cost_estimate=cost(2 * ROWS * w_down.size, 2 * w_down.size),
        name="down",
    )(parts, in_vmem(w_down))


def finish_kernel(own_ref, parts_ref, out_ref):
    total = own_ref[...]
    for i in range(KVH):
        total += parts_ref[i].astype(F32)
    out_ref[...] = total.astype(BF16)


def finish(own, parts):
    return pl.pallas_call(
        finish_kernel,
        out_shape=shape(own.shape, BF16),
        in_specs=[whole(own.shape), whole(parts.shape)],
        out_specs=whole(own.shape),
        compiler_params=params(8),
        name="finish",
    )(own, parts)


def exchange(value, axis, groups=None):
    return lax.all_to_all(value, axis, 0, 0, axis_index_groups=groups, tiled=True)


def exchange_kv(value, order):
    groups = [[kv * KVH + head for kv in order] for head in range(KVH)]
    return exchange(value, ("kv", "head"), groups)


def swap(value, step):
    return lax.ppermute(value, "head", [(j, j ^ step) for j in range(KVH)])


def on_device(
    queries,
    key_cache,
    value_cache,
    block_table,
    lengths,
    new_keys,
    new_values,
    residual,
    out_weight,
    norm_gain,
    w_gate,
    w_up,
    w_down,
):
    partials, weight = attention_partials(
        block_table, lengths, queries, key_cache, value_cache, new_keys, new_values, out_weight[0, 0]
    )
    keep, give = project(exchange_kv(partials, MERGE_ORDER), weight)
    parts = exchange_kv(add_pair(keep, swap(give, 1)), PROJ_ORDER)
    same_core = [[2 * y + c for y in Y_ORDER] for c in range(2)]
    parts = exchange(stream(parts, residual, norm_gain[None], w_up), "head", same_core)
    here = add_columns(parts, w_gate)
    gates, own = gate_up(here, swap(here, 1), w_gate, w_up)
    hidden = exchange_kv(hidden_units(exchange_kv(gates, GATE_ORDER)), HIDDEN_ORDER)
    parts = exchange(down(hidden, w_down), "head", [list(HEAD_ORDER)])
    return finish(own, parts)


def solution(mesh):
    in_specs = (
        P(None, "head"),
        P("kv", "head", None, None),
        P("kv", "head", None, None),
        P(None, "kv"),
        P(),
        P(None, "head"),
        P(None, "head"),
        P(None, ("kv", "head")),
        P("head", "kv", None, None),
        P(("kv", "head")),
        P("kv", "head"),
        P("kv", "head"),
        P("head", "kv"),
    )
    out_specs = P(None, ("kv", "head"))
    return jax.shard_map(
        on_device, mesh=mesh, in_specs=in_specs, out_specs=out_specs, check_vma=False
    )
```

```python
import math

import jax
import jax.numpy as jnp
from jax import lax
from jax.experimental import pallas as pl
from jax.experimental.pallas import tpu as pltpu
from jax.sharding import PartitionSpec as P

HQ = 128
KVH = 8
SEQS = 16
ROWS = 2 * SEQS
GROUP = HQ // KVH
HD = 128
SLOTS = 24
OWN = 128
HALF = 4 * OWN
N_KV = 16
UNITS = 3328
PART = UNITS // 2
EXTRA = 128
TILE = 256

F32 = jnp.float32
BF16 = jnp.bfloat16
MIB = 1 << 20
W_SPACE = pltpu.HBM
ATTENTION_ROOM = 57


def whole(shape, space=pltpu.VMEM):
    zeros = (0,) * len(shape)
    return pl.BlockSpec(shape, lambda *_: zeros, memory_space=space)


def is_even():
    return lax.axis_index("head") % 2 == 0


BACK = tuple(reversed(range(N_KV)))
SNAKE = tuple(4 * x + (3 - z if x % 2 else z) for x in range(4) for z in range(4))
MERGE_ORDER, PROJ_ORDER, GATE_ORDER, HIDDEN_ORDER = BACK, BACK, SNAKE, BACK
Y_ORDER = (3, 2, 1, 0)
HEAD_ORDER = (7, 5, 3, 1, 6, 4, 2, 0)


def own_y():
    return lax.axis_index("head") // 2


def params(mib, steps=0):
    kinds = ("arbitrary",) * steps if steps else None
    return pltpu.CompilerParams(vmem_limit_bytes=mib * MIB, dimension_semantics=kinds)


def in_hbm(array):
    return pltpu.with_memory_space_constraint(array, pltpu.HBM)


def in_vmem(array):
    return pltpu.with_memory_space_constraint(array, pltpu.VMEM)


def cost(flops, moved):
    return pl.CostEstimate(flops=flops, bytes_accessed=moved, transcendentals=0)


def shape(dims, kind):
    return jax.ShapeDtypeStruct(dims, kind)


def parts_of_copy(src, dst, sems):
    count = sems.shape[0]
    deep = dst.shape[0] // count
    return [
        pltpu.make_async_copy(
            src.at[i * deep : (i + 1) * deep, :], dst.at[i * deep : (i + 1) * deep, :], sems.at[i]
        )
        for i in range(count)
    ]


def attention_kernel(
    table_hbm, lengths_hbm, q_hbm, k_hbm, v_hbm, new_k_hbm, new_v_hbm, w_hbm,
    out_ref, w_ref, table, lengths, q_ref, k_ref, v_ref, new_k, new_v, sems, w_sems,
    q_rows, scores, tops, sums, numer,
):
    pairs = (
        (table_hbm, table), (lengths_hbm, lengths), (q_hbm, q_ref), (k_hbm, k_ref), (v_hbm, v_ref),
        (new_k_hbm, new_k), (new_v_hbm, new_v),
    )
    copies = [pltpu.make_async_copy(src, dst, sems.at[i]) for i, (src, dst) in enumerate(pairs)]
    for i in (2, 0, 1, 5, 6, 3, 4):
        copies[i].start()
    w_copies = parts_of_copy(w_hbm, w_ref, w_sems)
    for copy in w_copies:
        copy.start()
    tops[...] = jnp.full(tops.shape, -1e30, F32)
    sums[...] = jnp.zeros(sums.shape, F32)
    numer[...] = jnp.zeros(numer.shape, F32)
    lane = lax.broadcasted_iota(jnp.int32, (ROWS, HD), 1)
    unit = 1.0 / math.sqrt(HD)
    copies[2].wait()
    for g in range(GROUP):
        q_rows[pl.ds(g, ROWS, stride=GROUP), :] = q_ref[:, g * HD : (g + 1) * HD].astype(F32)
    copies[5].wait()
    copies[6].wait()
    mine = pl.ds(lax.axis_index("kv"), ROWS, stride=GROUP)
    query = q_rows[mine, :]
    keys, values = new_k[...].astype(F32), new_v[...].astype(F32)
    odd = lax.broadcasted_iota(jnp.int32, (ROWS, 1), 0) % 2 == 1
    at_own = jnp.sum(query * keys, axis=1, keepdims=True) * unit
    at_prev = jnp.sum(query * pltpu.roll(keys, 1, 0), axis=1, keepdims=True) * unit
    new_max = jnp.where(odd, jnp.maximum(at_own, at_prev), at_own)
    expo_own = jnp.exp(at_own - new_max)
    expo_prev = jnp.where(odd, jnp.exp(at_prev - new_max), 0.0)
    new_out = expo_own.astype(BF16).astype(F32) * values
    new_out += expo_prev.astype(BF16).astype(F32) * pltpu.roll(values, 1, 0)
    tops[mine, :] = jnp.broadcast_to(new_max, (ROWS, HD))
    copies[0].wait()
    copies[1].wait()
    copies[3].wait()
    rows_of = []
    for b in range(SLOTS):
        seq = table[0, b]
        limit = lengths[seq] - table[1, b] * HD
        here = pl.ds(pl.multiple_of(seq * ROWS, ROWS), ROWS)
        rows_of.append(here)
        raw = lax.dot_general(
            q_rows[here, :].astype(BF16), k_ref[b, 0], (((1,), (1,)), ((), ())),
            preferred_element_type=F32,
        )
        masked = jnp.where(lane < limit, raw * unit, -1e30)
        scores[b] = masked
        tops[here, :] = jnp.maximum(tops[here, :], jnp.max(masked, axis=1, keepdims=True))
    tops[...] = tops[...].astype(BF16).astype(F32)
    new_scale = jnp.exp(new_max - tops[mine, :])
    sums[mine, :] = new_scale * (expo_own + expo_prev)
    numer[mine, :] = new_scale * new_out
    copies[4].wait()
    for b in range(SLOTS):
        here = rows_of[b]
        masked = scores[b]
        expo = jnp.where(masked > -1e29, jnp.exp(masked - tops[here, :]), 0.0)
        sums[here, :] += jnp.sum(expo, axis=1, keepdims=True)
        numer[here, :] += jnp.dot(expo.astype(BF16), v_ref[b, 0], preferred_element_type=F32)
    by_head = lax.broadcasted_iota(jnp.int32, (GROUP, HD), 1)
    stats = jnp.zeros((GROUP, HD), F32)
    for row in range(ROWS):
        heads = slice(row * GROUP, (row + 1) * GROUP)
        high = sums[heads, :].astype(BF16).astype(F32)
        stats = jnp.where(by_head == row, tops[heads, :], stats)
        stats = jnp.where(by_head == row + ROWS, high, stats)
        stats = jnp.where(by_head == row + 2 * ROWS, sums[heads, :] - high, stats)
    for g in range(GROUP):
        at = MERGE_ORDER.index(g)
        out_ref[at, :ROWS, :] = numer[pl.ds(g, ROWS, stride=GROUP), :].astype(BF16)
        out_ref[at, ROWS:, :] = jnp.broadcast_to(stats[g : g + 1, :], (16, HD)).astype(BF16)
    for copy in w_copies:
        copy.wait()


def attention_partials(
    table, lengths, queries, key_cache, value_cache, new_keys, new_values, weight
):
    tall = pltpu.VMEM((ROWS * GROUP, HD), F32)
    arrays = (queries, key_cache, value_cache, new_keys, new_values)
    return pl.pallas_call(
        attention_kernel,
        out_shape=[pltpu.VMEM((GROUP, ROWS + 16, HD), BF16), pltpu.VMEM(weight.shape, BF16)],
        in_specs=[pl.BlockSpec(memory_space=W_SPACE)] * 8,
        out_specs=[whole((GROUP, ROWS + 16, HD)), whole(weight.shape)],
        scratch_shapes=[pltpu.SMEM(table.shape, jnp.int32), pltpu.SMEM(lengths.shape, jnp.int32)]
        + [pltpu.VMEM(a.shape, BF16) for a in arrays]
        + [pltpu.SemaphoreType.DMA((7,)), pltpu.SemaphoreType.DMA((8,))]
        + [tall, pltpu.VMEM((SLOTS, ROWS, HD), F32), tall, tall, tall],
        compiler_params=params(ATTENTION_ROOM),
        cost_estimate=cost(SLOTS * ROWS * HD * HD * 4, 4 * SLOTS * HD * HD),
        name="attention",
    )(*[in_hbm(a) for a in (table, lengths, *arrays, weight)])


def project_kernel(got_ref, w_ref, keep_ref, give_ref):
    row = lax.broadcasted_iota(jnp.int32, (N_KV, HD), 0)
    stats = jnp.zeros((N_KV, HD), F32)
    for i in range(N_KV):
        stats = jnp.where(row == i, got_ref[i, ROWS:, :].astype(F32), stats)
    stats = jnp.concatenate([stats, jnp.zeros((HD - N_KV, HD), F32)], axis=0).T
    maxes = stats[:ROWS]
    lane = lax.broadcasted_iota(jnp.int32, (ROWS, HD), 1)
    real = lane < N_KV
    peak = jnp.max(jnp.where(real, maxes, -1e30), axis=1, keepdims=True)
    scales = jnp.where(real, jnp.exp(maxes - peak), 0.0)
    denom = jnp.sum(scales * (stats[ROWS : 2 * ROWS] + stats[2 * ROWS : 3 * ROWS]), axis=1, keepdims=True)
    total = jnp.zeros((ROWS, HD), F32)
    for i in range(N_KV):
        total += scales[:, i : i + 1] * got_ref[i, :ROWS, :].astype(F32)
    attn = (total / denom).astype(BF16)
    even = is_even()
    for d in range(N_KV):
        for y in range(4):
            at = d * 2 * HALF + y * TILE
            both = jnp.dot(attn, w_ref[:, at : at + TILE], preferred_element_type=F32)
            here = slice(y * OWN, (y + 1) * OWN)
            place = PROJ_ORDER.index(d)
            keep_ref[place, :, here] = jnp.where(even, both[:, :OWN], both[:, OWN:])
            give_ref[place, :, here] = jnp.where(even, both[:, OWN:], both[:, :OWN]).astype(BF16)


def project(got, weight):
    out = (N_KV, ROWS, HALF)
    return pl.pallas_call(
        project_kernel,
        out_shape=[shape(out, F32), shape(out, BF16)],
        in_specs=[whole(got.shape), whole(weight.shape)],
        out_specs=[whole(out), whole(out)],
        compiler_params=params(8),
        cost_estimate=cost(2 * ROWS * weight.size, 2 * weight.size),
        name="project",
    )(got, weight)


def pair_kernel(keep_ref, got_ref, out_ref):
    out_ref[...] = (keep_ref[...] + got_ref[...].astype(F32)).astype(BF16)


def add_pair(keep, got):
    return pl.pallas_call(
        pair_kernel,
        out_shape=shape(keep.shape, BF16),
        in_specs=[whole(keep.shape), whole(got.shape)],
        out_specs=whole(keep.shape),
        compiler_params=params(8),
        name="add_pair",
    )(keep, got)


def stream_kernel(_, parts_ref, res_ref, gain_ref, out_ref):
    total = parts_ref[0].astype(F32)
    for i in range(1, N_KV):
        total += parts_ref[i].astype(F32)
    me = own_y()
    blocks = []
    for y in range(4):
        rest = jnp.where(me == y, res_ref[...].astype(F32), 0.0)
        blocks.append(total[:, y * OWN : (y + 1) * OWN] + rest)
    blocks.append(jnp.broadcast_to(gain_ref[...].astype(F32), (ROWS, OWN)))
    message = jnp.concatenate(blocks, axis=1).astype(BF16)
    for y in range(4):
        out_ref[y] = message


def stream(parts, residual, gain, held):
    out = (4, ROWS, HALF + OWN)
    return pl.pallas_call(
        stream_kernel,
        out_shape=shape(out, BF16),
        in_specs=[whole(a.shape) for a in (held, parts, residual, gain)],
        out_specs=whole(out),
        compiler_params=params(8),
        name="stream",
    )(in_vmem(held), parts, residual, gain)


def column_kernel(_, parts_ref, out_ref):
    total = parts_ref[0, :, :HALF].astype(F32)
    for y in range(1, 4):
        total += parts_ref[y, :, :HALF].astype(F32)
    out_ref[:, :HALF] = total.astype(BF16)
    row = lax.broadcasted_iota(jnp.int32, (ROWS, OWN), 0)
    gains = jnp.zeros((ROWS, OWN), F32)
    for y in range(4):
        gains = jnp.where(row == Y_ORDER[y], parts_ref[y, :, HALF:].astype(F32), gains)
    out_ref[:, HALF:] = gains.astype(BF16)


def add_columns(parts, held):
    out = parts.shape[1:]
    return pl.pallas_call(
        column_kernel,
        out_shape=shape(out, BF16),
        in_specs=[whole(held.shape), whole(parts.shape)],
        out_specs=whole(out),
        compiler_params=params(8),
        name="add_columns",
    )(in_vmem(held), parts)


def gate_kernel(mine_ref, other_ref, gate_w, up_w, out_ref, own_ref):
    tiles = UNITS // TILE
    even = is_even()
    mine, other = mine_ref[...].astype(F32), other_ref[...].astype(F32)
    halves = (jnp.where(even, mine, other), jnp.where(even, other, mine))
    square = jnp.zeros((ROWS, OWN), F32)
    own = jnp.zeros((ROWS, OWN), F32)
    blocks = []
    for y in range(4):
        for c in range(2):
            block = halves[c][:, y * OWN : (y + 1) * OWN]
            gain = halves[c][y : y + 1, HALF:]
            blocks.append((block * gain).astype(BF16))
            square += block * block
        own += jnp.where(own_y() == y, mine[:, y * OWN : (y + 1) * OWN], 0.0)
    own_ref[...] = own
    x = jnp.concatenate(blocks, axis=1)
    total = jnp.sum(square, axis=1, keepdims=True)
    high = total.astype(BF16).astype(F32)
    lane = lax.broadcasted_iota(jnp.int32, (ROWS, EXTRA), 1)
    squares = jnp.where(lane < 64, high, total - high).astype(BF16).astype(F32)
    for d in range(N_KV):
        out_ref[GATE_ORDER.index(d), :, 2 * PART :] = squares[4 * (d // 2) : 4 * (d // 2) + 4, :].astype(BF16)
    for tile in range(tiles):
        for which in range(2):
            weight = (gate_w, up_w)[which]
            lanes = slice(tile * TILE, (tile + 1) * TILE)
            result = jnp.dot(x, weight[:, lanes], preferred_element_type=F32)
            for part in range(2):
                column = 2 * tile + part
                at = which * PART + column % 13 * 128
                for r in range(8):
                    piece = result[4 * r : 4 * r + 4, part * 128 : (part + 1) * 128]
                    out_ref[GATE_ORDER.index(2 * r + column // 13), :, at : at + 128] = piece.astype(BF16)


def gate_up(mine, other, w_gate, w_up):
    wide = (N_KV, 4, 2 * PART + EXTRA)
    return pl.pallas_call(
        gate_kernel,
        out_shape=[shape(wide, BF16), shape((ROWS, OWN), F32)],
        in_specs=[whole(a.shape) for a in (mine, other, w_gate, w_up)],
        out_specs=[whole(wide), whole((ROWS, OWN))],
        compiler_params=params(8),
        cost_estimate=cost(4 * ROWS * w_gate.size, 4 * w_gate.size),
        name="gate_up",
    )(mine, other, in_vmem(w_gate), in_vmem(w_up))


def hidden_kernel(parts_ref, out_ref):
    total = parts_ref[0].astype(F32)
    for i in range(1, N_KV):
        total += parts_ref[i].astype(F32)
    squares = total[:, 2 * PART : 2 * PART + 1] + total[:, 2 * PART + 64 : 2 * PART + 65]
    scale = lax.rsqrt(squares / (HQ * HD) + 1e-05)
    gate, up = total[:, :PART] * scale, total[:, PART : 2 * PART] * scale
    hidden = (gate / (1.0 + jnp.exp(-gate)) * up).astype(BF16)
    for i in range(N_KV):
        out_ref[i] = hidden


def hidden_units(parts):
    return pl.pallas_call(
        hidden_kernel,
        out_shape=shape((N_KV, 4, PART), BF16),
        in_specs=[whole(parts.shape)],
        out_specs=whole((N_KV, 4, PART)),
        compiler_params=params(8),
        name="hidden_units",
    )(parts)


def down_kernel(parts_ref, w_ref, out_ref, x):
    for d in range(N_KV):
        piece = parts_ref[HIDDEN_ORDER.index(d)].astype(F32)
        x[4 * (d // 2) : 4 * (d // 2) + 4, d % 2 * PART : d % 2 * PART + PART] = piece
    total = jnp.dot(x[...].astype(BF16), w_ref[...], preferred_element_type=F32)
    for i in range(KVH):
        out_ref[HEAD_ORDER.index(i)] = total[:, i * OWN : (i + 1) * OWN].astype(BF16)


def down(parts, w_down):
    out = (KVH, ROWS, OWN)
    return pl.pallas_call(
        down_kernel,
        out_shape=shape(out, BF16),
        in_specs=[whole(parts.shape), whole(w_down.shape)],
        out_specs=whole(out),
        scratch_shapes=[pltpu.VMEM((ROWS, UNITS), F32)],
        compiler_params=params(8),
        cost_estimate=cost(2 * ROWS * w_down.size, 2 * w_down.size),
        name="down",
    )(parts, in_vmem(w_down))


def finish_kernel(own_ref, parts_ref, out_ref):
    total = own_ref[...]
    for i in range(KVH):
        total += parts_ref[i].astype(F32)
    out_ref[...] = total.astype(BF16)


def finish(own, parts):
    return pl.pallas_call(
        finish_kernel,
        out_shape=shape(own.shape, BF16),
        in_specs=[whole(own.shape), whole(parts.shape)],
        out_specs=whole(own.shape),
        compiler_params=params(8),
        name="finish",
    )(own, parts)


def exchange(value, axis, groups=None):
    return lax.all_to_all(value, axis, 0, 0, axis_index_groups=groups, tiled=True)


def exchange_kv(value, order):
    groups = [[kv * KVH + head for kv in order] for head in range(KVH)]
    return exchange(value, ("kv", "head"), groups)


def swap(value, step):
    return lax.ppermute(value, "head", [(j, j ^ step) for j in range(KVH)])


def on_device(
    queries,
    key_cache,
    value_cache,
    block_table,
    lengths,
    new_keys,
    new_values,
    residual,
    out_weight,
    norm_gain,
    w_gate,
    w_up,
    w_down,
):
    partials, weight = attention_partials(
        block_table, lengths, queries, key_cache, value_cache, new_keys, new_values, out_weight[0, 0]
    )
    keep, give = project(exchange_kv(partials, MERGE_ORDER), weight)
    parts = exchange_kv(add_pair(keep, swap(give, 1)), PROJ_ORDER)
    same_core = [[2 * y + c for y in Y_ORDER] for c in range(2)]
    parts = exchange(stream(parts, residual, norm_gain[None], w_up), "head", same_core)
    here = add_columns(parts, w_gate)
    gates, own = gate_up(here, swap(here, 1), w_gate, w_up)
    hidden = exchange_kv(hidden_units(exchange_kv(gates, GATE_ORDER)), HIDDEN_ORDER)
    parts = exchange(down(hidden, w_down), "head", [list(HEAD_ORDER)])
    return finish(own, parts)


def solution(mesh):
    in_specs = (
        P(None, "head"),
        P("kv", "head", None, None),
        P("kv", "head", None, None),
        P(None, "kv"),
        P(),
        P(None, "head"),
        P(None, "head"),
        P(None, ("kv", "head")),
        P("head", "kv", None, None),
        P(("kv", "head")),
        P("kv", "head"),
        P("kv", "head"),
        P("head", "kv"),
    )
    out_specs = P(None, ("kv", "head"))
    return jax.shard_map(
        on_device, mesh=mesh, in_specs=in_specs, out_specs=out_specs, check_vma=False
    )
```

```python
import math

import jax
import jax.numpy as jnp
from jax import lax
from jax.experimental import pallas as pl
from jax.experimental.pallas import tpu as pltpu
from jax.sharding import PartitionSpec as P

HQ = 128
KVH = 8
SEQS = 16
ROWS = 2 * SEQS
GROUP = HQ // KVH
HD = 128
SLOTS = 24
OWN = 128
HALF = 4 * OWN
N_KV = 16
UNITS = 3328
PART = UNITS // 2
EXTRA = 128
TILE = 256

F32 = jnp.float32
BF16 = jnp.bfloat16
MIB = 1 << 20
W_SPACE = pltpu.HBM
ATTENTION_ROOM = 57


def whole(shape, space=pltpu.VMEM):
    zeros = (0,) * len(shape)
    return pl.BlockSpec(shape, lambda *_: zeros, memory_space=space)


def is_even():
    return lax.axis_index("head") % 2 == 0


BACK = tuple(reversed(range(N_KV)))
MERGE_ORDER, PROJ_ORDER, GATE_ORDER, HIDDEN_ORDER = BACK, BACK, BACK, BACK
Y_ORDER = (3, 2, 1, 0)
HEAD_ORDER = (7, 5, 3, 1, 6, 4, 2, 0)


def own_y():
    return lax.axis_index("head") // 2


def params(mib, steps=0):
    kinds = ("arbitrary",) * steps if steps else None
    return pltpu.CompilerParams(vmem_limit_bytes=mib * MIB, dimension_semantics=kinds)


def in_hbm(array):
    return pltpu.with_memory_space_constraint(array, pltpu.HBM)


def in_vmem(array):
    return pltpu.with_memory_space_constraint(array, pltpu.VMEM)


def cost(flops, moved):
    return pl.CostEstimate(flops=flops, bytes_accessed=moved, transcendentals=0)


def shape(dims, kind):
    return jax.ShapeDtypeStruct(dims, kind)


def parts_of_copy(src, dst, sems):
    count = sems.shape[0]
    deep = dst.shape[0] // count
    return [
        pltpu.make_async_copy(
            src.at[i * deep : (i + 1) * deep, :], dst.at[i * deep : (i + 1) * deep, :], sems.at[i]
        )
        for i in range(count)
    ]


def attention_kernel(
    table_hbm, lengths_hbm, q_hbm, k_hbm, v_hbm, new_k_hbm, new_v_hbm, w_hbm,
    out_ref, w_ref, table, lengths, q_ref, k_ref, v_ref, new_k, new_v, sems, w_sems,
    q_rows, scores, tops, sums, numer,
):
    pairs = (
        (table_hbm, table), (lengths_hbm, lengths), (q_hbm, q_ref), (k_hbm, k_ref), (v_hbm, v_ref),
        (new_k_hbm, new_k), (new_v_hbm, new_v),
    )
    copies = [pltpu.make_async_copy(src, dst, sems.at[i]) for i, (src, dst) in enumerate(pairs)]
    for i in (2, 0, 1, 5, 6, 3, 4):
        copies[i].start()
    w_copies = parts_of_copy(w_hbm, w_ref, w_sems)
    for copy in w_copies:
        copy.start()
    tops[...] = jnp.full(tops.shape, -1e30, F32)
    sums[...] = jnp.zeros(sums.shape, F32)
    numer[...] = jnp.zeros(numer.shape, F32)
    lane = lax.broadcasted_iota(jnp.int32, (ROWS, HD), 1)
    unit = 1.0 / math.sqrt(HD)
    copies[2].wait()
    for g in range(GROUP):
        q_rows[pl.ds(g, ROWS, stride=GROUP), :] = q_ref[:, g * HD : (g + 1) * HD].astype(F32)
    copies[5].wait()
    copies[6].wait()
    mine = pl.ds(lax.axis_index("kv"), ROWS, stride=GROUP)
    query = q_rows[mine, :]
    keys, values = new_k[...].astype(F32), new_v[...].astype(F32)
    odd = lax.broadcasted_iota(jnp.int32, (ROWS, 1), 0) % 2 == 1
    at_own = jnp.sum(query * keys, axis=1, keepdims=True) * unit
    at_prev = jnp.sum(query * pltpu.roll(keys, 1, 0), axis=1, keepdims=True) * unit
    new_max = jnp.where(odd, jnp.maximum(at_own, at_prev), at_own)
    expo_own = jnp.exp(at_own - new_max)
    expo_prev = jnp.where(odd, jnp.exp(at_prev - new_max), 0.0)
    new_out = expo_own.astype(BF16).astype(F32) * values
    new_out += expo_prev.astype(BF16).astype(F32) * pltpu.roll(values, 1, 0)
    tops[mine, :] = jnp.broadcast_to(new_max, (ROWS, HD))
    copies[0].wait()
    copies[1].wait()
    copies[3].wait()
    rows_of = []
    for b in range(SLOTS):
        seq = table[0, b]
        limit = lengths[seq] - table[1, b] * HD
        here = pl.ds(pl.multiple_of(seq * ROWS, ROWS), ROWS)
        rows_of.append(here)
        raw = lax.dot_general(
            q_rows[here, :].astype(BF16), k_ref[b, 0], (((1,), (1,)), ((), ())),
            preferred_element_type=F32,
        )
        masked = jnp.where(lane < limit, raw * unit, -1e30)
        scores[b] = masked
        tops[here, :] = jnp.maximum(tops[here, :], jnp.max(masked, axis=1, keepdims=True))
    tops[...] = tops[...].astype(BF16).astype(F32)
    new_scale = jnp.exp(new_max - tops[mine, :])
    sums[mine, :] = new_scale * (expo_own + expo_prev)
    numer[mine, :] = new_scale * new_out
    copies[4].wait()
    for b in range(SLOTS):
        here = rows_of[b]
        masked = scores[b]
        expo = jnp.where(masked > -1e29, jnp.exp(masked - tops[here, :]), 0.0)
        sums[here, :] += jnp.sum(expo, axis=1, keepdims=True)
        numer[here, :] += jnp.dot(expo.astype(BF16), v_ref[b, 0], preferred_element_type=F32)
    by_head = lax.broadcasted_iota(jnp.int32, (GROUP, HD), 1)
    stats = jnp.zeros((GROUP, HD), F32)
    for row in range(ROWS):
        heads = slice(row * GROUP, (row + 1) * GROUP)
        high = sums[heads, :].astype(BF16).astype(F32)
        stats = jnp.where(by_head == row, tops[heads, :], stats)
        stats = jnp.where(by_head == row + ROWS, high, stats)
        stats = jnp.where(by_head == row + 2 * ROWS, sums[heads, :] - high, stats)
    for g in range(GROUP):
        at = MERGE_ORDER.index(g)
        out_ref[at, :ROWS, :] = numer[pl.ds(g, ROWS, stride=GROUP), :].astype(BF16)
        out_ref[at, ROWS:, :] = jnp.broadcast_to(stats[g : g + 1, :], (16, HD)).astype(BF16)
    for copy in w_copies:
        copy.wait()


def attention_partials(
    table, lengths, queries, key_cache, value_cache, new_keys, new_values, weight
):
    tall = pltpu.VMEM((ROWS * GROUP, HD), F32)
    arrays = (queries, key_cache, value_cache, new_keys, new_values)
    return pl.pallas_call(
        attention_kernel,
        out_shape=[pltpu.VMEM((GROUP, ROWS + 16, HD), BF16), pltpu.VMEM(weight.shape, BF16)],
        in_specs=[pl.BlockSpec(memory_space=W_SPACE)] * 8,
        out_specs=[whole((GROUP, ROWS + 16, HD)), whole(weight.shape)],
        scratch_shapes=[pltpu.SMEM(table.shape, jnp.int32), pltpu.SMEM(lengths.shape, jnp.int32)]
        + [pltpu.VMEM(a.shape, BF16) for a in arrays]
        + [pltpu.SemaphoreType.DMA((7,)), pltpu.SemaphoreType.DMA((8,))]
        + [tall, pltpu.VMEM((SLOTS, ROWS, HD), F32), tall, tall, tall],
        compiler_params=params(ATTENTION_ROOM),
        cost_estimate=cost(SLOTS * ROWS * HD * HD * 4, 4 * SLOTS * HD * HD),
        name="attention",
    )(*[in_hbm(a) for a in (table, lengths, *arrays, weight)])


def project_kernel(got_ref, w_ref, keep_ref, give_ref):
    row = lax.broadcasted_iota(jnp.int32, (N_KV, HD), 0)
    stats = jnp.zeros((N_KV, HD), F32)
    for i in range(N_KV):
        stats = jnp.where(row == i, got_ref[i, ROWS:, :].astype(F32), stats)
    stats = jnp.concatenate([stats, jnp.zeros((HD - N_KV, HD), F32)], axis=0).T
    maxes = stats[:ROWS]
    lane = lax.broadcasted_iota(jnp.int32, (ROWS, HD), 1)
    real = lane < N_KV
    peak = jnp.max(jnp.where(real, maxes, -1e30), axis=1, keepdims=True)
    scales = jnp.where(real, jnp.exp(maxes - peak), 0.0)
    denom = jnp.sum(scales * (stats[ROWS : 2 * ROWS] + stats[2 * ROWS : 3 * ROWS]), axis=1, keepdims=True)
    total = jnp.zeros((ROWS, HD), F32)
    for i in range(N_KV):
        total += scales[:, i : i + 1] * got_ref[i, :ROWS, :].astype(F32)
    attn = (total / denom).astype(BF16)
    even = is_even()
    for d in range(N_KV):
        for y in range(4):
            at = d * 2 * HALF + y * TILE
            both = jnp.dot(attn, w_ref[:, at : at + TILE], preferred_element_type=F32)
            here = slice(y * OWN, (y + 1) * OWN)
            place = PROJ_ORDER.index(d)
            keep_ref[place, :, here] = jnp.where(even, both[:, :OWN], both[:, OWN:])
            give_ref[place, :, here] = jnp.where(even, both[:, OWN:], both[:, :OWN]).astype(BF16)


def project(got, weight):
    out = (N_KV, ROWS, HALF)
    return pl.pallas_call(
        project_kernel,
        out_shape=[shape(out, F32), shape(out, BF16)],
        in_specs=[whole(got.shape), whole(weight.shape)],
        out_specs=[whole(out), whole(out)],
        compiler_params=params(8),
        cost_estimate=cost(2 * ROWS * weight.size, 2 * weight.size),
        name="project",
    )(got, weight)


def pair_kernel(keep_ref, got_ref, out_ref):
    out_ref[...] = (keep_ref[...] + got_ref[...].astype(F32)).astype(BF16)


def add_pair(keep, got):
    return pl.pallas_call(
        pair_kernel,
        out_shape=shape(keep.shape, BF16),
        in_specs=[whole(keep.shape), whole(got.shape)],
        out_specs=whole(keep.shape),
        compiler_params=params(8),
        name="add_pair",
    )(keep, got)


def stream_kernel(_, parts_ref, res_ref, gain_ref, out_ref):
    total = parts_ref[0].astype(F32)
    for i in range(1, N_KV):
        total += parts_ref[i].astype(F32)
    me = own_y()
    blocks = []
    for y in range(4):
        rest = jnp.where(me == y, res_ref[...].astype(F32), 0.0)
        blocks.append(total[:, y * OWN : (y + 1) * OWN] + rest)
    blocks.append(jnp.broadcast_to(gain_ref[...].astype(F32), (ROWS, OWN)))
    message = jnp.concatenate(blocks, axis=1).astype(BF16)
    for y in range(4):
        out_ref[y] = message


def stream(parts, residual, gain, held):
    out = (4, ROWS, HALF + OWN)
    return pl.pallas_call(
        stream_kernel,
        out_shape=shape(out, BF16),
        in_specs=[whole(a.shape) for a in (held, parts, residual, gain)],
        out_specs=whole(out),
        compiler_params=params(8),
        name="stream",
    )(in_vmem(held), parts, residual, gain)


def column_kernel(_, parts_ref, out_ref):
    total = parts_ref[0, :, :HALF].astype(F32)
    for y in range(1, 4):
        total += parts_ref[y, :, :HALF].astype(F32)
    out_ref[:, :HALF] = total.astype(BF16)
    row = lax.broadcasted_iota(jnp.int32, (ROWS, OWN), 0)
    gains = jnp.zeros((ROWS, OWN), F32)
    for y in range(4):
        gains = jnp.where(row == Y_ORDER[y], parts_ref[y, :, HALF:].astype(F32), gains)
    out_ref[:, HALF:] = gains.astype(BF16)


def add_columns(parts, held):
    out = parts.shape[1:]
    return pl.pallas_call(
        column_kernel,
        out_shape=shape(out, BF16),
        in_specs=[whole(held.shape), whole(parts.shape)],
        out_specs=whole(out),
        compiler_params=params(8),
        name="add_columns",
    )(in_vmem(held), parts)


def gate_kernel(mine_ref, other_ref, gate_w, up_w, out_ref, own_ref):
    tiles = UNITS // TILE
    even = is_even()
    mine, other = mine_ref[...].astype(F32), other_ref[...].astype(F32)
    halves = (jnp.where(even, mine, other), jnp.where(even, other, mine))
    square = jnp.zeros((ROWS, OWN), F32)
    own = jnp.zeros((ROWS, OWN), F32)
    blocks = []
    for y in range(4):
        for c in range(2):
            block = halves[c][:, y * OWN : (y + 1) * OWN]
            gain = halves[c][y : y + 1, HALF:]
            blocks.append((block * gain).astype(BF16))
            square += block * block
        own += jnp.where(own_y() == y, mine[:, y * OWN : (y + 1) * OWN], 0.0)
    own_ref[...] = own
    x = jnp.concatenate(blocks, axis=1)
    total = jnp.sum(square, axis=1, keepdims=True)
    high = total.astype(BF16).astype(F32)
    lane = lax.broadcasted_iota(jnp.int32, (ROWS, EXTRA), 1)
    squares = jnp.where(lane < 64, high, total - high).astype(BF16).astype(F32)
    for d in range(N_KV):
        out_ref[GATE_ORDER.index(d), :, 2 * PART :] = squares[4 * (d // 2) : 4 * (d // 2) + 4, :].astype(BF16)
    for tile in range(tiles):
        for which in range(2):
            weight = (gate_w, up_w)[which]
            lanes = slice(tile * TILE, (tile + 1) * TILE)
            result = jnp.dot(x, weight[:, lanes], preferred_element_type=F32)
            for part in range(2):
                column = 2 * tile + part
                at = which * PART + column % 13 * 128
                for r in range(8):
                    piece = result[4 * r : 4 * r + 4, part * 128 : (part + 1) * 128]
                    out_ref[GATE_ORDER.index(2 * r + column // 13), :, at : at + 128] = piece.astype(BF16)


def gate_up(mine, other, w_gate, w_up):
    wide = (N_KV, 4, 2 * PART + EXTRA)
    return pl.pallas_call(
        gate_kernel,
        out_shape=[shape(wide, BF16), shape((ROWS, OWN), F32)],
        in_specs=[whole(a.shape) for a in (mine, other, w_gate, w_up)],
        out_specs=[whole(wide), whole((ROWS, OWN))],
        compiler_params=params(8),
        cost_estimate=cost(4 * ROWS * w_gate.size, 4 * w_gate.size),
        name="gate_up",
    )(mine, other, in_vmem(w_gate), in_vmem(w_up))


def hidden_kernel(parts_ref, out_ref):
    total = parts_ref[0].astype(F32)
    for i in range(1, N_KV):
        total += parts_ref[i].astype(F32)
    squares = total[:, 2 * PART : 2 * PART + 1] + total[:, 2 * PART + 64 : 2 * PART + 65]
    scale = lax.rsqrt(squares / (HQ * HD) + 1e-05)
    gate, up = total[:, :PART] * scale, total[:, PART : 2 * PART] * scale
    hidden = (gate / (1.0 + jnp.exp(-gate)) * up).astype(BF16)
    for i in range(N_KV):
        out_ref[i] = hidden


def hidden_units(parts):
    return pl.pallas_call(
        hidden_kernel,
        out_shape=shape((N_KV, 4, PART), BF16),
        in_specs=[whole(parts.shape)],
        out_specs=whole((N_KV, 4, PART)),
        compiler_params=params(8),
        name="hidden_units",
    )(parts)


def down_kernel(parts_ref, w_ref, out_ref, x):
    for d in range(N_KV):
        piece = parts_ref[HIDDEN_ORDER.index(d)].astype(F32)
        x[4 * (d // 2) : 4 * (d // 2) + 4, d % 2 * PART : d % 2 * PART + PART] = piece
    total = jnp.dot(x[...].astype(BF16), w_ref[...], preferred_element_type=F32)
    for i in range(KVH):
        out_ref[HEAD_ORDER.index(i)] = total[:, i * OWN : (i + 1) * OWN].astype(BF16)


def down(parts, w_down):
    out = (KVH, ROWS, OWN)
    return pl.pallas_call(
        down_kernel,
        out_shape=shape(out, BF16),
        in_specs=[whole(parts.shape), whole(w_down.shape)],
        out_specs=whole(out),
        scratch_shapes=[pltpu.VMEM((ROWS, UNITS), F32)],
        compiler_params=params(8),
        cost_estimate=cost(2 * ROWS * w_down.size, 2 * w_down.size),
        name="down",
    )(parts, in_vmem(w_down))


def finish_kernel(own_ref, parts_ref, out_ref):
    total = own_ref[...]
    for i in range(KVH):
        total += parts_ref[i].astype(F32)
    out_ref[...] = total.astype(BF16)


def finish(own, parts):
    return pl.pallas_call(
        finish_kernel,
        out_shape=shape(own.shape, BF16),
        in_specs=[whole(own.shape), whole(parts.shape)],
        out_specs=whole(own.shape),
        compiler_params=params(8),
        name="finish",
    )(own, parts)


def exchange(value, axis, groups=None):
    return lax.all_to_all(value, axis, 0, 0, axis_index_groups=groups, tiled=True)


def exchange_kv(value, order):
    groups = [[kv * KVH + head for kv in order] for head in range(KVH)]
    return exchange(value, ("kv", "head"), groups)


def swap(value, step):
    return lax.ppermute(value, "head", [(j, j ^ step) for j in range(KVH)])


def on_device(
    queries,
    key_cache,
    value_cache,
    block_table,
    lengths,
    new_keys,
    new_values,
    residual,
    out_weight,
    norm_gain,
    w_gate,
    w_up,
    w_down,
):
    partials, weight = attention_partials(
        block_table, lengths, queries, key_cache, value_cache, new_keys, new_values, out_weight[0, 0]
    )
    keep, give = project(exchange_kv(partials, MERGE_ORDER), weight)
    parts = exchange_kv(add_pair(keep, swap(give, 1)), PROJ_ORDER)
    same_core = [[2 * y + c for y in Y_ORDER] for c in range(2)]
    parts = exchange(stream(parts, residual, norm_gain[None], w_up), "head", same_core)
    here = add_columns(parts, w_gate)
    gates, own = gate_up(here, swap(here, 1), w_gate, w_up)
    hidden = exchange_kv(hidden_units(exchange_kv(gates, GATE_ORDER)), HIDDEN_ORDER)
    parts = exchange(down(hidden, w_down), "head", [list(HEAD_ORDER)])
    return finish(own, parts)


def solution(mesh):
    in_specs = (
        P(None, "head"),
        P("kv", "head", None, None),
        P("kv", "head", None, None),
        P(None, "kv"),
        P(),
        P(None, "head"),
        P(None, "head"),
        P(None, ("kv", "head")),
        P("head", "kv", None, None),
        P(("kv", "head")),
        P("kv", "head"),
        P("kv", "head"),
        P("head", "kv"),
    )
    out_specs = P(None, ("kv", "head"))
    return jax.shard_map(
        on_device, mesh=mesh, in_specs=in_specs, out_specs=out_specs, check_vma=False
    )
```

```python
import math

import jax
import jax.numpy as jnp
from jax import lax
from jax.experimental import pallas as pl
from jax.experimental.pallas import tpu as pltpu
from jax.sharding import PartitionSpec as P

HQ = 128
KVH = 8
SEQS = 16
ROWS = 2 * SEQS
GROUP = HQ // KVH
HD = 128
SLOTS = 24
OWN = 128
HALF = 4 * OWN
N_KV = 16
UNITS = 3328
PART = UNITS // 2
EXTRA = 128
TILE = 256

F32 = jnp.float32
BF16 = jnp.bfloat16
MIB = 1 << 20
W_SPACE = pltpu.HBM
ATTENTION_ROOM = 57


def whole(shape, space=pltpu.VMEM):
    zeros = (0,) * len(shape)
    return pl.BlockSpec(shape, lambda *_: zeros, memory_space=space)


def is_even():
    return lax.axis_index("head") % 2 == 0


Z_BACK = tuple(4 * x + z for z in reversed(range(4)) for x in reversed(range(4)))
MERGE_ORDER, PROJ_ORDER, GATE_ORDER, HIDDEN_ORDER = Z_BACK, Z_BACK, Z_BACK, Z_BACK
Y_ORDER = (3, 2, 1, 0)
HEAD_ORDER = (7, 5, 3, 1, 6, 4, 2, 0)


def own_y():
    return lax.axis_index("head") // 2


def params(mib, steps=0):
    kinds = ("arbitrary",) * steps if steps else None
    return pltpu.CompilerParams(vmem_limit_bytes=mib * MIB, dimension_semantics=kinds)


def in_hbm(array):
    return pltpu.with_memory_space_constraint(array, pltpu.HBM)


def in_vmem(array):
    return pltpu.with_memory_space_constraint(array, pltpu.VMEM)


def cost(flops, moved):
    return pl.CostEstimate(flops=flops, bytes_accessed=moved, transcendentals=0)


def shape(dims, kind):
    return jax.ShapeDtypeStruct(dims, kind)


def parts_of_copy(src, dst, sems):
    count = sems.shape[0]
    deep = dst.shape[0] // count
    return [
        pltpu.make_async_copy(
            src.at[i * deep : (i + 1) * deep, :], dst.at[i * deep : (i + 1) * deep, :], sems.at[i]
        )
        for i in range(count)
    ]


def attention_kernel(
    table_hbm, lengths_hbm, q_hbm, k_hbm, v_hbm, new_k_hbm, new_v_hbm, w_hbm,
    out_ref, w_ref, table, lengths, q_ref, k_ref, v_ref, new_k, new_v, sems, w_sems,
    q_rows, scores, tops, sums, numer,
):
    pairs = (
        (table_hbm, table), (lengths_hbm, lengths), (q_hbm, q_ref), (k_hbm, k_ref), (v_hbm, v_ref),
        (new_k_hbm, new_k), (new_v_hbm, new_v),
    )
    copies = [pltpu.make_async_copy(src, dst, sems.at[i]) for i, (src, dst) in enumerate(pairs)]
    for i in (2, 0, 1, 5, 6, 3, 4):
        copies[i].start()
    w_copies = parts_of_copy(w_hbm, w_ref, w_sems)
    for copy in w_copies:
        copy.start()
    tops[...] = jnp.full(tops.shape, -1e30, F32)
    sums[...] = jnp.zeros(sums.shape, F32)
    numer[...] = jnp.zeros(numer.shape, F32)
    lane = lax.broadcasted_iota(jnp.int32, (ROWS, HD), 1)
    unit = 1.0 / math.sqrt(HD)
    copies[2].wait()
    for g in range(GROUP):
        q_rows[pl.ds(g, ROWS, stride=GROUP), :] = q_ref[:, g * HD : (g + 1) * HD].astype(F32)
    copies[5].wait()
    copies[6].wait()
    mine = pl.ds(lax.axis_index("kv"), ROWS, stride=GROUP)
    query = q_rows[mine, :]
    keys, values = new_k[...].astype(F32), new_v[...].astype(F32)
    odd = lax.broadcasted_iota(jnp.int32, (ROWS, 1), 0) % 2 == 1
    at_own = jnp.sum(query * keys, axis=1, keepdims=True) * unit
    at_prev = jnp.sum(query * pltpu.roll(keys, 1, 0), axis=1, keepdims=True) * unit
    new_max = jnp.where(odd, jnp.maximum(at_own, at_prev), at_own)
    expo_own = jnp.exp(at_own - new_max)
    expo_prev = jnp.where(odd, jnp.exp(at_prev - new_max), 0.0)
    new_out = expo_own.astype(BF16).astype(F32) * values
    new_out += expo_prev.astype(BF16).astype(F32) * pltpu.roll(values, 1, 0)
    tops[mine, :] = jnp.broadcast_to(new_max, (ROWS, HD))
    copies[0].wait()
    copies[1].wait()
    copies[3].wait()
    rows_of = []
    for b in range(SLOTS):
        seq = table[0, b]
        limit = lengths[seq] - table[1, b] * HD
        here = pl.ds(pl.multiple_of(seq * ROWS, ROWS), ROWS)
        rows_of.append(here)
        raw = lax.dot_general(
            q_rows[here, :].astype(BF16), k_ref[b, 0], (((1,), (1,)), ((), ())),
            preferred_element_type=F32,
        )
        masked = jnp.where(lane < limit, raw * unit, -1e30)
        scores[b] = masked
        tops[here, :] = jnp.maximum(tops[here, :], jnp.max(masked, axis=1, keepdims=True))
    tops[...] = tops[...].astype(BF16).astype(F32)
    new_scale = jnp.exp(new_max - tops[mine, :])
    sums[mine, :] = new_scale * (expo_own + expo_prev)
    numer[mine, :] = new_scale * new_out
    copies[4].wait()
    for b in range(SLOTS):
        here = rows_of[b]
        masked = scores[b]
        expo = jnp.where(masked > -1e29, jnp.exp(masked - tops[here, :]), 0.0)
        sums[here, :] += jnp.sum(expo, axis=1, keepdims=True)
        numer[here, :] += jnp.dot(expo.astype(BF16), v_ref[b, 0], preferred_element_type=F32)
    by_head = lax.broadcasted_iota(jnp.int32, (GROUP, HD), 1)
    stats = jnp.zeros((GROUP, HD), F32)
    for row in range(ROWS):
        heads = slice(row * GROUP, (row + 1) * GROUP)
        high = sums[heads, :].astype(BF16).astype(F32)
        stats = jnp.where(by_head == row, tops[heads, :], stats)
        stats = jnp.where(by_head == row + ROWS, high, stats)
        stats = jnp.where(by_head == row + 2 * ROWS, sums[heads, :] - high, stats)
    for g in range(GROUP):
        at = MERGE_ORDER.index(g)
        out_ref[at, :ROWS, :] = numer[pl.ds(g, ROWS, stride=GROUP), :].astype(BF16)
        out_ref[at, ROWS:, :] = jnp.broadcast_to(stats[g : g + 1, :], (16, HD)).astype(BF16)
    for copy in w_copies:
        copy.wait()


def attention_partials(
    table, lengths, queries, key_cache, value_cache, new_keys, new_values, weight
):
    tall = pltpu.VMEM((ROWS * GROUP, HD), F32)
    arrays = (queries, key_cache, value_cache, new_keys, new_values)
    return pl.pallas_call(
        attention_kernel,
        out_shape=[pltpu.VMEM((GROUP, ROWS + 16, HD), BF16), pltpu.VMEM(weight.shape, BF16)],
        in_specs=[pl.BlockSpec(memory_space=W_SPACE)] * 8,
        out_specs=[whole((GROUP, ROWS + 16, HD)), whole(weight.shape)],
        scratch_shapes=[pltpu.SMEM(table.shape, jnp.int32), pltpu.SMEM(lengths.shape, jnp.int32)]
        + [pltpu.VMEM(a.shape, BF16) for a in arrays]
        + [pltpu.SemaphoreType.DMA((7,)), pltpu.SemaphoreType.DMA((8,))]
        + [tall, pltpu.VMEM((SLOTS, ROWS, HD), F32), tall, tall, tall],
        compiler_params=params(ATTENTION_ROOM),
        cost_estimate=cost(SLOTS * ROWS * HD * HD * 4, 4 * SLOTS * HD * HD),
        name="attention",
    )(*[in_hbm(a) for a in (table, lengths, *arrays, weight)])


def project_kernel(got_ref, w_ref, keep_ref, give_ref):
    row = lax.broadcasted_iota(jnp.int32, (N_KV, HD), 0)
    stats = jnp.zeros((N_KV, HD), F32)
    for i in range(N_KV):
        stats = jnp.where(row == i, got_ref[i, ROWS:, :].astype(F32), stats)
    stats = jnp.concatenate([stats, jnp.zeros((HD - N_KV, HD), F32)], axis=0).T
    maxes = stats[:ROWS]
    lane = lax.broadcasted_iota(jnp.int32, (ROWS, HD), 1)
    real = lane < N_KV
    peak = jnp.max(jnp.where(real, maxes, -1e30), axis=1, keepdims=True)
    scales = jnp.where(real, jnp.exp(maxes - peak), 0.0)
    denom = jnp.sum(scales * (stats[ROWS : 2 * ROWS] + stats[2 * ROWS : 3 * ROWS]), axis=1, keepdims=True)
    total = jnp.zeros((ROWS, HD), F32)
    for i in range(N_KV):
        total += scales[:, i : i + 1] * got_ref[i, :ROWS, :].astype(F32)
    attn = (total / denom).astype(BF16)
    even = is_even()
    for d in range(N_KV):
        for y in range(4):
            at = d * 2 * HALF + y * TILE
            both = jnp.dot(attn, w_ref[:, at : at + TILE], preferred_element_type=F32)
            here = slice(y * OWN, (y + 1) * OWN)
            place = PROJ_ORDER.index(d)
            keep_ref[place, :, here] = jnp.where(even, both[:, :OWN], both[:, OWN:])
            give_ref[place, :, here] = jnp.where(even, both[:, OWN:], both[:, :OWN]).astype(BF16)


def project(got, weight):
    out = (N_KV, ROWS, HALF)
    return pl.pallas_call(
        project_kernel,
        out_shape=[shape(out, F32), shape(out, BF16)],
        in_specs=[whole(got.shape), whole(weight.shape)],
        out_specs=[whole(out), whole(out)],
        compiler_params=params(8),
        cost_estimate=cost(2 * ROWS * weight.size, 2 * weight.size),
        name="project",
    )(got, weight)


def pair_kernel(keep_ref, got_ref, out_ref):
    out_ref[...] = (keep_ref[...] + got_ref[...].astype(F32)).astype(BF16)


def add_pair(keep, got):
    return pl.pallas_call(
        pair_kernel,
        out_shape=shape(keep.shape, BF16),
        in_specs=[whole(keep.shape), whole(got.shape)],
        out_specs=whole(keep.shape),
        compiler_params=params(8),
        name="add_pair",
    )(keep, got)


def stream_kernel(_, parts_ref, res_ref, gain_ref, out_ref):
    total = parts_ref[0].astype(F32)
    for i in range(1, N_KV):
        total += parts_ref[i].astype(F32)
    me = own_y()
    blocks = []
    for y in range(4):
        rest = jnp.where(me == y, res_ref[...].astype(F32), 0.0)
        blocks.append(total[:, y * OWN : (y + 1) * OWN] + rest)
    blocks.append(jnp.broadcast_to(gain_ref[...].astype(F32), (ROWS, OWN)))
    message = jnp.concatenate(blocks, axis=1).astype(BF16)
    for y in range(4):
        out_ref[y] = message


def stream(parts, residual, gain, held):
    out = (4, ROWS, HALF + OWN)
    return pl.pallas_call(
        stream_kernel,
        out_shape=shape(out, BF16),
        in_specs=[whole(a.shape) for a in (held, parts, residual, gain)],
        out_specs=whole(out),
        compiler_params=params(8),
        name="stream",
    )(in_vmem(held), parts, residual, gain)


def column_kernel(_, parts_ref, out_ref):
    total = parts_ref[0, :, :HALF].astype(F32)
    for y in range(1, 4):
        total += parts_ref[y, :, :HALF].astype(F32)
    out_ref[:, :HALF] = total.astype(BF16)
    row = lax.broadcasted_iota(jnp.int32, (ROWS, OWN), 0)
    gains = jnp.zeros((ROWS, OWN), F32)
    for y in range(4):
        gains = jnp.where(row == Y_ORDER[y], parts_ref[y, :, HALF:].astype(F32), gains)
    out_ref[:, HALF:] = gains.astype(BF16)


def add_columns(parts, held):
    out = parts.shape[1:]
    return pl.pallas_call(
        column_kernel,
        out_shape=shape(out, BF16),
        in_specs=[whole(held.shape), whole(parts.shape)],
        out_specs=whole(out),
        compiler_params=params(8),
        name="add_columns",
    )(in_vmem(held), parts)


def gate_kernel(mine_ref, other_ref, gate_w, up_w, out_ref, own_ref):
    tiles = UNITS // TILE
    even = is_even()
    mine, other = mine_ref[...].astype(F32), other_ref[...].astype(F32)
    halves = (jnp.where(even, mine, other), jnp.where(even, other, mine))
    square = jnp.zeros((ROWS, OWN), F32)
    own = jnp.zeros((ROWS, OWN), F32)
    blocks = []
    for y in range(4):
        for c in range(2):
            block = halves[c][:, y * OWN : (y + 1) * OWN]
            gain = halves[c][y : y + 1, HALF:]
            blocks.append((block * gain).astype(BF16))
            square += block * block
        own += jnp.where(own_y() == y, mine[:, y * OWN : (y + 1) * OWN], 0.0)
    own_ref[...] = own
    x = jnp.concatenate(blocks, axis=1)
    total = jnp.sum(square, axis=1, keepdims=True)
    high = total.astype(BF16).astype(F32)
    lane = lax.broadcasted_iota(jnp.int32, (ROWS, EXTRA), 1)
    squares = jnp.where(lane < 64, high, total - high).astype(BF16).astype(F32)
    for d in range(N_KV):
        out_ref[GATE_ORDER.index(d), :, 2 * PART :] = squares[4 * (d // 2) : 4 * (d // 2) + 4, :].astype(BF16)
    for tile in range(tiles):
        for which in range(2):
            weight = (gate_w, up_w)[which]
            lanes = slice(tile * TILE, (tile + 1) * TILE)
            result = jnp.dot(x, weight[:, lanes], preferred_element_type=F32)
            for part in range(2):
                column = 2 * tile + part
                at = which * PART + column % 13 * 128
                for r in range(8):
                    piece = result[4 * r : 4 * r + 4, part * 128 : (part + 1) * 128]
                    out_ref[GATE_ORDER.index(2 * r + column // 13), :, at : at + 128] = piece.astype(BF16)


def gate_up(mine, other, w_gate, w_up):
    wide = (N_KV, 4, 2 * PART + EXTRA)
    return pl.pallas_call(
        gate_kernel,
        out_shape=[shape(wide, BF16), shape((ROWS, OWN), F32)],
        in_specs=[whole(a.shape) for a in (mine, other, w_gate, w_up)],
        out_specs=[whole(wide), whole((ROWS, OWN))],
        compiler_params=params(8),
        cost_estimate=cost(4 * ROWS * w_gate.size, 4 * w_gate.size),
        name="gate_up",
    )(mine, other, in_vmem(w_gate), in_vmem(w_up))


def hidden_kernel(parts_ref, out_ref):
    total = parts_ref[0].astype(F32)
    for i in range(1, N_KV):
        total += parts_ref[i].astype(F32)
    squares = total[:, 2 * PART : 2 * PART + 1] + total[:, 2 * PART + 64 : 2 * PART + 65]
    scale = lax.rsqrt(squares / (HQ * HD) + 1e-05)
    gate, up = total[:, :PART] * scale, total[:, PART : 2 * PART] * scale
    hidden = (gate / (1.0 + jnp.exp(-gate)) * up).astype(BF16)
    for i in range(N_KV):
        out_ref[i] = hidden


def hidden_units(parts):
    return pl.pallas_call(
        hidden_kernel,
        out_shape=shape((N_KV, 4, PART), BF16),
        in_specs=[whole(parts.shape)],
        out_specs=whole((N_KV, 4, PART)),
        compiler_params=params(8),
        name="hidden_units",
    )(parts)


def down_kernel(parts_ref, w_ref, out_ref, x):
    for d in range(N_KV):
        piece = parts_ref[HIDDEN_ORDER.index(d)].astype(F32)
        x[4 * (d // 2) : 4 * (d // 2) + 4, d % 2 * PART : d % 2 * PART + PART] = piece
    total = jnp.dot(x[...].astype(BF16), w_ref[...], preferred_element_type=F32)
    for i in range(KVH):
        out_ref[HEAD_ORDER.index(i)] = total[:, i * OWN : (i + 1) * OWN].astype(BF16)


def down(parts, w_down):
    out = (KVH, ROWS, OWN)
    return pl.pallas_call(
        down_kernel,
        out_shape=shape(out, BF16),
        in_specs=[whole(parts.shape), whole(w_down.shape)],
        out_specs=whole(out),
        scratch_shapes=[pltpu.VMEM((ROWS, UNITS), F32)],
        compiler_params=params(8),
        cost_estimate=cost(2 * ROWS * w_down.size, 2 * w_down.size),
        name="down",
    )(parts, in_vmem(w_down))


def finish_kernel(own_ref, parts_ref, out_ref):
    total = own_ref[...]
    for i in range(KVH):
        total += parts_ref[i].astype(F32)
    out_ref[...] = total.astype(BF16)


def finish(own, parts):
    return pl.pallas_call(
        finish_kernel,
        out_shape=shape(own.shape, BF16),
        in_specs=[whole(own.shape), whole(parts.shape)],
        out_specs=whole(own.shape),
        compiler_params=params(8),
        name="finish",
    )(own, parts)


def exchange(value, axis, groups=None):
    return lax.all_to_all(value, axis, 0, 0, axis_index_groups=groups, tiled=True)


def exchange_kv(value, order):
    groups = [[kv * KVH + head for kv in order] for head in range(KVH)]
    return exchange(value, ("kv", "head"), groups)


def swap(value, step):
    return lax.ppermute(value, "head", [(j, j ^ step) for j in range(KVH)])


def on_device(
    queries,
    key_cache,
    value_cache,
    block_table,
    lengths,
    new_keys,
    new_values,
    residual,
    out_weight,
    norm_gain,
    w_gate,
    w_up,
    w_down,
):
    partials, weight = attention_partials(
        block_table, lengths, queries, key_cache, value_cache, new_keys, new_values, out_weight[0, 0]
    )
    keep, give = project(exchange_kv(partials, MERGE_ORDER), weight)
    parts = exchange_kv(add_pair(keep, swap(give, 1)), PROJ_ORDER)
    same_core = [[2 * y + c for y in Y_ORDER] for c in range(2)]
    parts = exchange(stream(parts, residual, norm_gain[None], w_up), "head", same_core)
    here = add_columns(parts, w_gate)
    gates, own = gate_up(here, swap(here, 1), w_gate, w_up)
    hidden = exchange_kv(hidden_units(exchange_kv(gates, GATE_ORDER)), HIDDEN_ORDER)
    parts = exchange(down(hidden, w_down), "head", [list(HEAD_ORDER)])
    return finish(own, parts)


def solution(mesh):
    in_specs = (
        P(None, "head"),
        P("kv", "head", None, None),
        P("kv", "head", None, None),
        P(None, "kv"),
        P(),
        P(None, "head"),
        P(None, "head"),
        P(None, ("kv", "head")),
        P("head", "kv", None, None),
        P(("kv", "head")),
        P("kv", "head"),
        P("kv", "head"),
        P("head", "kv"),
    )
    out_specs = P(None, ("kv", "head"))
    return jax.shard_map(
        on_device, mesh=mesh, in_specs=in_specs, out_specs=out_specs, check_vma=False
    )
```
